512 devices in a mesh: segment: 8 (over y_lo, x), tile: 64 (over y_hi, z, core).
Axes of the slice: x: 4, y: 4 (y_hi: 2, y_lo: 2; y = y_hi * 2 + y_lo), z: 16, core: 2. Of those that a mesh axis runs over, the one named last changes fastest.
Arguments:
- stored_inputs: bfloat16 [8, 1, 64, 8, 16, 768], P('segment', None, 'tile'), may hold values from -6 to 6
- output_grads: bfloat16 [1, 64, 8, 16, 768], P(None, 'tile'), may hold values from -6 to 6
- norm_gain: float32 [8, 768], P('segment'), may hold values from 0.1 to 1.9
- position_bias: float32 [8, 12, 13, 13], P('segment'), may hold values from -3 to 300
- qkv_weight: bfloat16 [8, 768, 2304], P('segment', 'tile'), may hold values from -0.21875 to 0.21875
- out_weight: bfloat16 [8, 768, 768], P('segment', 'tile'), may hold values from -0.21875 to 0.21875
Outputs:
- input_grads: bfloat16 [8, 1, 64, 8, 16, 768], P('segment', None, 'tile')
The draws below stay inside these ranges and needn't reach their ends.
All inputs are finite; a program needn't handle non-finite values.
Results may differ from the reference program's by a relative error of at most 0.027.
Values may be sent and summed in bfloat16 or wider, within the bound.
A program may use at most 128 MiB of HBM per device.

```python
import jax
import jax.numpy as jnp
from jax import lax

D = 768
HEADS = 12
HD = 64
RAD = 6
TH = 8
TW = 16
MICRO = 1
SEGMENTS = 8
TILES = 64
GRID = 8


def draw_position_bias(key, part):
    window_span = 2 * RAD + 1
    shape_full = (SEGMENTS, HEADS, window_span, window_span)
    first_key = jax.random.fold_in(key, 0)
    return jnp.clip(jax.random.normal(first_key, shape_full, jnp.float32), -3.0, 3.0)


def level_of(rng, extent, cuts, least, top_value):
    factor_of, own = 1.0, jax.random.fold_in(rng, 6)
    for axis_at, blocks in cuts:
        steps = jnp.exp(jax.random.uniform(jax.random.fold_in(own, axis_at), (blocks,), jnp.float32, least / len(cuts), top_value / len(cuts)))
        factor_of = factor_of * jnp.repeat(steps, extent[axis_at] // blocks).reshape([-1 if axis == axis_at else 1 for axis in range(len(extent))])
    return factor_of


def bell_draw(own_key, shape, scale, bound, cuts=(), kind=jnp.bfloat16):
    factor_of = level_of(own_key, shape, cuts, -0.22, 0.18) if cuts else 1.0
    array = jax.random.normal(own_key, shape, jnp.float32) * scale * factor_of
    return jnp.minimum(jnp.maximum(array, -bound), bound).astype(kind)


def setup_inputs(seed: int = 0) -> dict:
    arg_keys = jax.random.split(jax.random.key(seed), 7)
    stored_inputs = bell_draw(arg_keys[0], (SEGMENTS, MICRO, TILES, TH, TW, D), 1.0, 6.0, ((0, 8), (2, 64)))
    output_grads = bell_draw(arg_keys[1], (MICRO, TILES, TH, TW, D), 1.0, 6.0, ((1, 64),))
    norm_gain = jnp.clip(1.0 + 0.18 * jax.random.normal(arg_keys[2], (SEGMENTS, D), jnp.float32), 0.1, 1.9)
    position_bias = draw_position_bias(jax.random.fold_in(arg_keys[6], 71), 0)
    qkv_weight = bell_draw(arg_keys[4], (SEGMENTS, D, 3 * D), D ** -0.5, 0.21875, ((0, 8), (1, 64)))
    out_weight = bell_draw(arg_keys[5], (SEGMENTS, D, D), D ** -0.5, 0.21875, ((0, 8), (1, 64)))
    return {"stored_inputs": stored_inputs, "output_grads": output_grads, "norm_gain": norm_gain, "position_bias": position_bias, "qkv_weight": qkv_weight, "out_weight": out_weight}


EPSILON = 1e-05
NEG_FILL = -1e+30

def window_tables(position_table, tile_row, tile_col):
    pad_rows = TH + 2 * RAD
    pad_cols = TW + 2 * RAD
    window_span = 2 * RAD + 1
    row_offset = jnp.arange(pad_rows, dtype=jnp.int32)[None, :] - RAD - jnp.arange(TH, dtype=jnp.int32)[:, None]
    col_offset = jnp.arange(pad_cols, dtype=jnp.int32)[None, :] - RAD - jnp.arange(TW, dtype=jnp.int32)[:, None]
    offsets = jnp.arange(window_span, dtype=jnp.int32) - RAD
    row_onehot = (row_offset[:, :, None] == offsets[None, None, :]).astype(jnp.float32)
    col_onehot = (col_offset[:, :, None] == offsets[None, None, :]).astype(jnp.float32)
    bias_full = jnp.einsum('huv,aiu,bjv->habij', position_table, row_onehot, col_onehot, precision=lax.Precision.HIGHEST).reshape(HEADS, TH * TW, pad_rows * pad_cols)
    global_row = tile_row * TH + jnp.arange(pad_rows, dtype=jnp.int32) - RAD
    global_col = tile_col * TW + jnp.arange(pad_cols, dtype=jnp.int32) - RAD
    row_inside = (global_row >= 0) & (global_row < GRID * TH)
    col_inside = (global_col >= 0) & (global_col < GRID * TW)
    row_valid = (jnp.abs(row_offset) <= RAD) & row_inside[None, :]
    col_valid = (jnp.abs(col_offset) <= RAD) & col_inside[None, :]
    valid_pairs = (row_valid[:, None, :, None] & col_valid[None, :, None, :]).reshape(TH * TW, pad_rows * pad_cols)
    return (bias_full, valid_pairs)

def attend_back(queries, keyvals, grad_attn, bias_full, valid_pairs):
    query_count = queries.shape[0]
    key_count = keyvals.shape[0]
    highest = lax.Precision.HIGHEST
    query_heads = queries.astype(jnp.float32).reshape(query_count, HEADS, HD)
    key_heads = keyvals[:, :D].astype(jnp.float32).reshape(key_count, HEADS, HD)
    value_heads = keyvals[:, D:].astype(jnp.float32).reshape(key_count, HEADS, HD)
    grad_heads = grad_attn.astype(jnp.float32).reshape(query_count, HEADS, HD)
    scores = jnp.einsum('nhd,phd->hnp', query_heads, key_heads, precision=highest) * 0.125 + bias_full
    scores = jnp.where(valid_pairs[None], scores, NEG_FILL)
    top_score = lax.optimization_barrier(jnp.max(scores, axis=-1, keepdims=True))
    raw_weight = jnp.exp(scores - top_score)
    probability = raw_weight / lax.optimization_barrier(jnp.sum(raw_weight, axis=-1, keepdims=True))
    prob_low = probability.astype(jnp.bfloat16).astype(jnp.float32)
    prob_grad = jnp.einsum('nhd,phd->hnp', grad_heads, value_heads, precision=highest)
    delta_term = lax.optimization_barrier(jnp.sum(probability * prob_grad, axis=-1, keepdims=True))
    score_grad = (prob_low * (prob_grad - delta_term)).astype(jnp.bfloat16).astype(jnp.float32)
    query_grad = jnp.einsum('hnp,phd->nhd', score_grad, key_heads, precision=highest) * 0.125
    key_grad = jnp.einsum('hnp,nhd->phd', score_grad, query_heads, precision=highest) * 0.125
    value_grad = jnp.einsum('hnp,nhd->phd', prob_low, grad_heads, precision=highest)
    block_grad = jnp.concatenate([key_grad.reshape(key_count, D), value_grad.reshape(key_count, D)], axis=1)
    return (query_grad.reshape(query_count, D).astype(jnp.bfloat16), block_grad.astype(jnp.bfloat16))

def segment_backward(stored, incoming, gain_row, position_table, qkv_full, out_full):
    pad_rows = TH + 2 * RAD
    pad_cols = TW + 2 * RAD
    token_count = TH * TW
    values = stored.astype(jnp.float32)
    center_mean = lax.optimization_barrier(jnp.mean(values, axis=-1, keepdims=True))
    deviation = values - center_mean
    variance = lax.optimization_barrier(jnp.mean(deviation * deviation, axis=-1, keepdims=True))
    inverse = lax.rsqrt(variance + EPSILON)
    normal_part = deviation * inverse
    normed = (normal_part * gain_row).astype(jnp.bfloat16)
    projected = jnp.dot(normed.reshape(-1, D), qkv_full, preferred_element_type=jnp.float32).astype(jnp.bfloat16)
    projected = projected.reshape(TILES, token_count, 3 * D)
    queries = projected[:, :, :D]
    keyvals = projected[:, :, D:].reshape(GRID, GRID, TH, TW, 2 * D).transpose(0, 2, 1, 3, 4)
    keyvals = keyvals.reshape(GRID * TH, GRID * TW, 2 * D)
    keyvals = jnp.pad(keyvals, ((RAD, RAD), (RAD, RAD), (0, 0)))
    grad_attn = jnp.dot(incoming.reshape(-1, D), out_full.T, preferred_element_type=jnp.float32).astype(jnp.bfloat16)
    grad_attn = grad_attn.reshape(TILES, token_count, D)
    query_weight = qkv_full[:, :D]
    keyval_weight = qkv_full[:, D:]

    def per_tile(tile_index):
        tile_row = tile_index // GRID
        tile_col = tile_index % GRID
        region = lax.dynamic_slice(keyvals, (tile_row * TH, tile_col * TW, jnp.int32(0)), (pad_rows, pad_cols, 2 * D)).reshape(-1, 2 * D)
        bias_full, valid_pairs = window_tables(position_table, tile_row, tile_col)
        query_grad, block_grad = attend_back(queries[tile_index], region, grad_attn[tile_index], bias_full, valid_pairs)
        own_part = jnp.dot(query_grad, query_weight.T, preferred_element_type=jnp.float32)
        spread = jnp.dot(block_grad, keyval_weight.T, preferred_element_type=jnp.float32).reshape(pad_rows, pad_cols, D)
        rim_grad = lax.optimization_barrier(spread.astype(jnp.bfloat16)).astype(jnp.float32)
        inner_part = spread[RAD:RAD + TH, RAD:RAD + TW] + own_part.reshape(TH, TW, D)
        return lax.dynamic_update_slice(rim_grad, inner_part, (jnp.int32(RAD), jnp.int32(RAD), jnp.int32(0)))
    mixed_all = lax.map(per_tile, jnp.arange(TILES, dtype=jnp.int32))

    def place(tile_index, canvas):
        tile_row = tile_index // GRID
        tile_col = tile_index % GRID
        start = (tile_row * TH, tile_col * TW, jnp.int32(0))
        current = lax.dynamic_slice(canvas, start, (pad_rows, pad_cols, D))
        return lax.dynamic_update_slice(canvas, current + mixed_all[tile_index], start)
    canvas = lax.fori_loop(jnp.int32(0), jnp.int32(TILES), place, jnp.zeros((GRID * TH + 2 * RAD, GRID * TW + 2 * RAD, D), jnp.float32))
    image_grad = canvas[RAD:RAD + GRID * TH, RAD:RAD + GRID * TW]
    token_grad = image_grad.reshape(GRID, TH, GRID, TW, D).transpose(0, 2, 1, 3, 4).reshape(TILES, TH, TW, D)
    scaled = token_grad * gain_row
    first_mean = lax.optimization_barrier(jnp.mean(scaled, axis=-1, keepdims=True))
    second_mean = lax.optimization_barrier(jnp.mean(scaled * normal_part, axis=-1, keepdims=True))
    branch = inverse * (scaled - first_mean - normal_part * second_mean)
    return (incoming.astype(jnp.float32) + branch).astype(jnp.bfloat16)

def reference(stored_inputs, output_grads, norm_gain, position_bias, qkv_weight, out_weight):

    def one_segment(incoming, params):
        stored, gain_row, position_table, qkv_full, out_full = params

        def one_micro(micro_pair):
            return segment_backward(micro_pair[0], micro_pair[1], gain_row, position_table, qkv_full, out_full)
        outgoing = lax.map(one_micro, (stored, incoming))
        return (outgoing, outgoing)
    params = jax.tree.map(lambda array_in: array_in[::-1], (stored_inputs, norm_gain, position_bias, qkv_weight, out_weight))
    final_grad, stacked = lax.scan(one_segment, output_grads, params)
    return stacked[::-1]
```

```python
import functools

import jax
import jax.numpy as jnp
from jax import lax
from jax.experimental import pallas as pl
from jax.experimental.pallas import tpu as pltpu
from jax.sharding import PartitionSpec as P

D = 768
HEADS = 12
RAD = 6
TH = 8
TW = 16
PAIRS = HEADS // 2
WIDE = 3 * D
OLW = D + 128
EPSILON = 1e-05
NEG_FILL = -1e30
MESH = pl.DeviceIdType.MESH
BF16 = jnp.bfloat16
F32 = jnp.float32

SLOTS = 640
GROUP = 160
T0, B0 = GROUP, 2 * GROUP
OWN_T, OWN_B = T0 + 48, B0 + 48


class Place:
    def __init__(self, tile_count):
        self.zs = tile_count // 4
        self.cols = self.zs // 2
        self.seg = lax.axis_index("segment")
        self.tile = lax.axis_index("tile")
        self.yh = self.tile // (2 * self.zs)
        self.z = (self.tile % (2 * self.zs)) // 2
        self.core = self.tile % 2
        self.rb = self.yh * 2 + self.core
        self.left = self.at(self.yh, (self.z + self.zs - 1) % self.zs, self.core)
        self.right = self.at(self.yh, (self.z + 1) % self.zs, self.core)
        self.mate = self.at(self.yh, self.z, 1 - self.core)
        self.cross = self.at(1 - self.yh, self.z, self.core)
        self.has_up = self.rb > 0
        self.has_down = self.rb < 3
        up = (self.rb + 3) % 4
        down = (self.rb + 1) % 4
        self.up = self.at(up // 2, self.z, up % 2)
        self.down = self.at(down // 2, self.z, down % 2)
        self.row = self.tile // self.cols
        self.col = self.tile % self.cols
        self.half = self.z % 2
        self.tile_t = (2 * self.rb) * self.cols + self.z // 2
        self.tile_b = (2 * self.rb + 1) * self.cols + self.z // 2

    def at(self, yh, z, core):
        return yh * (2 * self.zs) + z * 2 + core

    def block_of(self, half):
        rb = self.row // 2
        return self.at(rb // 2, 2 * self.col + half, rb % 2)


def remote(src, dst, send, recv, device):
    return pltpu.make_async_remote_copy(
        src_ref=src, dst_ref=dst, send_sem=send, recv_sem=recv, device_id=device, device_id_type=MESH
    )


def signal(sem, device):
    pl.semaphore_signal(sem, inc=1, device_id=device, device_id_type=MESH)


def one(flag):
    return jnp.where(flag, 1, 0).astype(jnp.int32)


def side_copies(place, buf, base, send, recv, at):
    left = (place.seg, place.left)
    right = (place.seg, place.right)
    return [
        remote(
            buf.at[pl.ds(base + 48, 48)], buf.at[pl.ds(base + 112, 48)],
            send.at[at], recv.at[at], left,
        ),
        remote(
            buf.at[pl.ds(base + 64, 48)], buf.at[pl.ds(base, 48)],
            send.at[at + 1], recv.at[at + 1], right,
        ),
    ]


class Vertical:
    def __init__(self, place, buf, send, recv, at):
        self.place = place
        self.go_up = remote(
            buf.at[pl.ds(T0, GROUP)], buf.at[pl.ds(3 * GROUP, GROUP)],
            send.at[at], recv.at[at], (place.seg, place.up),
        )
        self.go_down = remote(
            buf.at[pl.ds(B0, GROUP)], buf.at[pl.ds(0, GROUP)],
            send.at[at + 1], recv.at[at + 1], (place.seg, place.down),
        )

    def start(self):
        pl.when(self.place.has_up)(self.go_up.start)
        pl.when(self.place.has_down)(self.go_down.start)

    def wait_recv(self):
        pl.when(self.place.has_down)(self.go_up.wait_recv)
        pl.when(self.place.has_up)(self.go_down.wait_recv)

    def wait_send(self):
        pl.when(self.place.has_up)(self.go_up.wait_send)
        pl.when(self.place.has_down)(self.go_down.wait_send)


def clear_outside(place, buf):
    blank = jnp.zeros((GROUP, buf.shape[1]), buf.dtype)

    @pl.when(jnp.logical_not(place.has_up))
    def _():
        buf[0:GROUP, :] = blank

    @pl.when(jnp.logical_not(place.has_down))
    def _():
        buf[3 * GROUP : SLOTS, :] = blank


def gather_kernel(
    tile_count, pack_ref, x_ref, g_ref, all_ref, slots_ref, top_ref,
    ring_send, ring_recv, mate_send, mate_recv, send, recv, local,
):
    place = Place(tile_count)
    seg = place.seg
    zs = place.zs
    targets = [place.block_of(0), place.block_of(1)]
    sources = [place.tile_t, place.tile_b]
    barrier = pltpu.get_barrier_semaphore()
    for device in (place.left, place.right, place.mate, place.cross):
        signal(barrier, (seg, device))
    count = jnp.int32(4)

    @pl.when(place.has_up)
    def _():
        signal(barrier, (seg, place.up))

    @pl.when(place.has_down)
    def _():
        signal(barrier, (seg, place.down))

    count = count + one(place.has_up) + one(place.has_down)
    for source in sources:

        @pl.when(source != place.tile)
        def _():
            signal(barrier, (seg, source))

    for target in targets:
        count = count + one(target != place.tile)

    all_ref[place.z, place.core, place.yh] = pack_ref[...]
    clear_outside(place, slots_ref)
    pl.semaphore_wait(barrier, count)

    mine = all_ref.at[place.z, place.core, place.yh]
    theirs = all_ref.at[place.z, place.core, 1 - place.yh]
    over = remote(mine, mine, send.at[12], recv.at[12], (seg, place.cross))
    over.start()

    group = place.row % 2
    x_at = pl.multiple_of(OWN_T + group * GROUP, 16)
    g_at = pl.multiple_of(group * 64, 16)

    def moves(half):
        device = (seg, targets[half])
        rows = pl.ds(half * 64, 64)
        return (
            remote(x_ref.at[rows], slots_ref.at[pl.ds(x_at, 64)], send.at[half], recv.at[group], device),
            remote(g_ref.at[rows], top_ref.at[pl.ds(g_at, 64)], send.at[2 + half], recv.at[2 + group], device),
        )

    def local_moves(half):
        rows = pl.ds(half * 64, 64)
        return (
            pltpu.make_async_copy(x_ref.at[rows], slots_ref.at[pl.ds(x_at, 64)], local.at[0]),
            pltpu.make_async_copy(g_ref.at[rows], top_ref.at[pl.ds(g_at, 64)], local.at[1]),
        )

    for half in (0, 1):

        @pl.when(targets[half] != place.tile)
        def _():
            for copy in moves(half):
                copy.start()

        @pl.when(targets[half] == place.tile)
        def _():
            for copy in local_moves(half):
                copy.start()
            for copy in local_moves(half):
                copy.wait()

    remote(mine, theirs, send.at[12], recv.at[12], (seg, place.cross)).wait_recv()

    def pair(z):
        return all_ref.at[z, place.core]

    def right_copy(step):
        z = (place.z + zs - step) % zs
        return remote(pair(z), pair(z), ring_send.at[0, step], ring_recv.at[0, step], (seg, place.right))

    def left_copy(step):
        z = (place.z + step) % zs
        return remote(pair(z), pair(z), ring_send.at[1, step], ring_recv.at[1, step], (seg, place.left))

    def right_arrival(step):
        z = (place.z + zs - step - 1) % zs
        return remote(pair(z), pair(z), ring_send.at[0, step], ring_recv.at[0, step], (seg, place.right))

    def left_arrival(step):
        z = (place.z + step + 1) % zs
        return remote(pair(z), pair(z), ring_send.at[1, step], ring_recv.at[1, step], (seg, place.left))

    def mate_copy(offset):
        z = (place.z + offset) % zs
        return remote(pair(z), pair(z), mate_send.at[offset], mate_recv.at[offset], (seg, place.mate))

    def mate_arrival(offset):
        z = (place.z + offset) % zs
        block = all_ref.at[z, 1 - place.core]
        return remote(block, block, mate_send.at[offset], mate_recv.at[offset], (seg, place.mate))

    right_steps = zs // 2
    left_steps = zs - 1 - right_steps
    right_copy(0).start()
    left_copy(0).start()
    mate_copy(0).start()
    sides = side_copies(place, slots_ref, T0, send, recv, 4) + side_copies(place, slots_ref, B0, send, recv, 6)
    vertical = Vertical(place, slots_ref, send, recv, 8)
    for step in range(right_steps):
        right_arrival(step).wait_recv()
        if step + 1 < right_steps:
            right_copy(step + 1).start()
        mate_copy(zs - 1 - step).start()
        if step < left_steps:
            left_arrival(step).wait_recv()
            if step + 1 < left_steps:
                left_copy(step + 1).start()
            mate_copy(step + 1).start()
        if step == right_steps // 2 - 1:
            for source, index, own, top in ((place.tile_t, 0, OWN_T, 0), (place.tile_b, 1, OWN_B, 64)):

                @pl.when(source != place.tile)
                def _():
                    remote(
                        x_ref.at[0:64], slots_ref.at[pl.ds(own, 64)], send.at[index], recv.at[index],
                        (seg, place.left),
                    ).wait_recv()
                    remote(
                        g_ref.at[0:64], top_ref.at[pl.ds(top, 64)], send.at[2 + index], recv.at[2 + index],
                        (seg, place.left),
                    ).wait_recv()

            for copy in sides:
                copy.start()
        if step == right_steps - 2:
            for copy in sides:
                copy.wait_recv()
            vertical.start()
    for offset in range(zs):
        mate_arrival(offset).wait_recv()
    vertical.wait_recv()

    over.wait_send()
    for half in (0, 1):

        @pl.when(targets[half] != place.tile)
        def _():
            for copy in moves(half):
                copy.wait_send()

    for copy in sides:
        copy.wait_send()
    vertical.wait_send()
    for step in range(right_steps):
        right_copy(step).wait_send()
    for step in range(left_steps):
        left_copy(step).wait_send()
    for offset in range(zs):
        mate_copy(offset).wait_send()


def gather(pack, x_tokens, g_tokens, tile_count):
    zs = tile_count // 4
    vmem = pl.BlockSpec(memory_space=pltpu.VMEM)
    return pl.pallas_call(
        functools.partial(gather_kernel, tile_count),
        out_shape=(
            jax.ShapeDtypeStruct((zs, 2, 2, 16, WIDE), BF16),
            jax.ShapeDtypeStruct((SLOTS, D), BF16),
            jax.ShapeDtypeStruct((128, D), BF16),
        ),
        in_specs=[vmem] * 3,
        out_specs=(vmem,) * 3,
        scratch_shapes=[
            pltpu.SemaphoreType.DMA((2, zs)),
            pltpu.SemaphoreType.DMA((2, zs)),
            pltpu.SemaphoreType.DMA((zs,)),
            pltpu.SemaphoreType.DMA((zs,)),
            pltpu.SemaphoreType.DMA((13,)),
            pltpu.SemaphoreType.DMA((13,)),
            pltpu.SemaphoreType.DMA((2,)),
        ],
        compiler_params=pltpu.CompilerParams(
            collective_id=0, has_side_effects=True, vmem_limit_bytes=40 * 2**20
        ),
    )(pack, x_tokens, g_tokens)


def dot(left, right):
    return jnp.dot(left, right, preferred_element_type=F32)


def dot_nt(left, right):
    return lax.dot_general(left, right, (((1,), (1,)), ((), ())), preferred_element_type=F32)


def lanes_of(pair, offset=0):
    return pl.ds(pl.multiple_of(offset + pair * 128, 128), 128)


def own_rows(ref, lanes):
    return jnp.concatenate([ref[OWN_T : OWN_T + 64, lanes], ref[OWN_B : OWN_B + 64, lanes]], axis=0)


def put_own(ref, lanes, value):
    ref[OWN_T : OWN_T + 64, lanes] = value[:64]
    ref[OWN_B : OWN_B + 64, lanes] = value[64:]


def first_lanes():
    return lax.broadcasted_iota(jnp.int32, (128, 128), 1) < 64


def split_pair(value):
    low = first_lanes()
    zero = jnp.zeros_like(value)
    return jnp.concatenate([jnp.where(low, value, zero), jnp.where(low, zero, value)], axis=0)


def merge_pair(value):
    return jnp.where(first_lanes(), value[:128], value[128:])


def unpack_weights(all_ref, qkv_ref, out_ref, zs):
    groups = zs * 4 // 16
    rows = lax.broadcasted_iota(jnp.int32, (192, 256), 0)
    cols = lax.broadcasted_iota(jnp.int32, (192, 256), 1)
    yh = rows // 96
    z = (rows % 96) // 24
    core = (rows % 24) // 12
    feature = rows % 12
    shard = z * 4 + core * 2 + yh
    pick = (cols == shard * 16 + feature).astype(F32).astype(BF16)
    half = 96 * groups
    for group in range(groups):

        @pl.loop(0, 9)
        def _(chunk):
            lanes = pl.ds(pl.multiple_of(chunk * 256, 256), 256)
            block = dot(pick, all_ref[group * 256 : (group + 1) * 256, lanes]).astype(BF16)
            qkv_ref[group * 96 : (group + 1) * 96, lanes] = block[:96]
            qkv_ref[half + group * 96 : half + (group + 1) * 96, lanes] = block[96:]

    picks = [
        ((cols == shard * 16 + 12 + feature // 3) & (feature % 3 == part)).astype(F32).astype(BF16)
        for part in range(3)
    ]
    for group in range(groups):

        @pl.loop(0, 3)
        def _(chunk):
            lanes = pl.ds(pl.multiple_of(chunk * 256, 256), 256)
            total = jnp.zeros((192, 256), F32)
            for part in range(3):
                source = pl.ds(pl.multiple_of(part * D + chunk * 256, 256), 256)
                total = total + dot(picks[part], all_ref[group * 256 : (group + 1) * 256, source])
            block = total.astype(BF16)
            out_ref[group * 96 : (group + 1) * 96, lanes] = block[:96]
            out_ref[half + group * 96 : half + (group + 1) * 96, lanes] = block[96:]


def pair_bias(base_ref, side, pair):
    pieces = []
    for head in (0, 1):
        table = base_ref[side, 2 * pair + head]
        for group in (0, 1):
            rows = table[group * 8 : (group + 1) * 8]
            for col in range(8):
                pieces.append(rows if col == 0 else pltpu.roll(rows, 8 * col, axis=1))
    return jnp.concatenate(pieces, axis=0)


def main_kernel(
    tile_count, all_ref, slots_ref, top_ref, base_ref, edge_ref, gain_ref, out_ref,
    qkv_w, out_w, normed, qkv, prob_q, prob_k, ol, gs, ga, po, dqkv, normal, inverse, token, outb,
    lse_acc, rows_acc, send, recv, local,
):
    place = Place(tile_count)
    seg = place.seg
    last_seg = lax.axis_size("segment") - 1
    targets = [place.tile_t, place.tile_b]
    barrier = pltpu.get_barrier_semaphore()
    signal(barrier, (seg, place.left))
    signal(barrier, (seg, place.right))

    @pl.when(place.has_up)
    def _():
        signal(barrier, (seg, place.up))

    @pl.when(place.has_down)
    def _():
        signal(barrier, (seg, place.down))

    @pl.when(seg < last_seg)
    def _():
        signal(barrier, (seg + 1, place.tile))

    count = 2 + one(place.has_up) + one(place.has_down) + one(seg > 0)
    for half in (0, 1):
        source = place.block_of(half)

        @pl.when(source != place.tile)
        def _():
            signal(barrier, (seg, source))

    for target in targets:
        count = count + one(target != place.tile)

    clear_outside(place, ol)
    clear_outside(place, gs)

    unpack_weights(all_ref, qkv_w, out_w, place.zs)

    @pl.loop(0, 5)
    def _(chunk):
        rows = pl.ds(pl.multiple_of(chunk * 128, 128), 128)
        values = slots_ref[rows, :].astype(F32)
        deviation = values - jnp.mean(values, axis=-1, keepdims=True)
        variance = jnp.mean(deviation * deviation, axis=-1, keepdims=True)
        part = deviation * lax.rsqrt(variance + EPSILON)
        normed[rows, :] = (part * gain_ref[...]).astype(BF16)

    own_x = own_rows(slots_ref, slice(0, D)).astype(F32)
    deviation = own_x - jnp.mean(own_x, axis=-1, keepdims=True)
    variance = jnp.mean(deviation * deviation, axis=-1, keepdims=True)
    own_inverse = lax.rsqrt(variance + EPSILON)
    normal[...] = deviation * own_inverse
    inverse[...] = jnp.broadcast_to(own_inverse, (128, 128))

    @pl.loop(0, 9)
    def _(chunk):
        lanes = pl.ds(pl.multiple_of(chunk * 256, 256), 256)
        qkv[:, lanes] = dot(normed[...], qkv_w[:, lanes]).astype(BF16)

    edge = edge_ref[0:1, :]
    lse_acc[...] = jnp.zeros_like(lse_acc)
    head_lane = lax.broadcasted_iota(jnp.int32, (128, 128), 1)

    @pl.loop(0, PAIRS)
    def _(pair):
        query = split_pair(own_rows(qkv, lanes_of(pair)))
        scores = dot_nt(query, qkv[:, lanes_of(pair, D)]) * 0.125 + pair_bias(base_ref, 0, pair) + edge
        top = jnp.max(scores, axis=-1, keepdims=True)
        weight = jnp.exp(scores - top)
        total = jnp.sum(weight, axis=-1, keepdims=True)
        prob = (weight * (1.0 / total)).astype(BF16)
        prob_q[pl.ds(pl.multiple_of(pair * 256, 256), 256), :] = prob
        attn = merge_pair(dot(prob, qkv[:, lanes_of(pair, 2 * D)]))
        put_own(ol, lanes_of(pair), attn.astype(BF16))
        level = top + jnp.log(total)
        lse_acc[...] += jnp.where(head_lane == 2 * pair, level[:128], 0.0) + jnp.where(
            head_lane == 2 * pair + 1, level[128:], 0.0
        )

    level = lse_acc[...]
    high = level.astype(BF16).astype(F32)
    middle = (level - high).astype(BF16).astype(F32)
    low = level - high - middle
    packed = high + pltpu.roll(middle, 16, axis=1) + pltpu.roll(low, 32, axis=1)
    put_own(ol, slice(D, OLW), packed.astype(BF16))

    pl.semaphore_wait(barrier, count)
    ol_sides = side_copies(place, ol, T0, send, recv, 0) + side_copies(place, ol, B0, send, recv, 2)
    ol_vertical = Vertical(place, ol, send, recv, 4)
    for copy in ol_sides:
        copy.start()
    for copy in ol_sides:
        copy.wait_recv()
    ol_vertical.start()
    ol_vertical.wait_recv()

    thirds = lax.broadcasted_iota(jnp.int32, (16, 128), 1)
    head_row = lax.broadcasted_iota(jnp.int32, (16, 128), 0)
    pick = ((thirds < 48) & (thirds % 16 == head_row)).astype(F32).astype(BF16)
    rows_acc[...] = dot_nt(pick, ol[:, D:OLW])

    def pair_rows(pair):
        first = jnp.broadcast_to(rows_acc[pl.ds(2 * pair, 1), :], (128, SLOTS))
        second = jnp.broadcast_to(rows_acc[pl.ds(2 * pair + 1, 1), :], (128, SLOTS))
        return jnp.concatenate([first, second], axis=0)

    @pl.loop(0, PAIRS)
    def _(pair):
        key = split_pair(own_rows(qkv, lanes_of(pair, D)))
        scores = dot_nt(key, qkv[:, lanes_of(pair)]) * 0.125 + pair_bias(base_ref, 1, pair) + edge
        prob_k[pl.ds(pl.multiple_of(pair * 256, 256), 256), :] = jnp.exp(scores - pair_rows(pair)).astype(BF16)

    pass_t = remote(
        outb.at[0:64], gs.at[pl.ds(OWN_T, 64)], send.at[12], recv.at[12], (jnp.maximum(seg - 1, 0), place.tile)
    )
    pass_b = remote(
        outb.at[64:128], gs.at[pl.ds(OWN_B, 64)], send.at[13], recv.at[13], (jnp.maximum(seg - 1, 0), place.tile)
    )
    gs_sides_t = side_copies(place, gs, T0, send, recv, 6)
    gs_sides_b = side_copies(place, gs, B0, send, recv, 8)
    gs_vertical = Vertical(place, gs, send, recv, 10)

    @pl.when(seg == last_seg)
    def _():
        gs[OWN_T : OWN_T + 64, :] = top_ref[0:64, :]
        gs[OWN_B : OWN_B + 64, :] = top_ref[64:128, :]

    pl.when(seg < last_seg)(pass_t.wait_recv)
    for copy in gs_sides_t:
        copy.start()
    pl.when(seg < last_seg)(pass_b.wait_recv)
    for copy in gs_sides_b:
        copy.start()

    own_g = own_rows(gs, slice(0, D))
    for chunk in range(3):
        put_own(
            ga, slice(chunk * 256, (chunk + 1) * 256),
            dot_nt(own_g, out_w[chunk * 256 : (chunk + 1) * 256, :]).astype(BF16),
        )

    for copy in gs_sides_t:
        copy.wait_recv()
    for copy in gs_sides_b:
        copy.wait_recv()
    gs_vertical.start()

    @pl.loop(0, PAIRS)
    def _(pair):
        grad = own_rows(ga, lanes_of(pair))
        product = grad.astype(F32) * own_rows(ol, lanes_of(pair)).astype(F32)
        delta = jnp.sum(split_pair(product), axis=-1, keepdims=True)
        prob_grad = dot_nt(split_pair(grad), qkv[:, lanes_of(pair, 2 * D)])
        prob = prob_q[pl.ds(pl.multiple_of(pair * 256, 256), 256), :].astype(F32)
        score_grad = (prob * (prob_grad - delta)).astype(BF16)
        query_grad = merge_pair(dot(score_grad, qkv[:, lanes_of(pair, D)])) * 0.125
        dqkv[:, lanes_of(pair)] = query_grad.astype(BF16)

    gs_vertical.wait_recv()

    @pl.loop(0, 3)
    def _(chunk):
        rows = pl.ds(pl.multiple_of(chunk * 256, 256), 256)
        ga[:, rows] = dot_nt(gs[...], out_w[rows, :]).astype(BF16)
        po[:, rows] = ga[:, rows] * ol[:, rows]

    wide = lax.broadcasted_iota(jnp.int32, (16, D), 1)
    head_wide = lax.broadcasted_iota(jnp.int32, (16, D), 0)
    pick_wide = (wide // 64 == head_wide).astype(F32).astype(BF16)
    rows_acc[...] = dot_nt(pick_wide, po[...])

    @pl.loop(0, PAIRS)
    def _(pair):
        value = split_pair(own_rows(qkv, lanes_of(pair, 2 * D)))
        prob_grad = dot_nt(value, ga[:, lanes_of(pair)])
        prob = prob_k[pl.ds(pl.multiple_of(pair * 256, 256), 256), :]
        score_grad = (prob.astype(F32) * (prob_grad - pair_rows(pair))).astype(BF16)
        key_grad = merge_pair(dot(score_grad, qkv[:, lanes_of(pair)])) * 0.125
        value_grad = merge_pair(dot(prob, ga[:, lanes_of(pair)]))
        dqkv[:, lanes_of(pair, D)] = key_grad.astype(BF16)
        dqkv[:, lanes_of(pair, 2 * D)] = value_grad.astype(BF16)

    @pl.loop(0, 3)
    def _(chunk):
        rows = pl.ds(pl.multiple_of(chunk * 256, 256), 256)
        token[:, rows] = dot_nt(dqkv[...], qkv_w[rows, :])

    scaled = token[...] * gain_ref[...]
    part = normal[...]
    first_mean = jnp.mean(scaled, axis=-1, keepdims=True)
    second_mean = jnp.mean(scaled * part, axis=-1, keepdims=True)
    branch = inverse[:, 0:1] * (scaled - first_mean - part * second_mean)
    outb[...] = (own_rows(gs, slice(0, D)).astype(F32) + branch).astype(BF16)

    @pl.when(seg > 0)
    def _():
        pass_t.start()
        pass_b.start()

    row_at = pl.multiple_of(place.half * 64, 16)

    def back(group):
        return remote(
            outb.at[pl.ds(group * 64, 64)], out_ref.at[pl.ds(row_at, 64)],
            send.at[14 + group], recv.at[14 + place.half], (seg, targets[group]),
        )

    def back_local(group):
        return pltpu.make_async_copy(outb.at[pl.ds(group * 64, 64)], out_ref.at[pl.ds(row_at, 64)], local.at[group])

    for group in (0, 1):

        @pl.when(targets[group] != place.tile)
        def _():
            back(group).start()

        @pl.when(targets[group] == place.tile)
        def _():
            back_local(group).start()
            back_local(group).wait()

    for half in (0, 1):

        @pl.when(place.block_of(half) != place.tile)
        def _():
            remote(
                outb.at[0:64], out_ref.at[pl.ds(half * 64, 64)], send.at[14 + half], recv.at[14 + half],
                (seg, place.left),
            ).wait_recv()

    for group in (0, 1):

        @pl.when(targets[group] != place.tile)
        def _():
            back(group).wait_send()

    @pl.when(seg > 0)
    def _():
        pass_t.wait_send()
        pass_b.wait_send()

    for copy in ol_sides + gs_sides_t + gs_sides_b:
        copy.wait_send()
    ol_vertical.wait_send()
    gs_vertical.wait_send()


def main(all_weights, slots, top, base, edge, gain, tile_count):
    vmem = pl.BlockSpec(memory_space=pltpu.VMEM)
    return pl.pallas_call(
        functools.partial(main_kernel, tile_count),
        out_shape=jax.ShapeDtypeStruct((128, D), BF16),
        in_specs=[vmem] * 6,
        out_specs=vmem,
        scratch_shapes=[
            pltpu.VMEM((D, WIDE), BF16),
            pltpu.VMEM((D, D), BF16),
            pltpu.VMEM((SLOTS, D), BF16),
            pltpu.VMEM((SLOTS, WIDE), BF16),
            pltpu.VMEM((HEADS * 128, SLOTS), BF16),
            pltpu.VMEM((HEADS * 128, SLOTS), BF16),
            pltpu.VMEM((SLOTS, OLW), BF16),
            pltpu.VMEM((SLOTS, D), BF16),
            pltpu.VMEM((SLOTS, D), BF16),
            pltpu.VMEM((SLOTS, D), BF16),
            pltpu.VMEM((128, WIDE), BF16),
            pltpu.VMEM((128, D), F32),
            pltpu.VMEM((128, 128), F32),
            pltpu.VMEM((128, D), F32),
            pltpu.VMEM((128, D), BF16),
            pltpu.VMEM((128, 128), F32),
            pltpu.VMEM((16, SLOTS), F32),
            pltpu.SemaphoreType.DMA((16,)),
            pltpu.SemaphoreType.DMA((16,)),
            pltpu.SemaphoreType.DMA((2,)),
        ],
        compiler_params=pltpu.CompilerParams(
            collective_id=1, has_side_effects=True, vmem_limit_bytes=56 * 2**20
        ),
    )(all_weights, slots, top, base, edge, gain)


def bias_base(table):
    span = 2 * RAD + 1
    slot = jnp.arange(SLOTS, dtype=jnp.int32)[None, :]
    row = jnp.arange(16, dtype=jnp.int32)[:, None]
    up = 8 * (slot // GROUP - 1) + slot % 8 - row + RAD
    across = (slot % GROUP) // 8 + jnp.zeros_like(row)
    valid = (up >= 0) & (up < span) & (across < span)
    index = jnp.where(valid, up * span + across, -1).reshape(-1)
    onehot = (jnp.arange(span * span, dtype=jnp.int32)[:, None] == index[None, :]).astype(F32)
    both = jnp.stack([table, table[:, ::-1, ::-1]]).reshape(2 * HEADS, span * span)
    base = jnp.dot(both, onehot, precision=lax.Precision.HIGHEST).reshape(2, HEADS, 16, SLOTS)
    return jnp.where(valid[None, None], base, NEG_FILL)


def edge_mask(tile, tile_count):
    zs = tile_count // 4
    z = (tile % (2 * zs)) // 2
    rb = (tile // (2 * zs)) * 2 + tile % 2
    slot = jnp.arange(SLOTS, dtype=jnp.int32)
    group = slot // GROUP
    col = (slot % GROUP) // 8 - RAD
    outside = (
        ((col < 0) & (z == 0)) | ((col > 7) & (z == zs - 1))
        | ((group == 0) & (rb == 0)) | ((group == 3) & (rb == 3))
    )
    return jnp.broadcast_to(jnp.where(outside, NEG_FILL, 0.0)[None], (8, SLOTS)).astype(F32)


def half_tiles(tile):
    return tile.reshape(TH, 2, 8, D).transpose(1, 2, 0, 3).reshape(TH * TW, D)


def body(stored_inputs, output_grads, norm_gain, position_bias, qkv_weight, out_weight):
    tile_count = lax.axis_size("tile")
    tile = lax.axis_index("tile")
    pack = jnp.concatenate([qkv_weight[0], out_weight[0].reshape(-1, WIDE)], axis=0)
    x_tokens = half_tiles(stored_inputs[0, 0, 0])
    g_tokens = half_tiles(output_grads[0, 0])
    gathered, slots, top = gather(pack, x_tokens, g_tokens, tile_count)
    base = bias_base(position_bias[0])
    edge = edge_mask(tile, tile_count)
    out = main(gathered.reshape(-1, WIDE), slots, top, base, edge, norm_gain, tile_count)
    out = out.reshape(2, 8, TH, D).transpose(2, 0, 1, 3).reshape(TH, TW, D)
    return out[None, None, None]


def solution(mesh):
    return jax.shard_map(
        body,
        mesh=mesh,
        in_specs=(
            P("segment", None, "tile", None, None, None),
            P(None, "tile", None, None, None),
            P("segment", None),
            P("segment", None, None, None),
            P("segment", "tile", None),
            P("segment", "tile", None),
        ),
        out_specs=P("segment", None, "tile", None, None, None),
        check_vma=False,
    )
```

```python
import functools
import types

import jax
import jax.numpy as jnp
from jax import lax
from jax.experimental import pallas as pl
from jax.experimental.pallas import tpu as pltpu
from jax.sharding import PartitionSpec as P

D = 768
HEADS = 12
RAD = 6
TH = 8
TW = 16
WIDE = 3 * D
OLW = D + 128
EPSILON = 1e-05
NEG_FILL = -1e30
MESH = pl.DeviceIdType.MESH
BF16 = jnp.bfloat16
F32 = jnp.float32

SLOTS = 640
GROUP = 160
T0, B0 = GROUP, 2 * GROUP
OWN_T, OWN_B = T0 + 48, B0 + 48


class Place:
    def __init__(self, tile_count):
        self.zs = tile_count // 4
        self.cols = self.zs // 2
        self.seg = lax.axis_index("segment")
        self.tile = lax.axis_index("tile")
        self.yh = self.tile // (2 * self.zs)
        self.z = (self.tile % (2 * self.zs)) // 2
        self.core = self.tile % 2
        self.rb = self.yh * 2 + self.core
        self.left = self.at(self.yh, (self.z + self.zs - 1) % self.zs, self.core)
        self.right = self.at(self.yh, (self.z + 1) % self.zs, self.core)
        self.mate = self.at(self.yh, self.z, 1 - self.core)
        self.cross = self.at(1 - self.yh, self.z, self.core)
        self.has_up = self.rb > 0
        self.has_down = self.rb < 3
        up = (self.rb + 3) % 4
        down = (self.rb + 1) % 4
        self.up = self.at(up // 2, self.z, up % 2)
        self.down = self.at(down // 2, self.z, down % 2)
        z_left, z_right = (self.z + self.zs - 1) % self.zs, (self.z + 1) % self.zs
        self.up_left = self.at(up // 2, z_left, up % 2)
        self.up_right = self.at(up // 2, z_right, up % 2)
        self.down_left = self.at(down // 2, z_left, down % 2)
        self.down_right = self.at(down // 2, z_right, down % 2)
        self.row = self.tile // self.cols
        self.col = self.tile % self.cols
        self.half = self.z % 2
        self.tile_t = (2 * self.rb) * self.cols + self.z // 2
        self.tile_b = (2 * self.rb + 1) * self.cols + self.z // 2

    def at(self, yh, z, core):
        return yh * (2 * self.zs) + z * 2 + core

    def block_of(self, half):
        rb = self.row // 2
        return self.at(rb // 2, 2 * self.col + half, rb % 2)


def remote(src, dst, send, recv, device):
    return pltpu.make_async_remote_copy(
        src_ref=src, dst_ref=dst, send_sem=send, recv_sem=recv, device_id=device, device_id_type=MESH
    )


def signal(sem, device):
    pl.semaphore_signal(sem, inc=1, device_id=device, device_id_type=MESH)


def one(flag):
    return jnp.where(flag, 1, 0).astype(jnp.int32)


def clear_outside(place, buf):
    blank = jnp.zeros((GROUP, buf.shape[1]), buf.dtype)

    @pl.when(jnp.logical_not(place.has_up))
    def _():
        buf[0:GROUP, :] = blank

    @pl.when(jnp.logical_not(place.has_down))
    def _():
        buf[3 * GROUP : SLOTS, :] = blank


def dot(left, right):
    return jnp.dot(left, right, preferred_element_type=F32)


def dot_nt(left, right):
    return lax.dot_general(left, right, (((1,), (1,)), ((), ())), preferred_element_type=F32)


def own_rows(ref, lanes):
    return jnp.concatenate([ref[OWN_T : OWN_T + 64, lanes], ref[OWN_B : OWN_B + 64, lanes]], axis=0)


def put_own(ref, lanes, value):
    ref[OWN_T : OWN_T + 64, lanes] = value[:64]
    ref[OWN_B : OWN_B + 64, lanes] = value[64:]


QUADS = 3
WIN = 512


def low_lanes(rows):
    return lax.broadcasted_iota(jnp.int32, (rows, 128), 1) < 64


def split_quad(value):
    low = low_lanes(64)
    zero = jnp.zeros((64, 128), value.dtype)
    rows = []
    for part in (0, 1):
        piece = value[:, part * 128 : (part + 1) * 128]
        for keep in (jnp.where(low, piece, zero), jnp.where(low, zero, piece)):
            rows.append(jnp.concatenate([keep, zero] if part == 0 else [zero, keep], axis=1))
    return jnp.concatenate(rows, axis=0)


def merge_quad(value):
    low = low_lanes(64)
    return jnp.concatenate(
        [
            jnp.where(low, value[0:64, :128], value[64:128, :128]),
            jnp.where(low, value[128:192, 128:], value[192:256, 128:]),
        ],
        axis=1,
    )


def head_sums(value):
    low = low_lanes(64)
    sums = []
    for part in (0, 1):
        piece = value[:, part * 128 : (part + 1) * 128]
        sums.append(jnp.sum(jnp.where(low, piece, 0.0), axis=-1, keepdims=True))
        sums.append(jnp.sum(jnp.where(low, 0.0, piece), axis=-1, keepdims=True))
    return jnp.concatenate(sums, axis=0)


def quad_lanes(quad, offset=0):
    return slice(offset + quad * 256, offset + (quad + 1) * 256)


def window(group):
    return slice(0, WIN) if group == 0 else slice(SLOTS - WIN, SLOTS)


def own(group):
    base = OWN_T if group == 0 else OWN_B
    return slice(base, base + 64)


def quad_bias(base_ref, side, quad, group):
    shift = 0 if group == 0 else GROUP - (SLOTS - WIN)
    pieces = []
    for head in range(4 * quad, 4 * quad + 4):
        rows = base_ref[side, head]
        for col in range(8):
            turn = 8 * col + shift
            pieces.append(rows if turn == 0 else pltpu.roll(rows, turn, axis=1))
    return jnp.concatenate(pieces, axis=0)


def quad_rows(ref, quad, group):
    return jnp.concatenate(
        [jnp.broadcast_to(ref[head : head + 1, window(group)], (64, WIN)) for head in range(4 * quad, 4 * quad + 4)],
        axis=0,
    )


BLOCKS = [(quad, group) for quad in range(QUADS) for group in (0, 1)]


def query_probs(r):
    head_lane = lax.broadcasted_iota(jnp.int32, (64, 128), 1)
    levels = [jnp.zeros((64, 128), F32), jnp.zeros((64, 128), F32)]
    for quad, group in BLOCKS:
        query = split_quad(r.qkv[own(group), quad_lanes(quad)])
        scores = dot_nt(query, r.qkv[window(group), quad_lanes(quad, D)]) * 0.125
        scores = scores + quad_bias(r.base, 0, quad, group) + r.edge[0:1, window(group)]
        top = jnp.max(scores, axis=-1, keepdims=True)
        weight = jnp.exp(scores - top)
        total = jnp.sum(weight, axis=-1, keepdims=True)
        prob = (weight * (1.0 / total)).astype(BF16)
        r.prob_q[quad * 2 + group] = prob
        attn = merge_quad(dot(prob, r.qkv[window(group), quad_lanes(quad, 2 * D)]))
        r.ol[own(group), quad_lanes(quad)] = attn.astype(BF16)
        level = top + jnp.log(total)
        for head in range(4):
            levels[group] = jnp.where(
                head_lane == 4 * quad + head, level[head * 64 : (head + 1) * 64], levels[group]
            )
    for group in (0, 1):
        level = levels[group]
        high = level.astype(BF16).astype(F32)
        middle = (level - high).astype(BF16).astype(F32)
        low = level - high - middle
        packed = high + pltpu.roll(middle, 16, axis=1) + pltpu.roll(low, 32, axis=1)
        r.ol[own(group), D:OLW] = packed.astype(BF16)


def key_probs(r):
    for quad, group in BLOCKS:
        key = split_quad(r.qkv[own(group), quad_lanes(quad, D)])
        scores = dot_nt(key, r.qkv[window(group), quad_lanes(quad)]) * 0.125
        scores = scores + quad_bias(r.base, 1, quad, group) + r.edge[0:1, window(group)]
        r.prob_k[quad * 2 + group] = jnp.exp(scores - quad_rows(r.rows, quad, group)).astype(BF16)


def query_side(r, blocks):
    for quad, group in blocks:
        grad = r.ga[own(group), quad_lanes(quad)]
        delta = head_sums(grad.astype(F32) * r.ol[own(group), quad_lanes(quad)].astype(F32))
        prob_grad = dot_nt(split_quad(grad), r.qkv[window(group), quad_lanes(quad, 2 * D)])
        score_grad = r.prob_q[quad * 2 + group] * (prob_grad - delta).astype(BF16)
        query_grad = merge_quad(dot(score_grad, r.qkv[window(group), quad_lanes(quad, D)])) * 0.125
        r.dqkv[group * 64 : (group + 1) * 64, quad_lanes(quad)] = query_grad.astype(BF16)


def key_side(r):
    for quad, group in BLOCKS:
        value = split_quad(r.qkv[own(group), quad_lanes(quad, 2 * D)])
        prob_grad = dot_nt(value, r.ga[window(group), quad_lanes(quad)])
        prob = r.prob_k[quad * 2 + group]
        score_grad = prob * (prob_grad - quad_rows(r.rows, quad, group)).astype(BF16)
        key_grad = merge_quad(dot(score_grad, r.qkv[window(group), quad_lanes(quad)])) * 0.125
        value_grad = merge_quad(dot(prob, r.ga[window(group), quad_lanes(quad)]))
        rows = slice(group * 64, (group + 1) * 64)
        r.dqkv[rows, quad_lanes(quad, D)] = key_grad.astype(BF16)
        r.dqkv[rows, quad_lanes(quad, 2 * D)] = value_grad.astype(BF16)


def onehot(mask):
    return mask.astype(F32).astype(BF16)


def pack_shard(r, rows):
    at_row = lax.broadcasted_iota(jnp.int32, (16, 12), 0)
    at_col = lax.broadcasted_iota(jnp.int32, (16, 12), 1)
    whole = dot(onehot(at_row == at_col), r.qkv_in[...])
    for part in range(3):
        pick = onehot((at_row == 12 + at_col // 3) & (at_col % 3 == part))
        lanes = slice(part * D, (part + 1) * D)
        r.shards[rows, lanes] = (whole[:, lanes] + dot(pick, r.out_in[...])).astype(BF16)


def unpack_group(r, group, zs):
    rows = lax.broadcasted_iota(jnp.int32, (192, 256), 0)
    cols = lax.broadcasted_iota(jnp.int32, (192, 256), 1)
    shard = ((rows % 96) // 24) * 4 + ((rows % 24) // 12) * 2 + rows // 96
    feature = rows % 12
    source = pl.ds(pl.multiple_of(group * 256, 256), 256)
    low = pl.ds(pl.multiple_of(group * 96, 16), 96)
    high = pl.ds(pl.multiple_of(24 * zs + group * 96, 16), 96)
    block = dot(onehot(cols == shard * 16 + feature), r.shards[source, :]).astype(BF16)
    r.qkv_w[low, :] = block[:96]
    r.qkv_w[high, :] = block[96:]
    total = jnp.zeros((192, D), F32)
    for part in range(3):
        pick = onehot((cols == shard * 16 + 12 + feature // 3) & (feature % 3 == part))
        total = total + dot(pick, r.shards[source, part * D : (part + 1) * D])
    block = total.astype(BF16)
    r.out_w[low, :] = block[:96]
    r.out_w[high, :] = block[96:]


def half_order(rows, cols):
    return onehot(cols == (rows % 8) * TW + (rows // 64) * 8 + (rows % 64) // 8)


def fill_bias(r):
    span = 2 * RAD + 1
    table = r.table[...]
    high = table.astype(BF16)
    rest = table - high.astype(F32)
    middle = rest.astype(BF16)
    low = (rest - middle.astype(F32)).astype(BF16)
    index = lax.broadcasted_iota(jnp.int32, (span * span, WIN), 0)
    slot = lax.broadcasted_iota(jnp.int32, (1, WIN), 1)
    across = (slot % GROUP) // 8
    for row in range(8):
        up = 8 * (slot // GROUP - 1) + slot % 8 - row + RAD
        valid = (up >= 0) & (up < span) & (across < span) & (slot < 3 * GROUP)
        want = up * span + across
        for side in (0, 1):
            pick = onehot(index == (want if side == 0 else span * span - 1 - want))
            value = dot(high, pick) + dot(middle, pick) + dot(low, pick)
            value = jnp.where(valid, value, NEG_FILL)
            for head in range(HEADS):
                r.base[side, head, row : row + 1, :] = value[head : head + 1]


def fill_edge(r, place):
    slot = lax.broadcasted_iota(jnp.int32, (8, SLOTS), 1)
    group = slot // GROUP
    col = (slot % GROUP) // 8 - RAD
    first = jnp.where(place.z == 0, 0, -SLOTS)
    last = jnp.where(place.z == place.zs - 1, 7, SLOTS)
    top = jnp.where(place.has_up, 0, 1)
    bottom = jnp.where(place.has_down, 3, 2)
    outside = (col < first) | (col > last) | (group < top) | (group > bottom)
    r.edge[...] = jnp.where(outside, NEG_FILL, 0.0)


class Ring:
    def __init__(self, place, buf, send, recv, mate_send, mate_recv):
        self.place, self.buf = place, buf
        self.send, self.recv, self.mate_send, self.mate_recv = send, recv, mate_send, mate_recv
        self.half = place.zs // 2

    def rows(self, offset, core, which):
        z = (self.place.z + offset + self.place.zs) % self.place.zs
        yh = self.place.yh if which == 0 else 1 - self.place.yh
        return pl.ds(pl.multiple_of(((z * 2 + core) * 2 + yh) * 16, 16), 16)

    def copy(self, way, step, which, offset):
        part = self.buf.at[self.rows(offset, self.place.core, which)]
        device = self.place.right if way == 0 else self.place.left
        return remote(
            part, part, self.send.at[way, which, step], self.recv.at[way, which, step], (self.place.seg, device)
        )

    def has(self, way, step, which):
        return step < self.half - 1 or (step == self.half - 1 and which == way)

    def leave(self, way, step, which):
        return self.copy(way, step, which, -step if way == 0 else step)

    def arrive(self, way, step, which):
        return self.copy(way, step, which, -step - 1 if way == 0 else step + 1)

    def share(self, offset, which, core=None):
        core = self.place.core if core is None else core
        part = self.buf.at[self.rows(offset, core, which)]
        index = (offset + self.place.zs) % self.place.zs
        return remote(
            part, part, self.mate_send.at[which, index], self.mate_recv.at[which, index],
            (self.place.seg, self.place.mate),
        )

    def begin(self, which):
        self.leave(0, 0, which).start()
        self.leave(1, 0, which).start()
        self.share(0, which).start()

    def turn(self, step):
        for which in (0, 1):
            for way in (0, 1):
                if self.has(way, step, which):
                    self.arrive(way, step, which).wait_recv()
                    if self.has(way, step + 1, which):
                        self.leave(way, step + 1, which).start()
                    self.share(-step - 1 if way == 0 else step + 1, which).start()

    def wait_shared(self, group):
        for member in range(4):
            offset = (group * 4 + member - self.place.z + self.place.zs) % self.place.zs
            for which in (0, 1):
                self.share(offset, which, 1 - self.place.core).wait_recv()

    def wait_send(self):
        for which in (0, 1):
            for way in (0, 1):
                for step in range(self.half):
                    if self.has(way, step, which):
                        self.leave(way, step, which).wait_send()
            for offset in range(self.place.zs):
                self.share(offset, which).wait_send()


class Halo:
    def __init__(self, place, buf, send, recv, at, group):
        base = pl.multiple_of(T0 + group * GROUP, 16)
        over = pl.multiple_of(3 * GROUP * (1 - group), 16)
        self.has = jnp.where(group == 0, one(place.has_up), one(place.has_down)) > 0
        self.gets = jnp.where(group == 0, one(place.has_down), one(place.has_up)) > 0

        def pick(up, down):
            return (place.seg, jnp.where(group == 0, up, down))

        def copy(role, src, rows, dst, device):
            index = at + 5 * group + role
            return remote(
                buf.at[pl.ds(src, rows)], buf.at[pl.ds(dst, rows)], send.at[index], recv.at[index], device
            )

        self.vertical = [
            copy(0, base + 48, 64, over + 48, pick(place.up, place.down)),
            copy(1, base + 48, 48, over + 112, pick(place.up_left, place.down_left)),
            copy(2, base + 64, 48, over, pick(place.up_right, place.down_right)),
        ]
        self.sides = [
            copy(3, base + 48, 48, base + 112, (place.seg, place.left)),
            copy(4, base + 64, 48, base, (place.seg, place.right)),
        ]

    def start(self):
        @pl.when(self.has)
        def _():
            for copy in self.vertical:
                copy.start()

        for copy in self.sides:
            copy.start()

    def wait_sides(self):
        for copy in self.sides:
            copy.wait_recv()

    def wait_vertical(self):
        @pl.when(self.gets)
        def _():
            for copy in self.vertical:
                copy.wait_recv()

    def wait_send(self):
        @pl.when(self.has)
        def _():
            for copy in self.vertical:
                copy.wait_send()

        for copy in self.sides:
            copy.wait_send()


def greet(place, barrier):
    seg = place.seg
    signal(barrier, (seg, place.left))
    signal(barrier, (seg, place.right))

    @pl.when(place.has_up)
    def _():
        for device in (place.up, place.up_left, place.up_right):
            signal(barrier, (seg, device))

    @pl.when(place.has_down)
    def _():
        for device in (place.down, place.down_left, place.down_right):
            signal(barrier, (seg, device))

    return 2 + 3 * one(place.has_up) + 3 * one(place.has_down)


def own_layer_norm(r):
    own_x = own_rows(r.slots, slice(0, D)).astype(F32)
    deviation = own_x - jnp.mean(own_x, axis=-1, keepdims=True)
    variance = jnp.mean(deviation * deviation, axis=-1, keepdims=True)
    own_inverse = lax.rsqrt(variance + EPSILON)
    r.normal[...] = deviation * own_inverse
    r.inverse[...] = jnp.broadcast_to(own_inverse, (128, 128))


def window_layer_norm(r):
    @pl.loop(0, 5)
    def _(chunk):
        rows = pl.ds(pl.multiple_of(chunk * 128, 128), 128)
        values = r.slots[rows, :].astype(F32)
        deviation = values - jnp.mean(values, axis=-1, keepdims=True)
        variance = jnp.mean(deviation * deviation, axis=-1, keepdims=True)
        part = deviation * lax.rsqrt(variance + EPSILON)
        r.normed[rows, :] = (part * r.gain[...]).astype(BF16)


REFS = [
    "x", "g", "gain", "table", "qkv_in", "out_in", "out",
    "shards", "xs", "slots", "top", "qkv_w", "out_w", "qkv_t", "out_t", "normed", "qkv", "prob_q", "prob_k", "ol",
    "gs", "ga", "po", "dqkv", "outb", "got", "normal", "inverse", "token", "rows", "base", "edge",
]


def main_kernel(tile_count, *refs):
    r = types.SimpleNamespace(**dict(zip(REFS, refs)))
    send, recv, local, ring_send, ring_recv, mate_send, mate_recv = refs[len(REFS) :]
    place = Place(tile_count)
    seg, zs = place.seg, place.zs
    last_seg = lax.axis_size("segment") - 1
    tiles = [place.tile_t, place.tile_b]
    blocks = [place.block_of(0), place.block_of(1)]
    barrier = pltpu.get_barrier_semaphore()
    count = greet(place, barrier) + 2 + one(seg > 0)
    signal(barrier, (seg, place.mate))
    signal(barrier, (seg, place.cross))

    @pl.when(seg < last_seg)
    def _():
        signal(barrier, (seg + 1, place.tile))

    for device in tiles + blocks:

        @pl.when(device != place.tile)
        def _():
            signal(barrier, (seg, device))

        count = count + one(device != place.tile)

    ring = Ring(place, r.shards, ring_send, ring_recv, mate_send, mate_recv)
    pack_shard(r, ring.rows(0, place.core, 0))
    new_row = lax.broadcasted_iota(jnp.int32, (128, 128), 0)
    new_col = lax.broadcasted_iota(jnp.int32, (128, 128), 1)
    to_halves = half_order(new_row, new_col)
    r.xs[0:128, :] = dot(to_halves, r.x[...]).astype(BF16)
    for buf in (r.slots, r.ol, r.gs):
        clear_outside(place, buf)
    pl.semaphore_wait(barrier, count)

    mine = r.shards.at[ring.rows(0, place.core, 0)]
    theirs = r.shards.at[ring.rows(0, place.core, 1)]
    over = remote(mine, mine, send.at[44], recv.at[44], (seg, place.cross))
    over.start()
    ring.begin(0)

    tile_group = place.row % 2

    def move(src, half, dst, at):
        row = pl.multiple_of(at, 16)
        return remote(
            r.xs.at[pl.ds(src + half * 64, 64)], dst.at[pl.ds(row, 64)],
            send.at[src // 64 + half], recv.at[src // 64 + tile_group], (seg, blocks[half]),
        )

    def move_local(src, half, dst, at):
        row = pl.multiple_of(at, 16)
        return pltpu.make_async_copy(r.xs.at[pl.ds(src + half * 64, 64)], dst.at[pl.ds(row, 64)], local.at[src // 64 + half])

    def moves_start(src, dst, at):
        for half in (0, 1):

            @pl.when(blocks[half] != place.tile)
            def _():
                move(src, half, dst, at).start()

            @pl.when(blocks[half] == place.tile)
            def _():
                move_local(src, half, dst, at).start()
                move_local(src, half, dst, at).wait()

    def moves_wait_recv(src, dst, rows):
        for group in (0, 1):

            @pl.when(tiles[group] != place.tile)
            def _():
                remote(
                    r.xs.at[0:64], dst.at[rows[group]], send.at[src // 64 + group], recv.at[src // 64 + group],
                    (seg, place.left),
                ).wait_recv()

    def moves_wait_send(src, dst, at):
        for half in (0, 1):

            @pl.when(blocks[half] != place.tile)
            def _():
                move(src, half, dst, at).wait_send()

    x_at = OWN_T + tile_group * GROUP
    g_at = tile_group * 64
    moves_start(0, r.slots, x_at)
    remote(mine, theirs, send.at[44], recv.at[44], (seg, place.cross)).wait_recv()
    ring.begin(1)

    x_halos = [Halo(place, r.slots, send, recv, 4, group) for group in (0, 1)]
    near = jnp.where(place.z % 4 < 2, -1, 1)
    home = place.z // 4
    groups = zs // 4
    for step in range(ring.half):
        ring.turn(step)
        if step == 1:
            fill_edge(r, place)
            fill_bias(r)
        if step == ring.half - 5:
            moves_wait_recv(0, r.slots, [own(0), own(1)])
            for halo in x_halos:
                halo.start()
            own_layer_norm(r)
        if step == ring.half - 4:
            ring.wait_shared(home)
            unpack_group(r, home, zs)
        if step == ring.half - 3:
            ring.wait_shared((home + near + groups) % groups)
            unpack_group(r, (home + near + groups) % groups, zs)
        if step == ring.half - 2:
            for halo in x_halos:
                halo.wait_sides()
                halo.wait_vertical()
            window_layer_norm(r)
            ring.wait_shared((home - near + groups) % groups)
            unpack_group(r, (home - near + groups) % groups, zs)

    @pl.when(seg == last_seg)
    def _():
        r.xs[128:256, :] = dot(to_halves, r.g[...]).astype(BF16)
        moves_start(128, r.top, g_at)

    ring.wait_shared((home + 2) % groups)
    unpack_group(r, (home + 2) % groups, zs)
    r.qkv[...] = dot(r.normed[...], r.qkv_w[...]).astype(BF16)
    query_probs(r)

    ol_halos = [Halo(place, r.ol, send, recv, 14, group) for group in (0, 1)]
    for halo in ol_halos:
        halo.start()
    r.qkv_t[...] = r.qkv_w[...].T
    r.out_t[...] = r.out_w[...].T

    first, second = 1 - place.yh, place.yh

    def passing(group, index):
        rows = pl.multiple_of(group * 64, 16)
        slot = pl.multiple_of(OWN_T + group * GROUP, 16)
        return remote(
            r.outb.at[pl.ds(rows, 64)], r.gs.at[pl.ds(slot, 64)], send.at[index], recv.at[index],
            (jnp.maximum(seg - 1, 0), place.tile),
        )

    passes = [passing(first, 34), passing(second, 35)]
    gs_halos = [Halo(place, r.gs, send, recv, 24, group) for group in (first, second)]

    def as_queries():
        put_own(r.ga, slice(0, D), dot(own_rows(r.gs, slice(0, D)), r.out_t[...]).astype(BF16))
        query_side(r, BLOCKS)
        r.token[...] = dot(r.dqkv[:, 0:D], r.qkv_t[0:D, :])

    @pl.when(seg == last_seg)
    def _():
        moves_wait_recv(128, r.top, [slice(0, 64), slice(64, 128)])
        put_own(r.gs, slice(0, D), r.top[...])
        for halo in gs_halos:
            halo.start()
        as_queries()

    for halo in ol_halos:
        halo.wait_sides()
        halo.wait_vertical()
    thirds = lax.broadcasted_iota(jnp.int32, (16, 128), 1)
    head_row = lax.broadcasted_iota(jnp.int32, (16, 128), 0)
    r.rows[...] = dot_nt(onehot((thirds < 48) & (thirds % 16 == head_row)), r.ol[:, D:OLW])
    key_probs(r)

    @pl.when(seg < last_seg)
    def _():
        for one_pass, halo in zip(passes, gs_halos):
            one_pass.wait_recv()
            halo.start()
        as_queries()

    for halo in gs_halos:
        halo.wait_sides()
    middle = slice(T0, T0 + 2 * GROUP)
    r.ga[middle, :] = dot(r.gs[middle, :], r.out_t[...]).astype(BF16)
    for halo in gs_halos:
        halo.wait_vertical()
    outer = jnp.concatenate([r.gs[0:GROUP, :], r.gs[3 * GROUP : SLOTS, :]], axis=0)
    outer = dot(outer, r.out_t[...]).astype(BF16)
    r.ga[0:GROUP, :] = outer[:GROUP]
    r.ga[3 * GROUP : SLOTS, :] = outer[GROUP:]
    wide = lax.broadcasted_iota(jnp.int32, (16, D), 1)
    head_wide = lax.broadcasted_iota(jnp.int32, (16, D), 0)
    r.po[...] = r.ga[...] * r.ol[:, 0:D]
    r.rows[...] = dot_nt(onehot(wide // 64 == head_wide), r.po[...])
    key_side(r)

    token = r.token[...] + dot(r.dqkv[:, D:WIDE], r.qkv_t[D:WIDE, :])
    scaled = token * r.gain[...]
    part = r.normal[...]
    first_mean = jnp.mean(scaled, axis=-1, keepdims=True)
    second_mean = jnp.mean(scaled * part, axis=-1, keepdims=True)
    branch = r.inverse[:, 0:1] * (scaled - first_mean - part * second_mean)
    r.outb[...] = (own_rows(r.gs, slice(0, D)).astype(F32) + branch).astype(BF16)

    @pl.when(seg > 0)
    def _():
        for one_pass in passes:
            one_pass.start()

    row_at = pl.multiple_of(place.half * 64, 16)

    def back(group):
        return remote(
            r.outb.at[pl.ds(group * 64, 64)], r.got.at[pl.ds(row_at, 64)],
            send.at[36 + group], recv.at[36 + place.half], (seg, tiles[group]),
        )

    def back_local(group):
        return pltpu.make_async_copy(r.outb.at[pl.ds(group * 64, 64)], r.got.at[pl.ds(row_at, 64)], local.at[4 + group])

    for group in (0, 1):

        @pl.when(tiles[group] != place.tile)
        def _():
            back(group).start()

        @pl.when(tiles[group] == place.tile)
        def _():
            back_local(group).start()
            back_local(group).wait()

    ring.wait_send()
    over.wait_send()
    moves_wait_send(0, r.slots, x_at)

    @pl.when(seg == last_seg)
    def _():
        moves_wait_send(128, r.top, g_at)

    for halo in x_halos + ol_halos + gs_halos:
        halo.wait_send()

    for half in (0, 1):

        @pl.when(blocks[half] != place.tile)
        def _():
            remote(
                r.outb.at[0:64], r.got.at[pl.ds(half * 64, 64)], send.at[36 + half], recv.at[36 + half],
                (seg, place.left),
            ).wait_recv()

    r.out[...] = dot(half_order(new_col, new_row), r.got[...]).astype(BF16)

    for group in (0, 1):

        @pl.when(tiles[group] != place.tile)
        def _():
            back(group).wait_send()

    @pl.when(seg > 0)
    def _():
        for one_pass in passes:
            one_pass.wait_send()


def main(x, g, gain, table, qkv_in, out_in, tile_count):
    zs = tile_count // 4
    vmem = pl.BlockSpec(memory_space=pltpu.VMEM)
    bf16 = [
        (zs * 64, WIDE), (256, D), (SLOTS, D), (128, D), (D, WIDE), (D, D), (WIDE, D), (D, D), (SLOTS, D), (SLOTS, WIDE),
        (6, 256, WIN), (6, 256, WIN), (SLOTS, OLW), (SLOTS, D), (SLOTS, D), (SLOTS, D), (128, WIDE), (128, D), (128, D),
    ]
    f32 = [(128, D), (128, 128), (128, D), (16, SLOTS), (2, HEADS, 8, WIN), (8, SLOTS)]
    return pl.pallas_call(
        functools.partial(main_kernel, tile_count),
        out_shape=jax.ShapeDtypeStruct((128, D), BF16),
        in_specs=[vmem] * 6,
        out_specs=vmem,
        scratch_shapes=[pltpu.VMEM(shape, BF16) for shape in bf16]
        + [pltpu.VMEM(shape, F32) for shape in f32]
        + [
            pltpu.SemaphoreType.DMA((45,)),
            pltpu.SemaphoreType.DMA((45,)),
            pltpu.SemaphoreType.DMA((6,)),
            pltpu.SemaphoreType.DMA((2, 2, zs // 2)),
            pltpu.SemaphoreType.DMA((2, 2, zs // 2)),
            pltpu.SemaphoreType.DMA((2, zs)),
            pltpu.SemaphoreType.DMA((2, zs)),
        ],
        compiler_params=pltpu.CompilerParams(
            collective_id=0, has_side_effects=True, vmem_limit_bytes=58 * 2**20
        ),
    )(x, g, gain, table, qkv_in, out_in)


def body(stored_inputs, output_grads, norm_gain, position_bias, qkv_weight, out_weight):
    tokens = TH * TW
    out = main(
        stored_inputs.reshape(tokens, D), output_grads.reshape(tokens, D), norm_gain,
        position_bias.reshape(HEADS, -1), qkv_weight[0], out_weight[0], lax.axis_size("tile"),
    )
    return out.reshape(1, 1, 1, TH, TW, D)


def solution(mesh):
    return jax.shard_map(
        body,
        mesh=mesh,
        in_specs=(
            P("segment", None, "tile", None, None, None),
            P(None, "tile", None, None, None),
            P("segment", None),
            P("segment", None, None, None),
            P("segment", "tile", None),
            P("segment", "tile", None),
        ),
        out_specs=P("segment", None, "tile", None, None, None),
        check_vma=False,
    )
```

```python
import functools
import types

import jax
import jax.numpy as jnp
from jax import lax
from jax.experimental import pallas as pl
from jax.experimental.pallas import tpu as pltpu
from jax.sharding import PartitionSpec as P

D = 768
HEADS = 12
RAD = 6
TH = 8
TW = 16
WIDE = 3 * D
OLW = D + 128
EPSILON = 1e-05
NEG_FILL = -1e30
MESH = pl.DeviceIdType.MESH
BF16 = jnp.bfloat16
F32 = jnp.float32

SLOTS = 640
GROUP = 160
T0, B0 = GROUP, 2 * GROUP
OWN_T, OWN_B = T0 + 48, B0 + 48


class Place:
    def __init__(self, tile_count):
        self.zs = tile_count // 4
        self.cols = self.zs // 2
        self.seg = lax.axis_index("segment")
        self.tile = lax.axis_index("tile")
        self.yh = self.tile // (2 * self.zs)
        self.z = (self.tile % (2 * self.zs)) // 2
        self.core = self.tile % 2
        self.rb = self.yh * 2 + self.core
        self.left = self.at(self.yh, (self.z + self.zs - 1) % self.zs, self.core)
        self.right = self.at(self.yh, (self.z + 1) % self.zs, self.core)
        self.mate = self.at(self.yh, self.z, 1 - self.core)
        self.cross = self.at(1 - self.yh, self.z, self.core)
        self.has_up = self.rb > 0
        self.has_down = self.rb < 3
        up = (self.rb + 3) % 4
        down = (self.rb + 1) % 4
        self.up = self.at(up // 2, self.z, up % 2)
        self.down = self.at(down // 2, self.z, down % 2)
        z_left, z_right = (self.z + self.zs - 1) % self.zs, (self.z + 1) % self.zs
        self.up_left = self.at(up // 2, z_left, up % 2)
        self.up_right = self.at(up // 2, z_right, up % 2)
        self.down_left = self.at(down // 2, z_left, down % 2)
        self.down_right = self.at(down // 2, z_right, down % 2)
        self.mate_left = self.at(self.yh, z_left, 1 - self.core)
        self.mate_right = self.at(self.yh, z_right, 1 - self.core)
        self.row = self.tile // self.cols
        self.col = self.tile % self.cols
        self.half = self.z % 2
        self.tile_t = (2 * self.rb) * self.cols + self.z // 2
        self.tile_b = (2 * self.rb + 1) * self.cols + self.z // 2

    def at(self, yh, z, core):
        return yh * (2 * self.zs) + z * 2 + core

    def block_of(self, half):
        rb = self.row // 2
        return self.at(rb // 2, 2 * self.col + half, rb % 2)


def remote(src, dst, send, recv, device):
    return pltpu.make_async_remote_copy(
        src_ref=src, dst_ref=dst, send_sem=send, recv_sem=recv, device_id=device, device_id_type=MESH
    )


def signal(sem, device):
    pl.semaphore_signal(sem, inc=1, device_id=device, device_id_type=MESH)


def one(flag):
    return jnp.where(flag, 1, 0).astype(jnp.int32)


def clear_outside(place, buf):
    blank = jnp.zeros((GROUP, buf.shape[1]), buf.dtype)

    @pl.when(jnp.logical_not(place.has_up))
    def _():
        buf[0:GROUP, :] = blank

    @pl.when(jnp.logical_not(place.has_down))
    def _():
        buf[3 * GROUP : SLOTS, :] = blank


def dot(left, right):
    return jnp.dot(left, right, preferred_element_type=F32)


def dot_nt(left, right):
    return lax.dot_general(left, right, (((1,), (1,)), ((), ())), preferred_element_type=F32)


def own_rows(ref, lanes):
    return jnp.concatenate([ref[OWN_T : OWN_T + 64, lanes], ref[OWN_B : OWN_B + 64, lanes]], axis=0)


def put_own(ref, lanes, value):
    ref[OWN_T : OWN_T + 64, lanes] = value[:64]
    ref[OWN_B : OWN_B + 64, lanes] = value[64:]


QUADS = 3
WIN = 512


def low_lanes(rows):
    return lax.broadcasted_iota(jnp.int32, (rows, 128), 1) < 64


def split_quad(value):
    low = low_lanes(64)
    zero = jnp.zeros((64, 128), value.dtype)
    rows = []
    for part in (0, 1):
        piece = value[:, part * 128 : (part + 1) * 128]
        for keep in (jnp.where(low, piece, zero), jnp.where(low, zero, piece)):
            rows.append(jnp.concatenate([keep, zero] if part == 0 else [zero, keep], axis=1))
    return jnp.concatenate(rows, axis=0)


def merge_quad(value):
    low = low_lanes(64)
    return jnp.concatenate(
        [
            jnp.where(low, value[0:64, :128], value[64:128, :128]),
            jnp.where(low, value[128:192, 128:], value[192:256, 128:]),
        ],
        axis=1,
    )


def head_sums(value):
    low = low_lanes(64)
    sums = []
    for part in (0, 1):
        piece = value[:, part * 128 : (part + 1) * 128]
        sums.append(jnp.sum(jnp.where(low, piece, 0.0), axis=-1, keepdims=True))
        sums.append(jnp.sum(jnp.where(low, 0.0, piece), axis=-1, keepdims=True))
    return jnp.concatenate(sums, axis=0)


def quad_lanes(quad, offset=0):
    return slice(offset + quad * 256, offset + (quad + 1) * 256)


def window(group):
    return slice(0, WIN) if group == 0 else slice(SLOTS - WIN, SLOTS)


def own(group):
    base = OWN_T if group == 0 else OWN_B
    return slice(base, base + 64)


def quad_bias(base_ref, side, quad, group):
    shift = 0 if group == 0 else GROUP - (SLOTS - WIN)
    pieces = []
    for head in range(4 * quad, 4 * quad + 4):
        rows = base_ref[side, head]
        for col in range(8):
            turn = 8 * col + shift
            pieces.append(rows if turn == 0 else pltpu.roll(rows, turn, axis=1))
    return jnp.concatenate(pieces, axis=0)


def quad_rows(ref, quad, group):
    return jnp.concatenate(
        [jnp.broadcast_to(ref[head : head + 1, window(group)], (64, WIN)) for head in range(4 * quad, 4 * quad + 4)],
        axis=0,
    )


BLOCKS = [(quad, group) for quad in range(QUADS) for group in (0, 1)]


def query_probs(r):
    head_lane = lax.broadcasted_iota(jnp.int32, (64, 128), 1)
    levels = [jnp.zeros((64, 128), F32), jnp.zeros((64, 128), F32)]
    for quad, group in BLOCKS:
        query = split_quad(r.qkv[own(group), quad_lanes(quad)])
        scores = dot_nt(query, r.qkv[window(group), quad_lanes(quad, D)]) * 0.125
        scores = scores + quad_bias(r.base, 0, quad, group) + r.edge[0:1, window(group)]
        top = jnp.max(scores, axis=-1, keepdims=True)
        weight = jnp.exp(scores - top)
        total = jnp.sum(weight, axis=-1, keepdims=True)
        prob = (weight * (1.0 / total)).astype(BF16)
        r.prob_q[quad * 2 + group] = prob
        attn = merge_quad(dot(prob, r.qkv[window(group), quad_lanes(quad, 2 * D)]))
        r.ol[own(group), quad_lanes(quad)] = attn.astype(BF16)
        level = top + jnp.log(total)
        for head in range(4):
            levels[group] = jnp.where(
                head_lane == 4 * quad + head, level[head * 64 : (head + 1) * 64], levels[group]
            )
    for group in (0, 1):
        level = levels[group]
        high = level.astype(BF16).astype(F32)
        middle = (level - high).astype(BF16).astype(F32)
        low = level - high - middle
        packed = high + pltpu.roll(middle, 16, axis=1) + pltpu.roll(low, 32, axis=1)
        r.ol[own(group), D:OLW] = packed.astype(BF16)


def key_probs(r):
    for quad, group in BLOCKS:
        key = split_quad(r.qkv[own(group), quad_lanes(quad, D)])
        scores = dot_nt(key, r.qkv[window(group), quad_lanes(quad)]) * 0.125
        scores = scores + quad_bias(r.base, 1, quad, group) + r.edge[0:1, window(group)]
        r.prob_k[quad * 2 + group] = jnp.exp(scores - quad_rows(r.rows, quad, group)).astype(BF16)


def query_side(r, blocks):
    for quad, group in blocks:
        grad = r.ga[own(group), quad_lanes(quad)]
        delta = head_sums(grad.astype(F32) * r.ol[own(group), quad_lanes(quad)].astype(F32))
        prob_grad = dot_nt(split_quad(grad), r.qkv[window(group), quad_lanes(quad, 2 * D)])
        score_grad = r.prob_q[quad * 2 + group] * (prob_grad - delta).astype(BF16)
        query_grad = merge_quad(dot(score_grad, r.qkv[window(group), quad_lanes(quad, D)])) * 0.125
        r.dqkv[group * 64 : (group + 1) * 64, quad_lanes(quad)] = query_grad.astype(BF16)


def key_side(r):
    for quad, group in BLOCKS:
        value = split_quad(r.qkv[own(group), quad_lanes(quad, 2 * D)])
        prob_grad = dot_nt(value, r.ga[window(group), quad_lanes(quad)])
        prob = r.prob_k[quad * 2 + group]
        score_grad = prob * (prob_grad - quad_rows(r.rows, quad, group)).astype(BF16)
        key_grad = merge_quad(dot(score_grad, r.qkv[window(group), quad_lanes(quad)])) * 0.125
        value_grad = merge_quad(dot(prob, r.ga[window(group), quad_lanes(quad)]))
        rows = slice(group * 64, (group + 1) * 64)
        r.dqkv[rows, quad_lanes(quad, D)] = key_grad.astype(BF16)
        r.dqkv[rows, quad_lanes(quad, 2 * D)] = value_grad.astype(BF16)


def onehot(mask):
    return mask.astype(F32).astype(BF16)


def pack_shard(r, rows):
    at_row = lax.broadcasted_iota(jnp.int32, (16, 12), 0)
    at_col = lax.broadcasted_iota(jnp.int32, (16, 12), 1)
    whole = dot(onehot(at_row == at_col), r.qkv_in[...])
    for part in range(3):
        pick = onehot((at_row == 12 + at_col // 3) & (at_col % 3 == part))
        lanes = slice(part * D, (part + 1) * D)
        r.shards[rows, lanes] = (whole[:, lanes] + dot(pick, r.out_in[...])).astype(BF16)


def unpack_group(r, group, zs):
    rows = lax.broadcasted_iota(jnp.int32, (192, 256), 0)
    cols = lax.broadcasted_iota(jnp.int32, (192, 256), 1)
    shard = ((rows % 96) // 24) * 4 + ((rows % 24) // 12) * 2 + rows // 96
    feature = rows % 12
    source = pl.ds(pl.multiple_of(group * 256, 256), 256)
    low = pl.ds(pl.multiple_of(group * 96, 16), 96)
    high = pl.ds(pl.multiple_of(24 * zs + group * 96, 16), 96)
    block = dot(onehot(cols == shard * 16 + feature), r.shards[source, :]).astype(BF16)
    r.qkv_w[low, :] = block[:96]
    r.qkv_w[high, :] = block[96:]
    total = jnp.zeros((192, D), F32)
    for part in range(3):
        pick = onehot((cols == shard * 16 + 12 + feature // 3) & (feature % 3 == part))
        total = total + dot(pick, r.shards[source, part * D : (part + 1) * D])
    block = total.astype(BF16)
    r.out_w[low, :] = block[:96]
    r.out_w[high, :] = block[96:]


def half_order(rows, cols):
    return onehot(cols == (rows % 8) * TW + (rows // 64) * 8 + (rows % 64) // 8)


def fill_bias(r):
    span = 2 * RAD + 1
    table = r.table[...]
    high = table.astype(BF16)
    rest = table - high.astype(F32)
    middle = rest.astype(BF16)
    low = (rest - middle.astype(F32)).astype(BF16)
    index = lax.broadcasted_iota(jnp.int32, (span * span, WIN), 0)
    slot = lax.broadcasted_iota(jnp.int32, (1, WIN), 1)
    across = (slot % GROUP) // 8
    for row in range(8):
        up = 8 * (slot // GROUP - 1) + slot % 8 - row + RAD
        valid = (up >= 0) & (up < span) & (across < span) & (slot < 3 * GROUP)
        want = up * span + across
        for side in (0, 1):
            pick = onehot(index == (want if side == 0 else span * span - 1 - want))
            value = dot(high, pick) + dot(middle, pick) + dot(low, pick)
            value = jnp.where(valid, value, NEG_FILL)
            for head in range(HEADS):
                r.base[side, head, row : row + 1, :] = value[head : head + 1]


def fill_edge(r, place):
    slot = lax.broadcasted_iota(jnp.int32, (8, SLOTS), 1)
    group = slot // GROUP
    col = (slot % GROUP) // 8 - RAD
    first = jnp.where(place.z == 0, 0, -SLOTS)
    last = jnp.where(place.z == place.zs - 1, 7, SLOTS)
    top = jnp.where(place.has_up, 0, 1)
    bottom = jnp.where(place.has_down, 3, 2)
    outside = (col < first) | (col > last) | (group < top) | (group > bottom)
    r.edge[...] = jnp.where(outside, NEG_FILL, 0.0)


class Ring:
    def __init__(self, place, buf, send, recv, mate_send, mate_recv):
        self.place, self.buf = place, buf
        self.send, self.recv, self.mate_send, self.mate_recv = send, recv, mate_send, mate_recv
        self.half = place.zs // 2

    def rows(self, offset, core, which):
        z = (self.place.z + offset + self.place.zs) % self.place.zs
        yh = self.place.yh if which == 0 else 1 - self.place.yh
        return pl.ds(pl.multiple_of(((z * 2 + core) * 2 + yh) * 16, 16), 16)

    def copy(self, way, step, which, offset):
        part = self.buf.at[self.rows(offset, self.place.core, which)]
        device = self.place.right if way == 0 else self.place.left
        return remote(
            part, part, self.send.at[way, which, step], self.recv.at[way, which, step], (self.place.seg, device)
        )

    def has(self, way, step, which):
        return step < self.half - 1 or (step == self.half - 1 and which == way)

    def leave(self, way, step, which):
        return self.copy(way, step, which, -step if way == 0 else step)

    def arrive(self, way, step, which):
        return self.copy(way, step, which, -step - 1 if way == 0 else step + 1)

    def share(self, offset, which, core=None):
        core = self.place.core if core is None else core
        part = self.buf.at[self.rows(offset, core, which)]
        index = (offset + self.place.zs) % self.place.zs
        return remote(
            part, part, self.mate_send.at[which, index], self.mate_recv.at[which, index],
            (self.place.seg, self.place.mate),
        )

    def begin(self, which):
        self.leave(0, 0, which).start()
        self.leave(1, 0, which).start()
        self.share(0, which).start()

    def turn(self, step):
        for which in (0, 1):
            for way in (0, 1):
                if self.has(way, step, which):
                    self.arrive(way, step, which).wait_recv()
                    if self.has(way, step + 1, which):
                        self.leave(way, step + 1, which).start()
                    self.share(-step - 1 if way == 0 else step + 1, which).start()

    def wait_shared(self, group):
        for member in range(4):
            offset = (group * 4 + member - self.place.z + self.place.zs) % self.place.zs
            for which in (0, 1):
                self.share(offset, which, 1 - self.place.core).wait_recv()

    def wait_send(self):
        for which in (0, 1):
            for way in (0, 1):
                for step in range(self.half):
                    if self.has(way, step, which):
                        self.leave(way, step, which).wait_send()
            for offset in range(self.place.zs):
                self.share(offset, which).wait_send()


class Halo:
    def __init__(self, place, buf, send, recv, at, group, direct=False):
        base = pl.multiple_of(T0 + group * GROUP, 16)
        over = pl.multiple_of(3 * GROUP * (1 - group), 16)
        self.has = jnp.where(group == 0, one(place.has_up), one(place.has_down)) > 0
        self.gets = jnp.where(group == 0, one(place.has_down), one(place.has_up)) > 0

        def pick(up, down):
            return (place.seg, jnp.where(group == 0, up, down))

        def copy(role, src, rows, dst, device):
            index = at + 5 * group + role
            return remote(
                buf.at[pl.ds(src, rows)], buf.at[pl.ds(dst, rows)], send.at[index], recv.at[index], device
            )

        self.vertical = [copy(0, base + 48, 64, over + 48, pick(place.up, place.down))]
        self.corners = [
            copy(1, base + 48, 48, over + 112, pick(place.up_left, place.down_left)),
            copy(2, base + 64, 48, over, pick(place.up_right, place.down_right)),
        ]
        self.direct = direct
        self.beyond = self.has & ((group == place.core) if direct else True)
        self.expects = self.gets & ((group != place.core) if direct else True)
        self.sides = [
            copy(3, base + 48, 48, base + 112, (place.seg, place.left)),
            copy(4, base + 64, 48, base, (place.seg, place.right)),
        ]

    def start(self):
        @pl.when(self.beyond)
        def _():
            for copy in self.corners:
                copy.start()

        for copy in self.sides:
            copy.start()

        @pl.when(self.has)
        def _():
            for copy in self.vertical:
                copy.start()

    def wait_sides(self):
        for copy in self.sides:
            copy.wait_recv()

    def wait_vertical(self):
        @pl.when(self.gets)
        def _():
            for copy in self.vertical:
                copy.wait_recv()

        @pl.when(self.expects)
        def _():
            for copy in self.corners:
                copy.wait_recv()

    def wait_send(self):
        @pl.when(self.has)
        def _():
            for copy in self.vertical:
                copy.wait_send()

        @pl.when(self.beyond)
        def _():
            for copy in self.corners:
                copy.wait_send()

        for copy in self.sides:
            copy.wait_send()


def greet(place, barrier):
    seg = place.seg
    signal(barrier, (seg, place.left))
    signal(barrier, (seg, place.right))

    @pl.when(place.has_up)
    def _():
        for device in (place.up, place.up_left, place.up_right):
            signal(barrier, (seg, device))

    @pl.when(place.has_down)
    def _():
        for device in (place.down, place.down_left, place.down_right):
            signal(barrier, (seg, device))

    return 2 + 3 * one(place.has_up) + 3 * one(place.has_down)


def own_layer_norm(r):
    own_x = own_rows(r.slots, slice(0, D)).astype(F32)
    deviation = own_x - jnp.mean(own_x, axis=-1, keepdims=True)
    variance = jnp.mean(deviation * deviation, axis=-1, keepdims=True)
    own_inverse = lax.rsqrt(variance + EPSILON)
    r.normal[...] = deviation * own_inverse
    r.inverse[...] = jnp.broadcast_to(own_inverse, (128, 128))


def window_layer_norm(r):
    @pl.loop(0, 5)
    def _(chunk):
        rows = pl.ds(pl.multiple_of(chunk * 128, 128), 128)
        values = r.slots[rows, :].astype(F32)
        deviation = values - jnp.mean(values, axis=-1, keepdims=True)
        variance = jnp.mean(deviation * deviation, axis=-1, keepdims=True)
        part = deviation * lax.rsqrt(variance + EPSILON)
        r.normed[rows, :] = (part * r.gain[...]).astype(BF16)


REFS = [
    "x", "g", "gain", "table", "qkv_in", "out_in", "out",
    "shards", "xs", "slots", "top", "qkv_w", "out_w", "qkv_t", "out_t", "normed", "qkv", "prob_q", "prob_k", "ol",
    "gs", "ga", "po", "dqkv", "outb", "got", "lent", "normal", "inverse", "token", "rows", "base", "edge",
]


def main_kernel(tile_count, *refs):
    r = types.SimpleNamespace(**dict(zip(REFS, refs)))
    send, recv, local, ring_send, ring_recv, mate_send, mate_recv = refs[len(REFS) :]
    place = Place(tile_count)
    seg, zs = place.seg, place.zs
    last_seg = lax.axis_size("segment") - 1
    tiles = [place.tile_t, place.tile_b]
    blocks = [place.block_of(0), place.block_of(1)]
    barrier = pltpu.get_barrier_semaphore()
    helper = last_seg - 4
    count = greet(place, barrier) + 2 + 3 * one(seg > 0) + 3 * one(seg == helper) + 5 * one(seg == last_seg)
    signal(barrier, (seg, place.mate))
    signal(barrier, (seg, place.cross))

    @pl.when(seg < last_seg)
    def _():
        for device in (place.tile, place.mate_left, place.mate_right):
            signal(barrier, (seg + 1, device))

    @pl.when(seg == last_seg)
    def _():
        for device in (place.mate_left, place.mate_right):
            signal(barrier, (seg, device))

        for device in tiles:
            signal(barrier, (helper, device))

        signal(barrier, (helper, place.tile))

    @pl.when(seg == helper)
    def _():
        signal(barrier, (last_seg, place.tile))
        for device in blocks:
            signal(barrier, (last_seg, device))

    for device in tiles + blocks:

        @pl.when(device != place.tile)
        def _():
            signal(barrier, (seg, device))

        count = count + one(device != place.tile)

    ring = Ring(place, r.shards, ring_send, ring_recv, mate_send, mate_recv)
    pack_shard(r, ring.rows(0, place.core, 0))
    new_row = lax.broadcasted_iota(jnp.int32, (128, 128), 0)
    new_col = lax.broadcasted_iota(jnp.int32, (128, 128), 1)
    to_halves = half_order(new_row, new_col)
    r.xs[0:128, :] = dot(to_halves, r.x[...]).astype(BF16)
    for buf in (r.slots, r.ol, r.gs):
        clear_outside(place, buf)
    pl.semaphore_wait(barrier, count)

    mine = r.shards.at[ring.rows(0, place.core, 0)]
    theirs = r.shards.at[ring.rows(0, place.core, 1)]
    tile_group = place.row % 2
    x_at = OWN_T + tile_group * GROUP
    g_at = tile_group * 64

    def lend(part):
        rows = pl.ds(part * 128, 128)
        return remote(r.xs.at[rows], r.lent.at[rows], send.at[45 + part], recv.at[45 + part], (helper, place.tile))

    def forward(part, half):
        dst, at = ((r.slots, x_at), (r.top, g_at))[part]
        index = 2 * part + half
        return remote(
            r.lent.at[pl.ds(index * 64, 64)], dst.at[pl.ds(pl.multiple_of(at, 16), 64)],
            send.at[47 + index], recv.at[2 * part + tile_group], (last_seg, blocks[half]),
        )

    @pl.when(seg == last_seg)
    def _():
        lend(0).start()
        r.xs[128:256, :] = dot(to_halves, r.g[...]).astype(BF16)
        lend(1).start()

    @pl.when(seg == helper)
    def _():
        for part in (0, 1):
            lend(part).wait_recv()
            for half in (0, 1):
                forward(part, half).start()
        for part in (0, 1):
            for half in (0, 1):
                forward(part, half).wait_send()

    cross_send = remote(mine, mine, send.at[44], recv.at[44], (seg, place.cross))
    cross_send.start()
    ring.begin(0)

    def move(half):
        return remote(
            r.xs.at[pl.ds(half * 64, 64)], r.slots.at[pl.ds(pl.multiple_of(x_at, 16), 64)],
            send.at[half], recv.at[tile_group], (seg, blocks[half]),
        )

    def move_local(half):
        return pltpu.make_async_copy(
            r.xs.at[pl.ds(half * 64, 64)], r.slots.at[pl.ds(pl.multiple_of(x_at, 16), 64)], local.at[half]
        )

    for half in (0, 1):

        @pl.when((seg < last_seg) & (blocks[half] != place.tile))
        def _():
            move(half).start()

        @pl.when((seg < last_seg) & (blocks[half] == place.tile))
        def _():
            move_local(half).start()
            move_local(half).wait()

    def moves_wait_recv(part, dst, rows):
        for group in (0, 1):

            @pl.when((seg == last_seg) | (tiles[group] != place.tile))
            def _():
                index = 2 * part + group
                remote(
                    r.xs.at[0:64], dst.at[rows[group]], send.at[index], recv.at[index], (seg, place.left)
                ).wait_recv()

    remote(mine, theirs, send.at[44], recv.at[44], (seg, place.cross)).wait_recv()
    ring.begin(1)

    x_halos = [Halo(place, r.slots, send, recv, 4, group) for group in (0, 1)]
    near = jnp.where(place.z % 4 < 2, -1, 1)
    home = place.z // 4
    groups = zs // 4
    for step in range(ring.half):
        ring.turn(step)
        if step == 1:
            fill_edge(r, place)
            fill_bias(r)
        if step == ring.half - 5:
            moves_wait_recv(0, r.slots, [own(0), own(1)])
            for halo in x_halos:
                halo.start()
            own_layer_norm(r)
        if step == ring.half - 4:
            ring.wait_shared(home)
            unpack_group(r, home, zs)
        if step == ring.half - 3:
            ring.wait_shared((home + near + groups) % groups)
            unpack_group(r, (home + near + groups) % groups, zs)
        if step == ring.half - 2:
            for halo in x_halos:
                halo.wait_sides()
                halo.wait_vertical()
            window_layer_norm(r)
            ring.wait_shared((home - near + groups) % groups)
            unpack_group(r, (home - near + groups) % groups, zs)

    ring.wait_shared((home + 2) % groups)
    unpack_group(r, (home + 2) % groups, zs)
    r.qkv[...] = dot(r.normed[...], r.qkv_w[...]).astype(BF16)
    query_probs(r)

    ol_halos = [Halo(place, r.ol, send, recv, 14, group) for group in (0, 1)]
    for halo in ol_halos:
        halo.start()
    r.qkv_t[...] = r.qkv_w[...].T
    r.out_t[...] = r.out_w[...].T

    first, second = 1 - place.yh, place.yh

    def passing(group, index):
        rows = pl.multiple_of(group * 64, 16)
        slot = pl.multiple_of(OWN_T + group * GROUP, 16)
        return remote(
            r.outb.at[pl.ds(rows, 64)], r.gs.at[pl.ds(slot, 64)], send.at[index], recv.at[index],
            (jnp.maximum(seg - 1, 0), place.tile),
        )

    passes = [passing(first, 34), passing(second, 35)]
    gs_halos = [Halo(place, r.gs, send, recv, 24, group, True) for group in (first, second)]

    def mate_corners(src, base, device_seg):
        group = 1 - place.core
        over = pl.multiple_of(3 * GROUP * (1 - group), 16)
        return [
            remote(
                src.at[pl.ds(pl.multiple_of(base + skip, 16), 48)], r.gs.at[pl.ds(over + land, 48)],
                send.at[at], recv.at[at], (device_seg, device),
            )
            for skip, land, at, device in ((0, 112, 38, place.mate_left), (16, 0, 39, place.mate_right))
        ]

    below_corners = mate_corners(r.outb, 64 * (1 - place.core), jnp.maximum(seg - 1, 0))
    top_corners = mate_corners(r.gs, OWN_T + GROUP * (1 - place.core), seg)
    over = pl.multiple_of(3 * GROUP * (1 - place.core), 16)
    corner_arrivals = [
        remote(
            r.outb.at[0:48], r.gs.at[pl.ds(over + land, 48)], send.at[at], recv.at[at], (seg, place.left)
        )
        for land, at in ((112, 38), (0, 39))
    ]

    def as_queries():
        put_own(r.ga, slice(0, D), dot(own_rows(r.gs, slice(0, D)), r.out_t[...]).astype(BF16))
        query_side(r, BLOCKS)
        r.token[...] = dot(r.dqkv[:, 0:D], r.qkv_t[0:D, :])

    @pl.when(seg == last_seg)
    def _():
        moves_wait_recv(1, r.top, [slice(0, 64), slice(64, 128)])
        put_own(r.gs, slice(0, D), r.top[...])
        for halo in gs_halos:
            halo.start()
        for copy in top_corners:
            copy.start()
        as_queries()

    for halo in ol_halos:
        halo.wait_sides()
        halo.wait_vertical()
    thirds = lax.broadcasted_iota(jnp.int32, (16, 128), 1)
    head_row = lax.broadcasted_iota(jnp.int32, (16, 128), 0)
    r.rows[...] = dot_nt(onehot((thirds < 48) & (thirds % 16 == head_row)), r.ol[:, D:OLW])
    key_probs(r)

    @pl.when(seg < last_seg)
    def _():
        for one_pass, halo in zip(passes, gs_halos):
            one_pass.wait_recv()
            halo.start()
        as_queries()

    for halo in gs_halos:
        halo.wait_sides()
    middle = slice(T0, T0 + 2 * GROUP)
    r.ga[middle, :] = dot(r.gs[middle, :], r.out_t[...]).astype(BF16)
    for halo in gs_halos:
        halo.wait_vertical()
    for copy in corner_arrivals:
        copy.wait_recv()
    outer = jnp.concatenate([r.gs[0:GROUP, :], r.gs[3 * GROUP : SLOTS, :]], axis=0)
    outer = dot(outer, r.out_t[...]).astype(BF16)
    r.ga[0:GROUP, :] = outer[:GROUP]
    r.ga[3 * GROUP : SLOTS, :] = outer[GROUP:]
    wide = lax.broadcasted_iota(jnp.int32, (16, D), 1)
    head_wide = lax.broadcasted_iota(jnp.int32, (16, D), 0)
    r.po[...] = r.ga[...] * r.ol[:, 0:D]
    r.rows[...] = dot_nt(onehot(wide // 64 == head_wide), r.po[...])
    key_side(r)

    token = r.token[...] + dot(r.dqkv[:, D:WIDE], r.qkv_t[D:WIDE, :])
    scaled = token * r.gain[...]
    part = r.normal[...]
    first_mean = jnp.mean(scaled, axis=-1, keepdims=True)
    second_mean = jnp.mean(scaled * part, axis=-1, keepdims=True)
    branch = r.inverse[:, 0:1] * (scaled - first_mean - part * second_mean)
    r.outb[...] = (own_rows(r.gs, slice(0, D)).astype(F32) + branch).astype(BF16)

    @pl.when(seg > 0)
    def _():
        for one_pass in passes:
            one_pass.start()
        for copy in below_corners:
            copy.start()

    row_at = pl.multiple_of(place.half * 64, 16)

    def back(group):
        return remote(
            r.outb.at[pl.ds(group * 64, 64)], r.got.at[pl.ds(row_at, 64)],
            send.at[36 + group], recv.at[36 + place.half], (seg, tiles[group]),
        )

    def back_local(group):
        return pltpu.make_async_copy(r.outb.at[pl.ds(group * 64, 64)], r.got.at[pl.ds(row_at, 64)], local.at[4 + group])

    for group in (0, 1):

        @pl.when(tiles[group] != place.tile)
        def _():
            back(group).start()

        @pl.when(tiles[group] == place.tile)
        def _():
            back_local(group).start()
            back_local(group).wait()

    ring.wait_send()
    cross_send.wait_send()

    @pl.when(seg == last_seg)
    def _():
        lend(0).wait_send()
        lend(1).wait_send()

    for half in (0, 1):

        @pl.when((seg < last_seg) & (blocks[half] != place.tile))
        def _():
            move(half).wait_send()

    for halo in x_halos + ol_halos + gs_halos:
        halo.wait_send()

    for half in (0, 1):

        @pl.when(blocks[half] != place.tile)
        def _():
            remote(
                r.outb.at[0:64], r.got.at[pl.ds(half * 64, 64)], send.at[36 + half], recv.at[36 + half],
                (seg, place.left),
            ).wait_recv()

    r.out[...] = dot(half_order(new_col, new_row), r.got[...]).astype(BF16)

    for group in (0, 1):

        @pl.when(tiles[group] != place.tile)
        def _():
            back(group).wait_send()

    @pl.when(seg > 0)
    def _():
        for copy in passes + below_corners:
            copy.wait_send()

    @pl.when(seg == last_seg)
    def _():
        for copy in top_corners:
            copy.wait_send()


def main(x, g, gain, table, qkv_in, out_in, tile_count):
    zs = tile_count // 4
    vmem = pl.BlockSpec(memory_space=pltpu.VMEM)
    bf16 = [
        (zs * 64, WIDE), (256, D), (SLOTS, D), (128, D), (D, WIDE), (D, D), (WIDE, D), (D, D), (SLOTS, D), (SLOTS, WIDE),
        (6, 256, WIN), (6, 256, WIN), (SLOTS, OLW), (SLOTS, D), (SLOTS, D), (SLOTS, D), (128, WIDE), (128, D), (128, D),
        (256, D),
    ]
    f32 = [(128, D), (128, 128), (128, D), (16, SLOTS), (2, HEADS, 8, WIN), (8, SLOTS)]
    return pl.pallas_call(
        functools.partial(main_kernel, tile_count),
        out_shape=jax.ShapeDtypeStruct((128, D), BF16),
        in_specs=[vmem] * 6,
        out_specs=vmem,
        scratch_shapes=[pltpu.VMEM(shape, BF16) for shape in bf16]
        + [pltpu.VMEM(shape, F32) for shape in f32]
        + [
            pltpu.SemaphoreType.DMA((51,)),
            pltpu.SemaphoreType.DMA((51,)),
            pltpu.SemaphoreType.DMA((6,)),
            pltpu.SemaphoreType.DMA((2, 2, zs // 2)),
            pltpu.SemaphoreType.DMA((2, 2, zs // 2)),
            pltpu.SemaphoreType.DMA((2, zs)),
            pltpu.SemaphoreType.DMA((2, zs)),
        ],
        compiler_params=pltpu.CompilerParams(
            collective_id=0, has_side_effects=True, vmem_limit_bytes=58 * 2**20
        ),
    )(x, g, gain, table, qkv_in, out_in)


def body(stored_inputs, output_grads, norm_gain, position_bias, qkv_weight, out_weight):
    tokens = TH * TW
    out = main(
        stored_inputs.reshape(tokens, D), output_grads.reshape(tokens, D), norm_gain,
        position_bias.reshape(HEADS, -1), qkv_weight[0], out_weight[0], lax.axis_size("tile"),
    )
    return out.reshape(1, 1, 1, TH, TW, D)


def solution(mesh):
    return jax.shard_map(
        body,
        mesh=mesh,
        in_specs=(
            P("segment", None, "tile", None, None, None),
            P(None, "tile", None, None, None),
            P("segment", None),
            P("segment", None, None, None),
            P("segment", "tile", None),
            P("segment", "tile", None),
        ),
        out_specs=P("segment", None, "tile", None, None, None),
        check_vma=False,
    )
```

```python
import functools
import types

import jax
import jax.numpy as jnp
from jax import lax
from jax.experimental import pallas as pl
from jax.experimental.pallas import tpu as pltpu
from jax.sharding import PartitionSpec as P

D = 768
HEADS = 12
RAD = 6
TH = 8
TW = 16
WIDE = 3 * D
OLW = D + 128
EPSILON = 1e-05
NEG_FILL = -1e30
MESH = pl.DeviceIdType.MESH
BF16 = jnp.bfloat16
F32 = jnp.float32

SLOTS = 640
GROUP = 160
T0, B0 = GROUP, 2 * GROUP
OWN_T, OWN_B = T0 + 48, B0 + 48


class Place:
    def __init__(self, tile_count):
        self.zs = tile_count // 4
        self.cols = self.zs // 2
        self.seg = lax.axis_index("segment")
        self.tile = lax.axis_index("tile")
        self.yh = self.tile // (2 * self.zs)
        self.z = (self.tile % (2 * self.zs)) // 2
        self.core = self.tile % 2
        self.rb = self.yh * 2 + self.core
        self.left = self.at(self.yh, (self.z + self.zs - 1) % self.zs, self.core)
        self.right = self.at(self.yh, (self.z + 1) % self.zs, self.core)
        self.mate = self.at(self.yh, self.z, 1 - self.core)
        self.cross = self.at(1 - self.yh, self.z, self.core)
        self.has_up = self.rb > 0
        self.has_down = self.rb < 3
        up = (self.rb + 3) % 4
        down = (self.rb + 1) % 4
        self.up = self.at(up // 2, self.z, up % 2)
        self.down = self.at(down // 2, self.z, down % 2)
        z_left, z_right = (self.z + self.zs - 1) % self.zs, (self.z + 1) % self.zs
        self.up_left = self.at(up // 2, z_left, up % 2)
        self.up_right = self.at(up // 2, z_right, up % 2)
        self.down_left = self.at(down // 2, z_left, down % 2)
        self.down_right = self.at(down // 2, z_right, down % 2)
        self.row = self.tile // self.cols
        self.col = self.tile % self.cols
        self.half = self.z % 2
        self.tile_t = (2 * self.rb) * self.cols + self.z // 2
        self.tile_b = (2 * self.rb + 1) * self.cols + self.z // 2

    def at(self, yh, z, core):
        return yh * (2 * self.zs) + z * 2 + core

    def block_of(self, half):
        rb = self.row // 2
        return self.at(rb // 2, 2 * self.col + half, rb % 2)


def remote(src, dst, send, recv, device):
    return pltpu.make_async_remote_copy(
        src_ref=src, dst_ref=dst, send_sem=send, recv_sem=recv, device_id=device, device_id_type=MESH
    )


def signal(sem, device):
    pl.semaphore_signal(sem, inc=1, device_id=device, device_id_type=MESH)


def one(flag):
    return jnp.where(flag, 1, 0).astype(jnp.int32)


def clear_outside(place, buf):
    blank = jnp.zeros((GROUP, buf.shape[1]), buf.dtype)

    @pl.when(jnp.logical_not(place.has_up))
    def _():
        buf[0:GROUP, :] = blank

    @pl.when(jnp.logical_not(place.has_down))
    def _():
        buf[3 * GROUP : SLOTS, :] = blank


def dot(left, right):
    return jnp.dot(left, right, preferred_element_type=F32)


def dot_nt(left, right):
    return lax.dot_general(left, right, (((1,), (1,)), ((), ())), preferred_element_type=F32)


def own_rows(ref, lanes):
    return jnp.concatenate([ref[OWN_T : OWN_T + 64, lanes], ref[OWN_B : OWN_B + 64, lanes]], axis=0)


def put_own(ref, lanes, value):
    ref[OWN_T : OWN_T + 64, lanes] = value[:64]
    ref[OWN_B : OWN_B + 64, lanes] = value[64:]


QUADS = 3
WIN = 512


def low_lanes(rows):
    return lax.broadcasted_iota(jnp.int32, (rows, 128), 1) < 64


def split_quad(value):
    low = low_lanes(64)
    zero = jnp.zeros((64, 128), value.dtype)
    rows = []
    for part in (0, 1):
        piece = value[:, part * 128 : (part + 1) * 128]
        for keep in (jnp.where(low, piece, zero), jnp.where(low, zero, piece)):
            rows.append(jnp.concatenate([keep, zero] if part == 0 else [zero, keep], axis=1))
    return jnp.concatenate(rows, axis=0)


def merge_quad(value):
    low = low_lanes(64)
    return jnp.concatenate(
        [
            jnp.where(low, value[0:64, :128], value[64:128, :128]),
            jnp.where(low, value[128:192, 128:], value[192:256, 128:]),
        ],
        axis=1,
    )


def head_sums(value):
    low = low_lanes(64)
    sums = []
    for part in (0, 1):
        piece = value[:, part * 128 : (part + 1) * 128]
        sums.append(jnp.sum(jnp.where(low, piece, 0.0), axis=-1, keepdims=True))
        sums.append(jnp.sum(jnp.where(low, 0.0, piece), axis=-1, keepdims=True))
    return jnp.concatenate(sums, axis=0)


def quad_lanes(quad, offset=0):
    return slice(offset + quad * 256, offset + (quad + 1) * 256)


def span(start, size, unit):
    return pl.ds(start if isinstance(start, int) else pl.multiple_of(start, unit), size)


def window(group):
    return span(group * (SLOTS - WIN), WIN, 128)


def own(group):
    return span(OWN_T + group * GROUP, 64, 16)


def half(group):
    return span(group * 64, 64, 16)


def quad_bias(base_ref, side, quad, group):
    shift = 0 if group == 0 else GROUP - (SLOTS - WIN)
    pieces = []
    for head in range(4 * quad, 4 * quad + 4):
        rows = base_ref[side, head]
        for col in range(8):
            turn = 8 * col + shift
            pieces.append(rows if turn == 0 else pltpu.roll(rows, turn, axis=1))
    return jnp.concatenate(pieces, axis=0)


def quad_rows(ref, quad, group):
    return jnp.concatenate(
        [jnp.broadcast_to(ref[head : head + 1, window(group)], (64, WIN)) for head in range(4 * quad, 4 * quad + 4)],
        axis=0,
    )


BLOCKS = [(quad, group) for quad in range(QUADS) for group in (0, 1)]


def query_probs(r):
    head_lane = lax.broadcasted_iota(jnp.int32, (64, 128), 1)
    levels = [jnp.zeros((64, 128), F32), jnp.zeros((64, 128), F32)]
    for quad, group in BLOCKS:
        query = split_quad(r.qkv[own(group), quad_lanes(quad)])
        scores = dot_nt(query, r.qkv[window(group), quad_lanes(quad, D)]) * 0.125
        scores = scores + quad_bias(r.base, 0, quad, group) + r.edge[0:1, window(group)]
        top = jnp.max(scores, axis=-1, keepdims=True)
        weight = jnp.exp(scores - top)
        total = jnp.sum(weight, axis=-1, keepdims=True)
        prob = (weight * (1.0 / total)).astype(BF16)
        r.prob_q[quad * 2 + group] = prob
        attn = merge_quad(dot(prob, r.qkv[window(group), quad_lanes(quad, 2 * D)]))
        r.ol[own(group), quad_lanes(quad)] = attn.astype(BF16)
        level = top + jnp.log(total)
        for head in range(4):
            levels[group] = jnp.where(
                head_lane == 4 * quad + head, level[head * 64 : (head + 1) * 64], levels[group]
            )
    for group in (0, 1):
        level = levels[group]
        high = level.astype(BF16).astype(F32)
        middle = (level - high).astype(BF16).astype(F32)
        low = level - high - middle
        packed = high + pltpu.roll(middle, 16, axis=1) + pltpu.roll(low, 32, axis=1)
        r.ol[own(group), D:OLW] = packed.astype(BF16)


def key_probs(r):
    for quad, group in BLOCKS:
        key = split_quad(r.qkv[own(group), quad_lanes(quad, D)])
        scores = dot_nt(key, r.qkv[window(group), quad_lanes(quad)]) * 0.125
        scores = scores + quad_bias(r.base, 1, quad, group) + r.edge[0:1, window(group)]
        r.prob_k[quad * 2 + group] = jnp.exp(scores - quad_rows(r.rows, quad, group)).astype(BF16)


def query_side(r, group):
    for quad in range(QUADS):
        grad = r.ga[own(group), quad_lanes(quad)]
        delta = head_sums(grad.astype(F32) * r.ol[own(group), quad_lanes(quad)].astype(F32))
        prob_grad = dot_nt(split_quad(grad), r.qkv[window(group), quad_lanes(quad, 2 * D)])
        score_grad = r.prob_q[quad * 2 + group] * (prob_grad - delta).astype(BF16)
        query_grad = merge_quad(dot(score_grad, r.qkv[window(group), quad_lanes(quad, D)])) * 0.125
        r.dqkv[half(group), quad_lanes(quad)] = query_grad.astype(BF16)


def key_side(r, group):
    for quad in range(QUADS):
        value = split_quad(r.qkv[own(group), quad_lanes(quad, 2 * D)])
        prob_grad = dot_nt(value, r.ga[window(group), quad_lanes(quad)])
        prob = r.prob_k[quad * 2 + group]
        score_grad = prob * (prob_grad - quad_rows(r.rows, quad, group)).astype(BF16)
        key_grad = merge_quad(dot(score_grad, r.qkv[window(group), quad_lanes(quad)])) * 0.125
        value_grad = merge_quad(dot(prob, r.ga[window(group), quad_lanes(quad)]))
        r.dqkv[half(group), quad_lanes(quad, D)] = key_grad.astype(BF16)
        r.dqkv[half(group), quad_lanes(quad, 2 * D)] = value_grad.astype(BF16)


def attn_grads(r, regions):
    rows = [span(region * GROUP, GROUP, 16) for region in regions]
    grads = jnp.concatenate([r.gs[at, :] for at in rows], axis=0)
    grads = dot(grads, r.out_t[...]).astype(BF16)
    attn = jnp.concatenate([r.ol[at, 0:D] for at in rows], axis=0)
    wide = lax.broadcasted_iota(jnp.int32, (16, D), 1)
    head_wide = lax.broadcasted_iota(jnp.int32, (16, D), 0)
    deltas = dot_nt(onehot(wide // 64 == head_wide), grads * attn)
    for index, region in enumerate(regions):
        part = slice(index * GROUP, (index + 1) * GROUP)
        r.ga[rows[index], :] = grads[part]
        r.deltas[region, :, 0:GROUP] = deltas[:, part]


def join_deltas(r):
    r.rows[...] = jnp.concatenate([r.deltas[region, :, 0:GROUP] for region in range(4)], axis=1)


def finish(r, group):
    rows = half(group)
    token = r.token[rows, :] + dot(r.dqkv[rows, D:WIDE], r.qkv_t[D:WIDE, :])
    scaled = token * r.gain[...]
    part = r.normal[rows, :]
    first_mean = jnp.mean(scaled, axis=-1, keepdims=True)
    second_mean = jnp.mean(scaled * part, axis=-1, keepdims=True)
    branch = r.inverse[rows, 0:1] * (scaled - first_mean - part * second_mean)
    r.outb[rows, :] = (r.gs[own(group), :].astype(F32) + branch).astype(BF16)


def onehot(mask):
    return mask.astype(F32).astype(BF16)


def pack_shard(r, rows):
    at_row = lax.broadcasted_iota(jnp.int32, (16, 12), 0)
    at_col = lax.broadcasted_iota(jnp.int32, (16, 12), 1)
    whole = dot(onehot(at_row == at_col), r.qkv_in[...])
    for part in range(3):
        pick = onehot((at_row == 12 + at_col // 3) & (at_col % 3 == part))
        lanes = slice(part * D, (part + 1) * D)
        r.shards[rows, lanes] = (whole[:, lanes] + dot(pick, r.out_in[...])).astype(BF16)


def unpack_group(r, group, zs):
    rows = lax.broadcasted_iota(jnp.int32, (192, 256), 0)
    cols = lax.broadcasted_iota(jnp.int32, (192, 256), 1)
    shard = ((rows % 96) // 24) * 4 + ((rows % 24) // 12) * 2 + rows // 96
    feature = rows % 12
    source = pl.ds(pl.multiple_of(group * 256, 256), 256)
    low = pl.ds(pl.multiple_of(group * 96, 16), 96)
    high = pl.ds(pl.multiple_of(24 * zs + group * 96, 16), 96)
    block = dot(onehot(cols == shard * 16 + feature), r.shards[source, :]).astype(BF16)
    r.qkv_w[low, :] = block[:96]
    r.qkv_w[high, :] = block[96:]
    total = jnp.zeros((192, D), F32)
    for part in range(3):
        pick = onehot((cols == shard * 16 + 12 + feature // 3) & (feature % 3 == part))
        total = total + dot(pick, r.shards[source, part * D : (part + 1) * D])
    block = total.astype(BF16)
    r.out_w[low, :] = block[:96]
    r.out_w[high, :] = block[96:]


def half_order(rows, cols):
    return onehot(cols == (rows % 8) * TW + (rows // 64) * 8 + (rows % 64) // 8)


def fill_bias(r):
    span = 2 * RAD + 1
    table = r.table[...]
    high = table.astype(BF16)
    rest = table - high.astype(F32)
    middle = rest.astype(BF16)
    low = (rest - middle.astype(F32)).astype(BF16)
    index = lax.broadcasted_iota(jnp.int32, (span * span, WIN), 0)
    slot = lax.broadcasted_iota(jnp.int32, (1, WIN), 1)
    across = (slot % GROUP) // 8
    for row in range(8):
        up = 8 * (slot // GROUP - 1) + slot % 8 - row + RAD
        valid = (up >= 0) & (up < span) & (across < span) & (slot < 3 * GROUP)
        want = up * span + across
        for side in (0, 1):
            pick = onehot(index == (want if side == 0 else span * span - 1 - want))
            value = dot(high, pick) + dot(middle, pick) + dot(low, pick)
            value = jnp.where(valid, value, NEG_FILL)
            for head in range(HEADS):
                r.base[side, head, row : row + 1, :] = value[head : head + 1]


def fill_edge(r, place):
    slot = lax.broadcasted_iota(jnp.int32, (8, SLOTS), 1)
    group = slot // GROUP
    col = (slot % GROUP) // 8 - RAD
    first = jnp.where(place.z == 0, 0, -SLOTS)
    last = jnp.where(place.z == place.zs - 1, 7, SLOTS)
    top = jnp.where(place.has_up, 0, 1)
    bottom = jnp.where(place.has_down, 3, 2)
    outside = (col < first) | (col > last) | (group < top) | (group > bottom)
    r.edge[...] = jnp.where(outside, NEG_FILL, 0.0)


class Ring:
    def __init__(self, place, buf, send, recv, mate_send, mate_recv):
        self.place, self.buf = place, buf
        self.send, self.recv, self.mate_send, self.mate_recv = send, recv, mate_send, mate_recv
        self.half = place.zs // 2

    def rows(self, offset, core, which):
        z = (self.place.z + offset + self.place.zs) % self.place.zs
        yh = self.place.yh if which == 0 else 1 - self.place.yh
        return pl.ds(pl.multiple_of(((z * 2 + core) * 2 + yh) * 16, 16), 16)

    def copy(self, way, step, which, offset):
        part = self.buf.at[self.rows(offset, self.place.core, which)]
        device = self.place.right if way == 0 else self.place.left
        return remote(
            part, part, self.send.at[way, which, step], self.recv.at[way, which, step], (self.place.seg, device)
        )

    def has(self, way, step, which):
        return step < self.half - 1 or (step == self.half - 1 and which == way)

    def leave(self, way, step, which):
        return self.copy(way, step, which, -step if way == 0 else step)

    def arrive(self, way, step, which):
        return self.copy(way, step, which, -step - 1 if way == 0 else step + 1)

    def share(self, offset, which, core=None):
        core = self.place.core if core is None else core
        part = self.buf.at[self.rows(offset, core, which)]
        index = (offset + self.place.zs) % self.place.zs
        return remote(
            part, part, self.mate_send.at[which, index], self.mate_recv.at[which, index],
            (self.place.seg, self.place.mate),
        )

    def begin(self, which):
        self.leave(0, 0, which).start()
        self.leave(1, 0, which).start()
        self.share(0, which).start()

    def turn(self, step):
        for which in (0, 1):
            for way in (0, 1):
                if self.has(way, step, which):
                    self.arrive(way, step, which).wait_recv()
                    if self.has(way, step + 1, which):
                        self.leave(way, step + 1, which).start()
                    self.share(-step - 1 if way == 0 else step + 1, which).start()

    def wait_shared(self, group):
        for member in range(4):
            offset = (group * 4 + member - self.place.z + self.place.zs) % self.place.zs
            for which in (0, 1):
                self.share(offset, which, 1 - self.place.core).wait_recv()

    def wait_send(self):
        for which in (0, 1):
            for way in (0, 1):
                for step in range(self.half):
                    if self.has(way, step, which):
                        self.leave(way, step, which).wait_send()
            for offset in range(self.place.zs):
                self.share(offset, which).wait_send()


class Halo:
    def __init__(self, place, buf, send, recv, at, group, relay=False):
        base = pl.multiple_of(T0 + group * GROUP, 16)
        over = pl.multiple_of(3 * GROUP * (1 - group), 16)
        self.has = jnp.where(group == 0, one(place.has_up), one(place.has_down)) > 0
        self.gets = jnp.where(group == 0, one(place.has_down), one(place.has_up)) > 0

        def pick(up, down):
            return (place.seg, jnp.where(group == 0, up, down))

        def copy(role, src, rows, dst, device):
            index = at + 5 * group + role
            return remote(
                buf.at[pl.ds(src, rows)], buf.at[pl.ds(dst, rows)], send.at[index], recv.at[index], device
            )

        self.vertical = [copy(0, base + 48, 64, over + 48, pick(place.up, place.down))]
        self.corners = [
            copy(1, base + 48, 48, over + 112, pick(place.up_left, place.down_left)),
            copy(2, base + 64, 48, over, pick(place.up_right, place.down_right)),
        ]
        self.beyond = self.has & ((group == place.core) if relay else True)
        self.expects = self.gets & ((group != place.core) if relay else True)
        self.sides = [
            copy(3, base + 48, 48, base + 112, (place.seg, place.left)),
            copy(4, base + 64, 48, base, (place.seg, place.right)),
        ]

    def start(self):
        @pl.when(self.beyond)
        def _():
            for copy in self.corners:
                copy.start()

        for copy in self.sides:
            copy.start()

        @pl.when(self.has)
        def _():
            for copy in self.vertical:
                copy.start()

    def wait_sides(self):
        for copy in self.sides:
            copy.wait_recv()

    def wait_vertical(self):
        @pl.when(self.gets)
        def _():
            for copy in self.vertical:
                copy.wait_recv()

        @pl.when(self.expects)
        def _():
            for copy in self.corners:
                copy.wait_recv()

    def wait_send(self):
        @pl.when(self.has)
        def _():
            for copy in self.vertical:
                copy.wait_send()

        @pl.when(self.beyond)
        def _():
            for copy in self.corners:
                copy.wait_send()

        for copy in self.sides:
            copy.wait_send()


def greet(place, barrier):
    seg = place.seg
    signal(barrier, (seg, place.left))
    signal(barrier, (seg, place.right))

    @pl.when(place.has_up)
    def _():
        for device in (place.up, place.up_left, place.up_right):
            signal(barrier, (seg, device))

    @pl.when(place.has_down)
    def _():
        for device in (place.down, place.down_left, place.down_right):
            signal(barrier, (seg, device))

    return 2 + 3 * one(place.has_up) + 3 * one(place.has_down)


def own_layer_norm(r):
    own_x = own_rows(r.slots, slice(0, D)).astype(F32)
    deviation = own_x - jnp.mean(own_x, axis=-1, keepdims=True)
    variance = jnp.mean(deviation * deviation, axis=-1, keepdims=True)
    own_inverse = lax.rsqrt(variance + EPSILON)
    r.normal[...] = deviation * own_inverse
    r.inverse[...] = jnp.broadcast_to(own_inverse, (128, 128))


def window_layer_norm(r):
    @pl.loop(0, 5)
    def _(chunk):
        rows = pl.ds(pl.multiple_of(chunk * 128, 128), 128)
        values = r.slots[rows, :].astype(F32)
        deviation = values - jnp.mean(values, axis=-1, keepdims=True)
        variance = jnp.mean(deviation * deviation, axis=-1, keepdims=True)
        part = deviation * lax.rsqrt(variance + EPSILON)
        r.normed[rows, :] = (part * r.gain[...]).astype(BF16)


REFS = [
    "x", "g", "gain", "table", "qkv_in", "out_in", "out",
    "shards", "xs", "slots", "top", "qkv_w", "out_w", "qkv_t", "out_t", "normed", "qkv", "prob_q", "prob_k", "ol",
    "gs", "ga", "dqkv", "outb", "got", "lent", "normal", "inverse", "token", "rows", "deltas", "base", "edge",
]


def main_kernel(tile_count, *refs):
    r = types.SimpleNamespace(**dict(zip(REFS, refs)))
    send, recv, local, ring_send, ring_recv, mate_send, mate_recv = refs[len(REFS) :]
    place = Place(tile_count)
    seg, zs = place.seg, place.zs
    last_seg = lax.axis_size("segment") - 1
    tiles = [place.tile_t, place.tile_b]
    blocks = [place.block_of(0), place.block_of(1)]
    barrier = pltpu.get_barrier_semaphore()
    helper = last_seg - 4
    count = greet(place, barrier) + 2 + one(seg > 0) + 3 * one(seg == helper) + 3 * one(seg == last_seg)
    signal(barrier, (seg, place.mate))
    signal(barrier, (seg, place.cross))

    @pl.when(seg < last_seg)
    def _():
        signal(barrier, (seg + 1, place.tile))

    @pl.when(seg == last_seg)
    def _():
        for device in tiles:
            signal(barrier, (helper, device))

        signal(barrier, (helper, place.tile))

    @pl.when(seg == helper)
    def _():
        signal(barrier, (last_seg, place.tile))
        for device in blocks:
            signal(barrier, (last_seg, device))

    @pl.when(seg == 4)
    def _():
        signal(barrier, (0, place.tile))

    @pl.when((seg == 0) & (place.row % 2 == 1))
    def _():
        for device in blocks:
            signal(barrier, (4, device))

    count = count + one(seg == 0) + one(seg == 4)
    for device in tiles + blocks:

        @pl.when(device != place.tile)
        def _():
            signal(barrier, (seg, device))

        count = count + one(device != place.tile)

    ring = Ring(place, r.shards, ring_send, ring_recv, mate_send, mate_recv)
    pack_shard(r, ring.rows(0, place.core, 0))
    new_row = lax.broadcasted_iota(jnp.int32, (128, 128), 0)
    new_col = lax.broadcasted_iota(jnp.int32, (128, 128), 1)
    to_halves = half_order(new_row, new_col)
    r.xs[0:128, :] = dot(to_halves, r.x[...]).astype(BF16)
    for buf in (r.slots, r.ol, r.gs):
        clear_outside(place, buf)
    r.ga[...] = jnp.zeros_like(r.ga)
    r.deltas[...] = jnp.zeros_like(r.deltas)
    pl.semaphore_wait(barrier, count)

    mine = r.shards.at[ring.rows(0, place.core, 0)]
    theirs = r.shards.at[ring.rows(0, place.core, 1)]
    tile_group = place.row % 2
    x_at = OWN_T + tile_group * GROUP
    g_at = tile_group * 64

    def lend(part):
        rows = pl.ds(part * 128, 128)
        return remote(r.xs.at[rows], r.lent.at[rows], send.at[45 + part], recv.at[45 + part], (helper, place.tile))

    def forward(part, side_half):
        dst, at = ((r.slots, x_at), (r.top, g_at))[part]
        index = 2 * part + side_half
        return remote(
            r.lent.at[pl.ds(index * 64, 64)], dst.at[pl.ds(pl.multiple_of(at, 16), 64)],
            send.at[47 + index], recv.at[2 * part + tile_group], (last_seg, blocks[side_half]),
        )

    @pl.when(seg == helper)
    def _():
        for part in (0, 1):
            lend(part).wait_recv()
            for side_half in (0, 1):
                forward(part, side_half).start()
        for part in (0, 1):
            for side_half in (0, 1):
                forward(part, side_half).wait_send()

    cross_send = remote(mine, mine, send.at[44], recv.at[44], (seg, place.cross))
    cross_send.start()
    ring.begin(0)

    def move(side_half):
        return remote(
            r.xs.at[pl.ds(side_half * 64, 64)], r.slots.at[pl.ds(pl.multiple_of(x_at, 16), 64)],
            send.at[side_half], recv.at[tile_group], (seg, blocks[side_half]),
        )

    def move_local(side_half):
        return pltpu.make_async_copy(
            r.xs.at[pl.ds(side_half * 64, 64)], r.slots.at[pl.ds(pl.multiple_of(x_at, 16), 64)], local.at[side_half]
        )

    for side_half in (0, 1):

        @pl.when((seg < last_seg) & (blocks[side_half] != place.tile))
        def _():
            move(side_half).start()

        @pl.when((seg < last_seg) & (blocks[side_half] == place.tile))
        def _():
            move_local(side_half).start()
            move_local(side_half).wait()

    def moves_wait_recv(part, dst, rows):
        for group in (0, 1):

            @pl.when((seg == last_seg) | (tiles[group] != place.tile))
            def _():
                index = 2 * part + group
                remote(
                    r.xs.at[0:64], dst.at[rows[group]], send.at[index], recv.at[index], (seg, place.left)
                ).wait_recv()

    remote(mine, theirs, send.at[44], recv.at[44], (seg, place.cross)).wait_recv()
    ring.begin(1)

    @pl.when(seg == last_seg)
    def _():
        lend(0).start()
        r.xs[128:256, :] = dot(to_halves, r.g[...]).astype(BF16)

    x_halos = [Halo(place, r.slots, send, recv, 4, group) for group in (0, 1)]
    near = jnp.where(place.z % 4 < 2, -1, 1)
    home = place.z // 4
    groups = zs // 4
    for step in range(ring.half):
        ring.turn(step)
        if step == 2:

            @pl.when(seg == last_seg)
            def _():
                lend(1).start()

        if step == 1:
            fill_edge(r, place)
            fill_bias(r)
        if step == ring.half - 5:
            moves_wait_recv(0, r.slots, [own(0), own(1)])
            for halo in x_halos:
                halo.start()
            own_layer_norm(r)
        if step == ring.half - 4:
            ring.wait_shared(home)
            unpack_group(r, home, zs)
        if step == ring.half - 3:
            ring.wait_shared((home + near + groups) % groups)
            unpack_group(r, (home + near + groups) % groups, zs)
        if step == ring.half - 2:
            for halo in x_halos:
                halo.wait_sides()
                halo.wait_vertical()
            window_layer_norm(r)
            ring.wait_shared((home - near + groups) % groups)
            unpack_group(r, (home - near + groups) % groups, zs)

    ring.wait_shared((home + 2) % groups)
    unpack_group(r, (home + 2) % groups, zs)
    r.qkv[...] = dot(r.normed[...], r.qkv_w[...]).astype(BF16)
    query_probs(r)

    ol_halos = [Halo(place, r.ol, send, recv, 14, group) for group in (0, 1)]
    for halo in ol_halos:
        halo.start()
    r.qkv_t[...] = r.qkv_w[...].T
    r.out_t[...] = r.out_w[...].T

    first, second = place.core, 1 - place.core

    def passing(group, index):
        rows = pl.multiple_of(group * 64, 16)
        slot = pl.multiple_of(OWN_T + group * GROUP, 16)
        return remote(
            r.outb.at[pl.ds(rows, 64)], r.gs.at[pl.ds(slot, 64)], send.at[index], recv.at[index],
            (jnp.maximum(seg - 1, 0), place.tile),
        )

    passes = [passing(first, 34), passing(second, 35)]
    gs_halos = [Halo(place, r.gs, send, recv, 24, group, True) for group in (first, second)]

    relay_group = 1 - place.core
    side_at = pl.multiple_of(T0 + GROUP * relay_group, 16)
    over = pl.multiple_of(3 * GROUP * place.core, 16)
    corners = [
        remote(
            r.gs.at[pl.ds(side_at + skip, 48)], r.gs.at[pl.ds(over + skip, 48)],
            send.at[at], recv.at[at], (seg, place.mate),
        )
        for skip, at in ((0, 38), (112, 39))
    ]
    over_here = pl.multiple_of(3 * GROUP * (1 - place.core), 16)
    corner_arrivals = [
        remote(
            r.gs.at[pl.ds(side_at + skip, 48)], r.gs.at[pl.ds(over_here + skip, 48)],
            send.at[at], recv.at[at], (seg, place.mate),
        )
        for skip, at in ((0, 38), (112, 39))
    ]

    def as_queries(group):
        r.ga[own(group), :] = dot(r.gs[own(group), :], r.out_t[...]).astype(BF16)
        query_side(r, group)

    def query_tokens():
        r.token[...] = dot(r.dqkv[:, 0:D], r.qkv_t[0:D, :])

    @pl.when(seg == last_seg)
    def _():
        moves_wait_recv(1, r.top, [slice(0, 64), slice(64, 128)])
        put_own(r.gs, slice(0, D), r.top[...])
        for halo in gs_halos:
            halo.start()
        for group in (0, 1):
            as_queries(group)
        query_tokens()

    for halo in ol_halos:
        halo.wait_sides()
        halo.wait_vertical()
    thirds = lax.broadcasted_iota(jnp.int32, (16, 128), 1)
    head_row = lax.broadcasted_iota(jnp.int32, (16, 128), 0)
    r.rows[...] = dot_nt(onehot((thirds < 48) & (thirds % 16 == head_row)), r.ol[:, D:OLW])
    key_probs(r)

    @pl.when(seg < last_seg)
    def _():
        for one_pass, halo, group in zip(passes, gs_halos, (first, second)):
            one_pass.wait_recv()
            halo.start()
            as_queries(group)
        query_tokens()

    def send_on(one_pass):
        pl.when(seg > 0)(one_pass.start)

    gs_halos[0].wait_sides()
    attn_grads(r, [1 + first])
    gs_halos[1].wait_sides()
    for copy in corners:
        copy.start()
    gs_halos[1].wait_vertical()
    attn_grads(r, [1 + second, 3 * first])
    join_deltas(r)
    key_side(r, first)
    finish(r, first)
    send_on(passes[0])

    gs_halos[0].wait_vertical()
    for copy in corner_arrivals:
        copy.wait_recv()
    attn_grads(r, [3 * second])
    join_deltas(r)
    key_side(r, second)
    finish(r, second)
    send_on(passes[1])

    @pl.when(seg > 0)
    def _():
        for one_pass in passes:
            one_pass.wait_send()

    row_at = pl.multiple_of(place.half * 64, 16)

    def back(group):
        return remote(
            r.outb.at[pl.ds(group * 64, 64)], r.got.at[pl.ds(row_at, 64)],
            send.at[36 + group], recv.at[36 + place.half], (seg, tiles[group]),
        )

    def back_local(group):
        return pltpu.make_async_copy(r.outb.at[pl.ds(group * 64, 64)], r.got.at[pl.ds(row_at, 64)], local.at[4 + group])

    porter = 4

    def hand(chunk):
        return remote(
            r.outb.at[pl.ds(64 + chunk * 32, 32)], r.lent.at[pl.ds(chunk * 32, 32)],
            send.at[51 + chunk], recv.at[51 + chunk], (porter, place.tile),
        )

    def carry(chunk):
        row = pl.multiple_of(row_at + chunk * 32, 16)
        return remote(
            r.lent.at[pl.ds(chunk * 32, 32)], r.got.at[pl.ds(row, 32)],
            send.at[53 + chunk], recv.at[40 + 2 * place.half + chunk], (0, tiles[1]),
        )

    @pl.when(seg == 0)
    def _():
        hand(0).start()
        hand(1).start()

    def straight(group):
        return True if group == 0 else seg > 0

    for group in (0, 1):

        @pl.when((tiles[group] != place.tile) & straight(group))
        def _():
            back(group).start()

        @pl.when((tiles[group] == place.tile) & straight(group))
        def _():
            back_local(group).start()
            back_local(group).wait()

    ring.wait_send()
    cross_send.wait_send()

    @pl.when(seg == last_seg)
    def _():
        lend(0).wait_send()
        lend(1).wait_send()

    for side_half in (0, 1):

        @pl.when((seg < last_seg) & (blocks[side_half] != place.tile))
        def _():
            move(side_half).wait_send()

    for halo in x_halos + ol_halos + gs_halos:
        halo.wait_send()
    for copy in corners:
        copy.wait_send()

    @pl.when(seg == porter)
    def _():
        for chunk in (0, 1):
            hand(chunk).wait_recv()
            carry(chunk).start()

    carried = (seg == 0) & (tile_group == 1)
    for side_half in (0, 1):

        @pl.when((blocks[side_half] != place.tile) & jnp.logical_not(carried))
        def _():
            remote(
                r.outb.at[0:64], r.got.at[pl.ds(side_half * 64, 64)], send.at[36 + side_half], recv.at[36 + side_half],
                (seg, place.left),
            ).wait_recv()

        @pl.when(carried)
        def _():
            for chunk in (0, 1):
                index = 40 + 2 * side_half + chunk
                remote(
                    r.outb.at[0:32], r.got.at[pl.ds(side_half * 64 + chunk * 32, 32)], send.at[index], recv.at[index],
                    (seg, place.left),
                ).wait_recv()

    r.out[...] = dot(half_order(new_col, new_row), r.got[...]).astype(BF16)

    for group in (0, 1):

        @pl.when((tiles[group] != place.tile) & straight(group))
        def _():
            back(group).wait_send()

    @pl.when(seg == 0)
    def _():
        hand(0).wait_send()
        hand(1).wait_send()

    @pl.when(seg == porter)
    def _():
        carry(0).wait_send()
        carry(1).wait_send()


def main(x, g, gain, table, qkv_in, out_in, tile_count):
    zs = tile_count // 4
    vmem = pl.BlockSpec(memory_space=pltpu.VMEM)
    bf16 = [
        (zs * 64, WIDE), (256, D), (SLOTS, D), (128, D), (D, WIDE), (D, D), (WIDE, D), (D, D), (SLOTS, D), (SLOTS, WIDE),
        (6, 256, WIN), (6, 256, WIN), (SLOTS, OLW), (SLOTS, D), (SLOTS, D), (128, WIDE), (128, D), (128, D),
        (256, D),
    ]
    f32 = [(128, D), (128, 128), (128, D), (16, SLOTS), (4, 16, 256), (2, HEADS, 8, WIN), (8, SLOTS)]
    return pl.pallas_call(
        functools.partial(main_kernel, tile_count),
        out_shape=jax.ShapeDtypeStruct((128, D), BF16),
        in_specs=[vmem] * 6,
        out_specs=vmem,
        scratch_shapes=[pltpu.VMEM(shape, BF16) for shape in bf16]
        + [pltpu.VMEM(shape, F32) for shape in f32]
        + [
            pltpu.SemaphoreType.DMA((55,)),
            pltpu.SemaphoreType.DMA((55,)),
            pltpu.SemaphoreType.DMA((6,)),
            pltpu.SemaphoreType.DMA((2, 2, zs // 2)),
            pltpu.SemaphoreType.DMA((2, 2, zs // 2)),
            pltpu.SemaphoreType.DMA((2, zs)),
            pltpu.SemaphoreType.DMA((2, zs)),
        ],
        compiler_params=pltpu.CompilerParams(
            collective_id=0, has_side_effects=True, vmem_limit_bytes=58 * 2**20
        ),
    )(x, g, gain, table, qkv_in, out_in)


def body(stored_inputs, output_grads, norm_gain, position_bias, qkv_weight, out_weight):
    tokens = TH * TW
    out = main(
        stored_inputs.reshape(tokens, D), output_grads.reshape(tokens, D), norm_gain,
        position_bias.reshape(HEADS, -1), qkv_weight[0], out_weight[0], lax.axis_size("tile"),
    )
    return out.reshape(1, 1, 1, TH, TW, D)


def solution(mesh):
    return jax.shard_map(
        body,
        mesh=mesh,
        in_specs=(
            P("segment", None, "tile", None, None, None),
            P(None, "tile", None, None, None),
            P("segment", None),
            P("segment", None, None, None),
            P("segment", "tile", None),
            P("segment", "tile", None),
        ),
        out_specs=P("segment", None, "tile", None, None, None),
        check_vma=False,
    )
```

```python
import functools
import types

import jax
import jax.numpy as jnp
from jax import lax
from jax.experimental import pallas as pl
from jax.experimental.pallas import tpu as pltpu
from jax.sharding import PartitionSpec as P

D = 768
HEADS = 12
RAD = 6
TH = 8
TW = 16
WIDE = 3 * D
OLW = D + 128
EPSILON = 1e-05
NEG_FILL = -1e30
MESH = pl.DeviceIdType.MESH
BF16 = jnp.bfloat16
F32 = jnp.float32

SLOTS = 640
GROUP = 160
T0, B0 = GROUP, 2 * GROUP
OWN_T, OWN_B = T0 + 48, B0 + 48


class Place:
    def __init__(self, tile_count):
        self.zs = tile_count // 4
        self.cols = self.zs // 2
        self.seg = lax.axis_index("segment")
        self.tile = lax.axis_index("tile")
        self.yh = self.tile // (2 * self.zs)
        self.z = (self.tile % (2 * self.zs)) // 2
        self.core = self.tile % 2
        self.rb = self.yh * 2 + self.core
        self.left = self.at(self.yh, (self.z + self.zs - 1) % self.zs, self.core)
        self.right = self.at(self.yh, (self.z + 1) % self.zs, self.core)
        self.mate = self.at(self.yh, self.z, 1 - self.core)
        self.cross = self.at(1 - self.yh, self.z, self.core)
        self.has_up = self.rb > 0
        self.has_down = self.rb < 3
        up = (self.rb + 3) % 4
        down = (self.rb + 1) % 4
        self.up = self.at(up // 2, self.z, up % 2)
        self.down = self.at(down // 2, self.z, down % 2)
        z_left, z_right = (self.z + self.zs - 1) % self.zs, (self.z + 1) % self.zs
        self.up_left = self.at(up // 2, z_left, up % 2)
        self.up_right = self.at(up // 2, z_right, up % 2)
        self.down_left = self.at(down // 2, z_left, down % 2)
        self.down_right = self.at(down // 2, z_right, down % 2)
        self.row = self.tile // self.cols
        self.col = self.tile % self.cols
        self.half = self.z % 2
        self.tile_t = (2 * self.rb) * self.cols + self.z // 2
        self.tile_b = (2 * self.rb + 1) * self.cols + self.z // 2

    def at(self, yh, z, core):
        return yh * (2 * self.zs) + z * 2 + core

    def block_of(self, half):
        rb = self.row // 2
        return self.at(rb // 2, 2 * self.col + half, rb % 2)


def remote(src, dst, send, recv, device):
    return pltpu.make_async_remote_copy(
        src_ref=src, dst_ref=dst, send_sem=send, recv_sem=recv, device_id=device, device_id_type=MESH
    )


def signal(sem, device):
    pl.semaphore_signal(sem, inc=1, device_id=device, device_id_type=MESH)


def one(flag):
    return jnp.where(flag, 1, 0).astype(jnp.int32)


def clear_outside(place, buf):
    blank = jnp.zeros((GROUP, buf.shape[1]), buf.dtype)

    @pl.when(jnp.logical_not(place.has_up))
    def _():
        buf[0:GROUP, :] = blank

    @pl.when(jnp.logical_not(place.has_down))
    def _():
        buf[3 * GROUP : SLOTS, :] = blank


def dot(left, right):
    return jnp.dot(left, right, preferred_element_type=F32)


def dot_nt(left, right):
    return lax.dot_general(left, right, (((1,), (1,)), ((), ())), preferred_element_type=F32)


def own_rows(ref, lanes):
    return jnp.concatenate([ref[OWN_T : OWN_T + 64, lanes], ref[OWN_B : OWN_B + 64, lanes]], axis=0)


def put_own(ref, lanes, value):
    ref[OWN_T : OWN_T + 64, lanes] = value[:64]
    ref[OWN_B : OWN_B + 64, lanes] = value[64:]


QUADS = 3
WIN = 512


def low_lanes(rows):
    return lax.broadcasted_iota(jnp.int32, (rows, 128), 1) < 64


def split_quad(value):
    low = low_lanes(64)
    zero = jnp.zeros((64, 128), value.dtype)
    rows = []
    for part in (0, 1):
        piece = value[:, part * 128 : (part + 1) * 128]
        for keep in (jnp.where(low, piece, zero), jnp.where(low, zero, piece)):
            rows.append(jnp.concatenate([keep, zero] if part == 0 else [zero, keep], axis=1))
    return jnp.concatenate(rows, axis=0)


def merge_quad(value):
    low = low_lanes(64)
    return jnp.concatenate(
        [
            jnp.where(low, value[0:64, :128], value[64:128, :128]),
            jnp.where(low, value[128:192, 128:], value[192:256, 128:]),
        ],
        axis=1,
    )


def head_sums(value):
    low = low_lanes(64)
    sums = []
    for part in (0, 1):
        piece = value[:, part * 128 : (part + 1) * 128]
        sums.append(jnp.sum(jnp.where(low, piece, 0.0), axis=-1, keepdims=True))
        sums.append(jnp.sum(jnp.where(low, 0.0, piece), axis=-1, keepdims=True))
    return jnp.concatenate(sums, axis=0)


def quad_lanes(quad, offset=0):
    return slice(offset + quad * 256, offset + (quad + 1) * 256)


def span(start, size, unit):
    return pl.ds(start if isinstance(start, int) else pl.multiple_of(start, unit), size)


def window(group):
    return span(group * (SLOTS - WIN), WIN, 128)


def own(group):
    return span(OWN_T + group * GROUP, 64, 16)


def half(group):
    return span(group * 64, 64, 16)


def quad_bias(base_ref, side, quad, group):
    shift = 0 if group == 0 else GROUP - (SLOTS - WIN)
    pieces = []
    for head in range(4 * quad, 4 * quad + 4):
        rows = base_ref[side, head]
        for col in range(8):
            turn = 8 * col + shift
            pieces.append(rows if turn == 0 else pltpu.roll(rows, turn, axis=1))
    return jnp.concatenate(pieces, axis=0)


def quad_rows(ref, quad, group):
    return jnp.concatenate(
        [jnp.broadcast_to(ref[head : head + 1, window(group)], (64, WIN)) for head in range(4 * quad, 4 * quad + 4)],
        axis=0,
    )


BLOCKS = [(quad, group) for quad in range(QUADS) for group in (0, 1)]


def query_probs(r, group):
    head_lane = lax.broadcasted_iota(jnp.int32, (64, 128), 1)
    levels = {group: jnp.zeros((64, 128), F32)}
    for quad in range(QUADS):
        query = split_quad(r.qkv[own(group), quad_lanes(quad)])
        scores = dot_nt(query, r.qkv[window(group), quad_lanes(quad, D)]) * 0.125
        scores = scores + quad_bias(r.base, 0, quad, group) + r.edge[0:1, window(group)]
        top = jnp.max(scores, axis=-1, keepdims=True)
        weight = jnp.exp(scores - top)
        total = jnp.sum(weight, axis=-1, keepdims=True)
        prob = (weight * (1.0 / total)).astype(BF16)
        r.prob_q[quad * 2 + group] = prob
        attn = merge_quad(dot(prob, r.qkv[window(group), quad_lanes(quad, 2 * D)]))
        r.ol[own(group), quad_lanes(quad)] = attn.astype(BF16)
        level = top + jnp.log(total)
        for head in range(4):
            levels[group] = jnp.where(
                head_lane == 4 * quad + head, level[head * 64 : (head + 1) * 64], levels[group]
            )
    level = levels[group]
    high = level.astype(BF16).astype(F32)
    middle = (level - high).astype(BF16).astype(F32)
    low = level - high - middle
    packed = high + pltpu.roll(middle, 16, axis=1) + pltpu.roll(low, 32, axis=1)
    r.ol[own(group), D:OLW] = packed.astype(BF16)


def key_probs(r):
    for quad, group in BLOCKS:
        key = split_quad(r.qkv[own(group), quad_lanes(quad, D)])
        scores = dot_nt(key, r.qkv[window(group), quad_lanes(quad)]) * 0.125
        scores = scores + quad_bias(r.base, 1, quad, group) + r.edge[0:1, window(group)]
        r.prob_k[quad * 2 + group] = jnp.exp(scores - quad_rows(r.rows, quad, group)).astype(BF16)


def query_side(r, group):
    for quad in range(QUADS):
        grad = r.ga[own(group), quad_lanes(quad)]
        delta = head_sums(grad.astype(F32) * r.ol[own(group), quad_lanes(quad)].astype(F32))
        prob_grad = dot_nt(split_quad(grad), r.qkv[window(group), quad_lanes(quad, 2 * D)])
        score_grad = r.prob_q[quad * 2 + group] * (prob_grad - delta).astype(BF16)
        query_grad = merge_quad(dot(score_grad, r.qkv[window(group), quad_lanes(quad, D)])) * 0.125
        r.dqkv[half(group), quad_lanes(quad)] = query_grad.astype(BF16)


def key_side(r, group):
    for quad in range(QUADS):
        value = split_quad(r.qkv[own(group), quad_lanes(quad, 2 * D)])
        prob_grad = dot_nt(value, r.ga[window(group), quad_lanes(quad)])
        prob = r.prob_k[quad * 2 + group]
        score_grad = prob * (prob_grad - quad_rows(r.rows, quad, group)).astype(BF16)
        key_grad = merge_quad(dot(score_grad, r.qkv[window(group), quad_lanes(quad)])) * 0.125
        value_grad = merge_quad(dot(prob, r.ga[window(group), quad_lanes(quad)]))
        r.dqkv[half(group), quad_lanes(quad, D)] = key_grad.astype(BF16)
        r.dqkv[half(group), quad_lanes(quad, 2 * D)] = value_grad.astype(BF16)


def attn_grads(r, regions):
    rows = [span(region * GROUP, GROUP, 16) for region in regions]
    grads = jnp.concatenate([r.gs[at, :] for at in rows], axis=0)
    grads = dot(grads, r.out_t[...]).astype(BF16)
    attn = jnp.concatenate([r.ol[at, 0:D] for at in rows], axis=0)
    wide = lax.broadcasted_iota(jnp.int32, (16, D), 1)
    head_wide = lax.broadcasted_iota(jnp.int32, (16, D), 0)
    deltas = dot_nt(onehot(wide // 64 == head_wide), grads * attn)
    for index, region in enumerate(regions):
        part = slice(index * GROUP, (index + 1) * GROUP)
        r.ga[rows[index], :] = grads[part]
        r.deltas[region, :, 0:GROUP] = deltas[:, part]


def join_deltas(r):
    r.rows[...] = jnp.concatenate([r.deltas[region, :, 0:GROUP] for region in range(4)], axis=1)


def finish(r, group):
    rows = half(group)
    token = r.token[rows, :] + dot(r.dqkv[rows, D:WIDE], r.qkv_t[D:WIDE, :])
    scaled = token * r.gain[...]
    part = r.normal[rows, :]
    first_mean = jnp.mean(scaled, axis=-1, keepdims=True)
    second_mean = jnp.mean(scaled * part, axis=-1, keepdims=True)
    branch = r.inverse[rows, 0:1] * (scaled - first_mean - part * second_mean)
    r.outb[rows, :] = (r.gs[own(group), :].astype(F32) + branch).astype(BF16)


def onehot(mask):
    return mask.astype(F32).astype(BF16)


def pack_shard(r, rows):
    at_row = lax.broadcasted_iota(jnp.int32, (16, 12), 0)
    at_col = lax.broadcasted_iota(jnp.int32, (16, 12), 1)
    whole = dot(onehot(at_row == at_col), r.qkv_in[...])
    for part in range(3):
        pick = onehot((at_row == 12 + at_col // 3) & (at_col % 3 == part))
        lanes = slice(part * D, (part + 1) * D)
        r.shards[rows, lanes] = (whole[:, lanes] + dot(pick, r.out_in[...])).astype(BF16)


def unpack_group(r, group, zs):
    rows = lax.broadcasted_iota(jnp.int32, (192, 256), 0)
    cols = lax.broadcasted_iota(jnp.int32, (192, 256), 1)
    shard = ((rows % 96) // 24) * 4 + ((rows % 24) // 12) * 2 + rows // 96
    feature = rows % 12
    source = pl.ds(pl.multiple_of(group * 256, 256), 256)
    low = pl.ds(pl.multiple_of(group * 96, 16), 96)
    high = pl.ds(pl.multiple_of(24 * zs + group * 96, 16), 96)
    block = dot(onehot(cols == shard * 16 + feature), r.shards[source, :]).astype(BF16)
    r.qkv_w[low, :] = block[:96]
    r.qkv_w[high, :] = block[96:]
    total = jnp.zeros((192, D), F32)
    for part in range(3):
        pick = onehot((cols == shard * 16 + 12 + feature // 3) & (feature % 3 == part))
        total = total + dot(pick, r.shards[source, part * D : (part + 1) * D])
    block = total.astype(BF16)
    r.out_w[low, :] = block[:96]
    r.out_w[high, :] = block[96:]


def half_order(rows, cols):
    return onehot(cols == (rows % 8) * TW + (rows // 64) * 8 + (rows % 64) // 8)


def fill_bias(r):
    span = 2 * RAD + 1
    table = r.table[...]
    high = table.astype(BF16)
    rest = table - high.astype(F32)
    middle = rest.astype(BF16)
    low = (rest - middle.astype(F32)).astype(BF16)
    index = lax.broadcasted_iota(jnp.int32, (span * span, WIN), 0)
    slot = lax.broadcasted_iota(jnp.int32, (1, WIN), 1)
    across = (slot % GROUP) // 8
    for row in range(8):
        up = 8 * (slot // GROUP - 1) + slot % 8 - row + RAD
        valid = (up >= 0) & (up < span) & (across < span) & (slot < 3 * GROUP)
        want = up * span + across
        for side in (0, 1):
            pick = onehot(index == (want if side == 0 else span * span - 1 - want))
            value = dot(high, pick) + dot(middle, pick) + dot(low, pick)
            value = jnp.where(valid, value, NEG_FILL)
            for head in range(HEADS):
                r.base[side, head, row : row + 1, :] = value[head : head + 1]


def fill_edge(r, place):
    slot = lax.broadcasted_iota(jnp.int32, (8, SLOTS), 1)
    group = slot // GROUP
    col = (slot % GROUP) // 8 - RAD
    first = jnp.where(place.z == 0, 0, -SLOTS)
    last = jnp.where(place.z == place.zs - 1, 7, SLOTS)
    top = jnp.where(place.has_up, 0, 1)
    bottom = jnp.where(place.has_down, 3, 2)
    outside = (col < first) | (col > last) | (group < top) | (group > bottom)
    r.edge[...] = jnp.where(outside, NEG_FILL, 0.0)


class Ring:
    def __init__(self, place, buf, send, recv, mate_send, mate_recv):
        self.place, self.buf = place, buf
        self.send, self.recv, self.mate_send, self.mate_recv = send, recv, mate_send, mate_recv
        self.half = place.zs // 2

    def rows(self, offset, core, which):
        z = (self.place.z + offset + self.place.zs) % self.place.zs
        yh = self.place.yh if which < 2 else 1 - self.place.yh
        return pl.ds(pl.multiple_of(((z * 2 + core) * 2 + yh) * 16, 16), 16)

    def copy(self, way, step, which, offset):
        lanes = slice(which % 2 * (WIDE // 2), (which % 2 + 1) * (WIDE // 2))
        part = self.buf.at[self.rows(offset, self.place.core, which), lanes]
        device = self.place.right if way == 0 else self.place.left
        return remote(
            part, part, self.send.at[way, which, step], self.recv.at[way, which, step], (self.place.seg, device)
        )

    def has(self, way, step, which):
        return step < self.half - 1 or (step == self.half - 1 and which // 2 == way)

    def leave(self, way, step, which):
        return self.copy(way, step, which, -step if way == 0 else step)

    def arrive(self, way, step, which):
        return self.copy(way, step, which, -step - 1 if way == 0 else step + 1)

    def share(self, offset, shard, core=None):
        core = self.place.core if core is None else core
        part = self.buf.at[self.rows(offset, core, 2 * shard)]
        index = (offset + self.place.zs) % self.place.zs
        return remote(
            part, part, self.mate_send.at[shard, index], self.mate_recv.at[shard, index],
            (self.place.seg, self.place.mate),
        )

    def begin(self, shard):
        for which in (2 * shard, 2 * shard + 1):
            self.leave(0, 0, which).start()
            self.leave(1, 0, which).start()
        self.share(0, shard).start()

    def turn(self, step, shard):
        for which in (2 * shard, 2 * shard + 1):
            for way in (0, 1):
                if self.has(way, step, which):
                    self.arrive(way, step, which).wait_recv()
                    if self.has(way, step + 1, which):
                        self.leave(way, step + 1, which).start()
                    if which % 2 == 1:
                        self.share(-step - 1 if way == 0 else step + 1, which // 2).start()

    def wait_shared(self, group):
        for member in range(4):
            offset = (group * 4 + member - self.place.z + self.place.zs) % self.place.zs
            for shard in (0, 1):
                self.share(offset, shard, 1 - self.place.core).wait_recv()

    def wait_send(self):
        for which in range(4):
            for way in (0, 1):
                for step in range(self.half):
                    if self.has(way, step, which):
                        self.leave(way, step, which).wait_send()
        for shard in (0, 1):
            for offset in range(self.place.zs):
                self.share(offset, shard).wait_send()


class Halo:
    def __init__(self, place, buf, send, recv, at, group, relay=False, more=0):
        base = pl.multiple_of(T0 + group * GROUP, 16)
        over = pl.multiple_of(3 * GROUP * (1 - group), 16)
        self.has = jnp.where(group == 0, one(place.has_up), one(place.has_down)) > 0
        self.gets = jnp.where(group == 0, one(place.has_down), one(place.has_up)) > 0

        def pick(up, down):
            return (place.seg, jnp.where(group == 0, up, down))

        def copy(role, src, rows, dst, device):
            index = at + 5 * group + role
            return remote(
                buf.at[pl.ds(src, rows)], buf.at[pl.ds(dst, rows)], send.at[index], recv.at[index], device
            )

        self.vertical = [copy(0, base + 48, 64, over + 48, pick(place.up, place.down))]
        self.corners = [
            copy(1, base + 48, 48, over + 112, pick(place.up_left, place.down_left)),
            copy(2, base + 64, 48, over, pick(place.up_right, place.down_right)),
        ]
        self.beyond = self.has & ((group == place.core) if relay else True)
        self.expects = self.gets & ((group != place.core) if relay else True)
        left, right = (place.seg, place.left), (place.seg, place.right)
        self.rest = []
        if more:
            self.sides = [copy(3, base + 48, 32, base + 112, left), copy(4, base + 64, 16, base, right)]
            self.rest = [
                remote(buf.at[pl.ds(base + src, rows)], buf.at[pl.ds(base + dst, rows)], send.at[index], recv.at[index], device)
                for src, rows, dst, index, device in ((80, 16, 144, more, left), (80, 32, 16, more + 1, right))
            ]
        else:
            self.sides = [copy(3, base + 48, 48, base + 112, left), copy(4, base + 64, 48, base, right)]

    def start_sides(self):
        for copy in self.sides:
            copy.start()

    def start_vertical(self):
        @pl.when(self.has)
        def _():
            for copy in self.vertical:
                copy.start()

        @pl.when(self.beyond)
        def _():
            for copy in self.corners:
                copy.start()

    def start(self, sides=True):
        if not self.rest:
            self.start_vertical()
        for copy in (self.sides if sides else []) + self.rest:
            copy.start()
        if self.rest:
            self.start_vertical()

    def wait_sides(self):
        for copy in self.sides + self.rest:
            copy.wait_recv()

    def wait_vertical(self):
        @pl.when(self.gets)
        def _():
            for copy in self.vertical:
                copy.wait_recv()

        @pl.when(self.expects)
        def _():
            for copy in self.corners:
                copy.wait_recv()

    def wait_send(self):
        @pl.when(self.has)
        def _():
            for copy in self.vertical:
                copy.wait_send()

        @pl.when(self.beyond)
        def _():
            for copy in self.corners:
                copy.wait_send()

        for copy in self.sides + self.rest:
            copy.wait_send()


def greet(place, barrier):
    seg = place.seg
    signal(barrier, (seg, place.left))
    signal(barrier, (seg, place.right))

    @pl.when(place.has_up)
    def _():
        for device in (place.up, place.up_left, place.up_right):
            signal(barrier, (seg, device))

    @pl.when(place.has_down)
    def _():
        for device in (place.down, place.down_left, place.down_right):
            signal(barrier, (seg, device))

    return 2 + 3 * one(place.has_up) + 3 * one(place.has_down)


def own_layer_norm(r):
    own_x = own_rows(r.slots, slice(0, D)).astype(F32)
    deviation = own_x - jnp.mean(own_x, axis=-1, keepdims=True)
    variance = jnp.mean(deviation * deviation, axis=-1, keepdims=True)
    own_inverse = lax.rsqrt(variance + EPSILON)
    r.normal[...] = deviation * own_inverse
    r.inverse[...] = jnp.broadcast_to(own_inverse, (128, 128))


def window_layer_norm(r):
    @pl.loop(0, 5)
    def _(chunk):
        rows = pl.ds(pl.multiple_of(chunk * 128, 128), 128)
        values = r.slots[rows, :].astype(F32)
        deviation = values - jnp.mean(values, axis=-1, keepdims=True)
        variance = jnp.mean(deviation * deviation, axis=-1, keepdims=True)
        part = deviation * lax.rsqrt(variance + EPSILON)
        r.normed[rows, :] = (part * r.gain[...]).astype(BF16)


REFS = [
    "x", "g", "gain", "table", "qkv_in", "out_in", "out",
    "shards", "xs", "slots", "top", "qkv_w", "out_w", "qkv_t", "out_t", "normed", "qkv", "prob_q", "prob_k", "ol",
    "gs", "ga", "dqkv", "outb", "got", "lent", "normal", "inverse", "token", "rows", "deltas", "base", "edge",
]


def main_kernel(tile_count, *refs):
    r = types.SimpleNamespace(**dict(zip(REFS, refs)))
    send, recv, local, ring_send, ring_recv, mate_send, mate_recv = refs[len(REFS) :]
    place = Place(tile_count)
    seg, zs = place.seg, place.zs
    last_seg = lax.axis_size("segment") - 1
    tiles = [place.tile_t, place.tile_b]
    blocks = [place.block_of(0), place.block_of(1)]
    barrier = pltpu.get_barrier_semaphore()
    helper = last_seg - 4
    count = greet(place, barrier) + 2 + one(seg > 0) + 3 * one(seg == helper) + 3 * one(seg == last_seg)
    signal(barrier, (seg, place.mate))
    signal(barrier, (seg, place.cross))

    @pl.when(seg < last_seg)
    def _():
        signal(barrier, (seg + 1, place.tile))

    @pl.when(seg == last_seg)
    def _():
        for device in tiles:
            signal(barrier, (helper, device))

        signal(barrier, (helper, place.tile))

    @pl.when(seg == helper)
    def _():
        signal(barrier, (last_seg, place.tile))
        for device in blocks:
            signal(barrier, (last_seg, device))

    @pl.when(seg == 4)
    def _():
        signal(barrier, (0, place.tile))

    @pl.when((seg == 0) & (place.row % 2 == 1))
    def _():
        for device in blocks:
            signal(barrier, (4, device))

    count = count + one(seg == 0) + one(seg == 4)
    for device in tiles + blocks:

        @pl.when(device != place.tile)
        def _():
            signal(barrier, (seg, device))

        count = count + one(device != place.tile)

    ring = Ring(place, r.shards, ring_send, ring_recv, mate_send, mate_recv)
    pack_shard(r, ring.rows(0, place.core, 0))
    new_row = lax.broadcasted_iota(jnp.int32, (128, 128), 0)
    new_col = lax.broadcasted_iota(jnp.int32, (128, 128), 1)
    to_halves = half_order(new_row, new_col)
    r.xs[0:128, :] = dot(to_halves, r.x[...]).astype(BF16)
    for buf in (r.slots, r.ol, r.gs):
        clear_outside(place, buf)
    r.ga[...] = jnp.zeros_like(r.ga)
    r.deltas[...] = jnp.zeros_like(r.deltas)
    pl.semaphore_wait(barrier, count)

    mine = r.shards.at[ring.rows(0, place.core, 0)]
    theirs = r.shards.at[ring.rows(0, place.core, 2)]
    tile_group = place.row % 2
    x_at = OWN_T + tile_group * GROUP
    g_at = tile_group * 64

    def lend(part):
        rows = pl.ds(part * 128, 128)
        return remote(r.xs.at[rows], r.lent.at[rows], send.at[45 + part], recv.at[45 + part], (helper, place.tile))

    def forward(part, side_half):
        dst, at = ((r.slots, x_at), (r.top, g_at))[part]
        index = 2 * part + side_half
        return remote(
            r.lent.at[pl.ds(index * 64, 64)], dst.at[pl.ds(pl.multiple_of(at, 16), 64)],
            send.at[47 + index], recv.at[2 * part + tile_group], (last_seg, blocks[side_half]),
        )

    @pl.when(seg == helper)
    def _():
        for part in (0, 1):
            lend(part).wait_recv()
            for side_half in (0, 1):
                forward(part, side_half).start()
        for part in (0, 1):
            for side_half in (0, 1):
                forward(part, side_half).wait_send()

    cross_send = remote(mine, mine, send.at[44], recv.at[44], (seg, place.cross))
    cross_send.start()
    ring.begin(0)

    def move(side_half):
        return remote(
            r.xs.at[pl.ds(side_half * 64, 64)], r.slots.at[pl.ds(pl.multiple_of(x_at, 16), 64)],
            send.at[side_half], recv.at[tile_group], (seg, blocks[side_half]),
        )

    def move_local(side_half):
        return pltpu.make_async_copy(
            r.xs.at[pl.ds(side_half * 64, 64)], r.slots.at[pl.ds(pl.multiple_of(x_at, 16), 64)], local.at[side_half]
        )

    for side_half in (0, 1):

        @pl.when((seg < last_seg) & (blocks[side_half] != place.tile))
        def _():
            move(side_half).start()

        @pl.when((seg < last_seg) & (blocks[side_half] == place.tile))
        def _():
            move_local(side_half).start()
            move_local(side_half).wait()

    def moves_wait_recv(part, dst, rows):
        for group in (0, 1):

            @pl.when((seg == last_seg) | (tiles[group] != place.tile))
            def _():
                index = 2 * part + group
                remote(
                    r.xs.at[0:64], dst.at[rows[group]], send.at[index], recv.at[index], (seg, place.left)
                ).wait_recv()

    ring.turn(0, 0)
    fill_edge(r, place)
    fill_bias(r)
    remote(mine, theirs, send.at[44], recv.at[44], (seg, place.cross)).wait_recv()
    ring.begin(1)

    @pl.when(seg == last_seg)
    def _():
        lend(0).start()
        r.xs[128:256, :] = dot(to_halves, r.g[...]).astype(BF16)

    x_halos = [Halo(place, r.slots, send, recv, 4, group) for group in (0, 1)]
    near = jnp.where(place.z % 4 < 2, -1, 1)
    home = place.z // 4
    groups = zs // 4
    for step in range(ring.half):
        ring.turn(step, 1)
        if step + 1 < ring.half:
            ring.turn(step + 1, 0)
        if step == 2:

            @pl.when(seg == last_seg)
            def _():
                lend(1).start()

        if step == ring.half - 4:
            moves_wait_recv(0, r.slots, [own(0), own(1)])
            for halo in x_halos:
                halo.start()
            own_layer_norm(r)
            ring.wait_shared(home)
            unpack_group(r, home, zs)
        if step == ring.half - 3:
            ring.wait_shared((home + near + groups) % groups)
            unpack_group(r, (home + near + groups) % groups, zs)
        if step == ring.half - 2:
            for halo in x_halos:
                halo.wait_sides()
                halo.wait_vertical()
            window_layer_norm(r)
            ring.wait_shared((home - near + groups) % groups)
            unpack_group(r, (home - near + groups) % groups, zs)

    ring.wait_shared((home + 2) % groups)
    unpack_group(r, (home + 2) % groups, zs)
    r.qkv[...] = dot(r.normed[...], r.qkv_w[...]).astype(BF16)
    ol_halos = [Halo(place, r.ol, send, recv, 14, group) for group in (0, 1)]
    for group in (0, 1):
        query_probs(r, group)
        ol_halos[group].start()
    r.qkv_t[...] = r.qkv_w[...].T
    r.out_t[...] = r.out_w[...].T

    first, second = place.core, 1 - place.core

    def passing(group, skip, size, index):
        row = pl.multiple_of(group * 64 + skip, 16)
        slot = pl.multiple_of(OWN_T + group * GROUP + skip, 16)
        return remote(
            r.outb.at[pl.ds(row, size)], r.gs.at[pl.ds(slot, size)], send.at[index], recv.at[index],
            (jnp.maximum(seg - 1, 0), place.tile),
        )

    passes = [passing(first, 0, 64, 34), passing(second, 0, 32, 35), passing(second, 32, 32, 55)]
    gs_halos = [
        Halo(place, r.gs, send, recv, 24, first, True),
        Halo(place, r.gs, send, recv, 24, second, True, 56),
    ]

    relay_group = 1 - place.core
    side_at = pl.multiple_of(T0 + GROUP * relay_group, 16)
    over = pl.multiple_of(3 * GROUP * place.core, 16)
    corners = [
        remote(
            r.gs.at[pl.ds(side_at + skip, 48)], r.gs.at[pl.ds(over + skip, 48)],
            send.at[at], recv.at[at], (seg, place.mate),
        )
        for skip, at in ((0, 38), (112, 39))
    ]
    over_here = pl.multiple_of(3 * GROUP * (1 - place.core), 16)
    corner_arrivals = [
        remote(
            r.gs.at[pl.ds(side_at + skip, 48)], r.gs.at[pl.ds(over_here + skip, 48)],
            send.at[at], recv.at[at], (seg, place.mate),
        )
        for skip, at in ((0, 38), (112, 39))
    ]

    def as_queries(group):
        r.ga[own(group), :] = dot(r.gs[own(group), :], r.out_t[...]).astype(BF16)
        query_side(r, group)

    def query_tokens():
        r.token[...] = dot(r.dqkv[:, 0:D], r.qkv_t[0:D, :])

    @pl.when(seg == last_seg)
    def _():
        moves_wait_recv(1, r.top, [slice(0, 64), slice(64, 128)])
        put_own(r.gs, slice(0, D), r.top[...])
        for halo in gs_halos:
            halo.start()
        for group in (0, 1):
            as_queries(group)
        query_tokens()

    for halo in ol_halos:
        halo.wait_sides()
        halo.wait_vertical()
    thirds = lax.broadcasted_iota(jnp.int32, (16, 128), 1)
    head_row = lax.broadcasted_iota(jnp.int32, (16, 128), 0)
    r.rows[...] = dot_nt(onehot((thirds < 48) & (thirds % 16 == head_row)), r.ol[:, D:OLW])
    key_probs(r)

    @pl.when(seg < last_seg)
    def _():
        passes[0].wait_recv()
        gs_halos[0].start()
        as_queries(first)
        passes[1].wait_recv()
        gs_halos[1].start_sides()
        passes[2].wait_recv()
        gs_halos[1].start(sides=False)
        as_queries(second)
        query_tokens()

    row_at = pl.multiple_of(place.half * 64, 16)

    def back(group):
        return remote(
            r.outb.at[pl.ds(group * 64, 64)], r.got.at[pl.ds(row_at, 64)],
            send.at[36 + group], recv.at[36 + place.half], (seg, tiles[group]),
        )

    def back_local(group):
        return pltpu.make_async_copy(r.outb.at[pl.ds(group * 64, 64)], r.got.at[pl.ds(row_at, 64)], local.at[4 + group])

    porter = 4

    def hand(chunk):
        return remote(
            r.outb.at[pl.ds(64 + chunk * 32, 32)], r.lent.at[pl.ds(chunk * 32, 32)],
            send.at[51 + chunk], recv.at[51 + chunk], (porter, place.tile),
        )

    def carry(chunk):
        row = pl.multiple_of(row_at + chunk * 32, 16)
        return remote(
            r.lent.at[pl.ds(chunk * 32, 32)], r.got.at[pl.ds(row, 32)],
            send.at[53 + chunk], recv.at[40 + 2 * place.half + chunk], (0, tiles[1]),
        )

    def straight(group):
        return True if group == 0 else seg > 0

    def go_back(group, when):
        @pl.when((tiles[group] != place.tile) & when)
        def _():
            back(group).start()

        @pl.when((tiles[group] == place.tile) & when)
        def _():
            back_local(group).start()
            back_local(group).wait()

    def go_home(upper):
        go_back(0, (seg == 0) & upper)

        @pl.when((seg == 0) & jnp.logical_not(upper))
        def _():
            hand(0).start()
            hand(1).start()

    def send_on(copies):
        @pl.when(seg > 0)
        def _():
            for copy in copies:
                copy.start()

    gs_halos[0].wait_sides()
    gs_halos[1].wait_vertical()
    attn_grads(r, [1 + first, 3 * first])
    gs_halos[1].wait_sides()
    for copy in corners:
        copy.start()
    attn_grads(r, [1 + second])
    join_deltas(r)
    key_side(r, first)
    finish(r, first)
    send_on(passes[:1])
    go_home(first == 0)

    gs_halos[0].wait_vertical()
    for copy in corner_arrivals:
        copy.wait_recv()
    attn_grads(r, [3 * second])
    join_deltas(r)
    key_side(r, second)
    finish(r, second)
    send_on(passes[1:])
    go_home(second == 0)

    @pl.when(seg > 0)
    def _():
        for one_pass in passes:
            one_pass.wait_send()

    for group in (0, 1):
        go_back(group, seg > 0)

    ring.wait_send()
    cross_send.wait_send()

    @pl.when(seg == last_seg)
    def _():
        lend(0).wait_send()
        lend(1).wait_send()

    for side_half in (0, 1):

        @pl.when((seg < last_seg) & (blocks[side_half] != place.tile))
        def _():
            move(side_half).wait_send()

    for halo in x_halos + ol_halos + gs_halos:
        halo.wait_send()
    for copy in corners:
        copy.wait_send()

    @pl.when(seg == porter)
    def _():
        for chunk in (0, 1):
            hand(chunk).wait_recv()
            carry(chunk).start()

    carried = (seg == 0) & (tile_group == 1)
    for side_half in (0, 1):

        @pl.when((blocks[side_half] != place.tile) & jnp.logical_not(carried))
        def _():
            remote(
                r.outb.at[0:64], r.got.at[pl.ds(side_half * 64, 64)], send.at[36 + side_half], recv.at[36 + side_half],
                (seg, place.left),
            ).wait_recv()

        @pl.when(carried)
        def _():
            for chunk in (0, 1):
                index = 40 + 2 * side_half + chunk
                remote(
                    r.outb.at[0:32], r.got.at[pl.ds(side_half * 64 + chunk * 32, 32)], send.at[index], recv.at[index],
                    (seg, place.left),
                ).wait_recv()

    r.out[...] = dot(half_order(new_col, new_row), r.got[...]).astype(BF16)

    for group in (0, 1):

        @pl.when((tiles[group] != place.tile) & straight(group))
        def _():
            back(group).wait_send()

    @pl.when(seg == 0)
    def _():
        hand(0).wait_send()
        hand(1).wait_send()

    @pl.when(seg == porter)
    def _():
        carry(0).wait_send()
        carry(1).wait_send()


def main(x, g, gain, table, qkv_in, out_in, tile_count):
    zs = tile_count // 4
    vmem = pl.BlockSpec(memory_space=pltpu.VMEM)
    bf16 = [
        (zs * 64, WIDE), (256, D), (SLOTS, D), (128, D), (D, WIDE), (D, D), (WIDE, D), (D, D), (SLOTS, D), (SLOTS, WIDE),
        (6, 256, WIN), (6, 256, WIN), (SLOTS, OLW), (SLOTS, D), (SLOTS, D), (128, WIDE), (128, D), (128, D),
        (256, D),
    ]
    f32 = [(128, D), (128, 128), (128, D), (16, SLOTS), (4, 16, 256), (2, HEADS, 8, WIN), (8, SLOTS)]
    return pl.pallas_call(
        functools.partial(main_kernel, tile_count),
        out_shape=jax.ShapeDtypeStruct((128, D), BF16),
        in_specs=[vmem] * 6,
        out_specs=vmem,
        scratch_shapes=[pltpu.VMEM(shape, BF16) for shape in bf16]
        + [pltpu.VMEM(shape, F32) for shape in f32]
        + [
            pltpu.SemaphoreType.DMA((58,)),
            pltpu.SemaphoreType.DMA((58,)),
            pltpu.SemaphoreType.DMA((6,)),
            pltpu.SemaphoreType.DMA((2, 4, zs // 2)),
            pltpu.SemaphoreType.DMA((2, 4, zs // 2)),
            pltpu.SemaphoreType.DMA((2, zs)),
            pltpu.SemaphoreType.DMA((2, zs)),
        ],
        compiler_params=pltpu.CompilerParams(
            collective_id=0, has_side_effects=True, vmem_limit_bytes=58 * 2**20
        ),
    )(x, g, gain, table, qkv_in, out_in)


def body(stored_inputs, output_grads, norm_gain, position_bias, qkv_weight, out_weight):
    tokens = TH * TW
    out = main(
        stored_inputs.reshape(tokens, D), output_grads.reshape(tokens, D), norm_gain,
        position_bias.reshape(HEADS, -1), qkv_weight[0], out_weight[0], lax.axis_size("tile"),
    )
    return out.reshape(1, 1, 1, TH, TW, D)


def solution(mesh):
    return jax.shard_map(
        body,
        mesh=mesh,
        in_specs=(
            P("segment", None, "tile", None, None, None),
            P(None, "tile", None, None, None),
            P("segment", None),
            P("segment", None, None, None),
            P("segment", "tile", None),
            P("segment", "tile", None),
        ),
        out_specs=P("segment", None, "tile", None, None, None),
        check_vma=False,
    )
```

```python
import functools
import types

import jax
import jax.numpy as jnp
from jax import lax
from jax.experimental import pallas as pl
from jax.experimental.pallas import tpu as pltpu
from jax.sharding import PartitionSpec as P

D = 768
HEADS = 12
RAD = 6
TH = 8
TW = 16
WIDE = 3 * D
OLW = D + 128
EPSILON = 1e-05
NEG_FILL = -1e30
MESH = pl.DeviceIdType.MESH
BF16 = jnp.bfloat16
F32 = jnp.float32

SLOTS = 640
GROUP = 160
T0, B0 = GROUP, 2 * GROUP
OWN_T, OWN_B = T0 + 48, B0 + 48


class Place:
    def __init__(self, tile_count):
        self.zs = tile_count // 4
        self.cols = self.zs // 2
        self.seg = lax.axis_index("segment")
        self.tile = lax.axis_index("tile")
        self.yh = self.tile // (2 * self.zs)
        self.z = (self.tile % (2 * self.zs)) // 2
        self.core = self.tile % 2
        self.rb = self.yh * 2 + self.core
        self.left = self.at(self.yh, (self.z + self.zs - 1) % self.zs, self.core)
        self.right = self.at(self.yh, (self.z + 1) % self.zs, self.core)
        self.mate = self.at(self.yh, self.z, 1 - self.core)
        self.cross = self.at(1 - self.yh, self.z, self.core)
        self.has_up = self.rb > 0
        self.has_down = self.rb < 3
        up = (self.rb + 3) % 4
        down = (self.rb + 1) % 4
        self.up = self.at(up // 2, self.z, up % 2)
        self.down = self.at(down // 2, self.z, down % 2)
        z_left, z_right = (self.z + self.zs - 1) % self.zs, (self.z + 1) % self.zs
        self.up_left = self.at(up // 2, z_left, up % 2)
        self.up_right = self.at(up // 2, z_right, up % 2)
        self.down_left = self.at(down // 2, z_left, down % 2)
        self.down_right = self.at(down // 2, z_right, down % 2)
        self.row = self.tile // self.cols
        self.col = self.tile % self.cols
        self.half = self.z % 2
        self.tile_t = (2 * self.rb) * self.cols + self.z // 2
        self.tile_b = (2 * self.rb + 1) * self.cols + self.z // 2

    def at(self, yh, z, core):
        return yh * (2 * self.zs) + z * 2 + core

    def block_of(self, half):
        rb = self.row // 2
        return self.at(rb // 2, 2 * self.col + half, rb % 2)


def remote(src, dst, send, recv, device):
    return pltpu.make_async_remote_copy(
        src_ref=src, dst_ref=dst, send_sem=send, recv_sem=recv, device_id=device, device_id_type=MESH
    )


def signal(sem, device):
    pl.semaphore_signal(sem, inc=1, device_id=device, device_id_type=MESH)


def one(flag):
    return jnp.where(flag, 1, 0).astype(jnp.int32)


def clear_outside(place, buf):
    blank = jnp.zeros((GROUP, buf.shape[1]), buf.dtype)

    @pl.when(jnp.logical_not(place.has_up))
    def _():
        buf[0:GROUP, :] = blank

    @pl.when(jnp.logical_not(place.has_down))
    def _():
        buf[3 * GROUP : SLOTS, :] = blank


def dot(left, right):
    return jnp.dot(left, right, preferred_element_type=F32)


def dot_nt(left, right):
    return lax.dot_general(left, right, (((1,), (1,)), ((), ())), preferred_element_type=F32)


def own_rows(ref, lanes):
    return jnp.concatenate([ref[OWN_T : OWN_T + 64, lanes], ref[OWN_B : OWN_B + 64, lanes]], axis=0)


def put_own(ref, lanes, value):
    ref[OWN_T : OWN_T + 64, lanes] = value[:64]
    ref[OWN_B : OWN_B + 64, lanes] = value[64:]


QUADS = 3
WIN = 512


def low_lanes(rows):
    return lax.broadcasted_iota(jnp.int32, (rows, 128), 1) < 64


def split_quad(value):
    low = low_lanes(64)
    zero = jnp.zeros((64, 128), value.dtype)
    rows = []
    for part in (0, 1):
        piece = value[:, part * 128 : (part + 1) * 128]
        for keep in (jnp.where(low, piece, zero), jnp.where(low, zero, piece)):
            rows.append(jnp.concatenate([keep, zero] if part == 0 else [zero, keep], axis=1))
    return jnp.concatenate(rows, axis=0)


def merge_quad(value):
    low = low_lanes(64)
    return jnp.concatenate(
        [
            jnp.where(low, value[0:64, :128], value[64:128, :128]),
            jnp.where(low, value[128:192, 128:], value[192:256, 128:]),
        ],
        axis=1,
    )


def head_sums(value):
    low = low_lanes(64)
    sums = []
    for part in (0, 1):
        piece = value[:, part * 128 : (part + 1) * 128]
        sums.append(jnp.sum(jnp.where(low, piece, 0.0), axis=-1, keepdims=True))
        sums.append(jnp.sum(jnp.where(low, 0.0, piece), axis=-1, keepdims=True))
    return jnp.concatenate(sums, axis=0)


def quad_lanes(quad, offset=0):
    return slice(offset + quad * 256, offset + (quad + 1) * 256)


def span(start, size, unit):
    return pl.ds(start if isinstance(start, int) else pl.multiple_of(start, unit), size)


def window(group):
    return span(group * (SLOTS - WIN), WIN, 128)


def own(group):
    return span(OWN_T + group * GROUP, 64, 16)


def half(group):
    return span(group * 64, 64, 16)


def quad_bias(base_ref, side, quad, group):
    shift = 0 if group == 0 else GROUP - (SLOTS - WIN)
    pieces = []
    for head in range(4 * quad, 4 * quad + 4):
        rows = base_ref[side, head]
        for col in range(8):
            turn = 8 * col + shift
            pieces.append(rows if turn == 0 else pltpu.roll(rows, turn, axis=1))
    return jnp.concatenate(pieces, axis=0)


def quad_rows(ref, quad, group):
    return jnp.concatenate(
        [jnp.broadcast_to(ref[head : head + 1, window(group)], (64, WIN)) for head in range(4 * quad, 4 * quad + 4)],
        axis=0,
    )


BLOCKS = [(quad, group) for quad in range(QUADS) for group in (0, 1)]


def query_probs(r, group):
    head_lane = lax.broadcasted_iota(jnp.int32, (64, 128), 1)
    levels = {group: jnp.zeros((64, 128), F32)}
    for quad in range(QUADS):
        query = split_quad(r.qkv[own(group), quad_lanes(quad)])
        scores = dot_nt(query, r.qkv[window(group), quad_lanes(quad, D)]) * 0.125
        scores = scores + quad_bias(r.base, 0, quad, group) + r.edge[0:1, window(group)]
        top = jnp.max(scores, axis=-1, keepdims=True)
        weight = jnp.exp(scores - top)
        total = jnp.sum(weight, axis=-1, keepdims=True)
        prob = (weight * (1.0 / total)).astype(BF16)
        r.prob_q[quad * 2 + group] = prob
        attn = merge_quad(dot(prob, r.qkv[window(group), quad_lanes(quad, 2 * D)]))
        r.ol[own(group), quad_lanes(quad)] = attn.astype(BF16)
        level = top + jnp.log(total)
        for head in range(4):
            levels[group] = jnp.where(
                head_lane == 4 * quad + head, level[head * 64 : (head + 1) * 64], levels[group]
            )
    level = levels[group]
    high = level.astype(BF16).astype(F32)
    middle = (level - high).astype(BF16).astype(F32)
    low = level - high - middle
    packed = high + pltpu.roll(middle, 16, axis=1) + pltpu.roll(low, 32, axis=1)
    r.ol[own(group), D:OLW] = packed.astype(BF16)


def key_probs(r):
    for quad, group in BLOCKS:
        key = split_quad(r.qkv[own(group), quad_lanes(quad, D)])
        scores = dot_nt(key, r.qkv[window(group), quad_lanes(quad)]) * 0.125
        scores = scores + quad_bias(r.base, 1, quad, group) + r.edge[0:1, window(group)]
        r.prob_k[quad * 2 + group] = jnp.exp(scores - quad_rows(r.rows, quad, group)).astype(BF16)


def query_side(r, group):
    for quad in range(QUADS):
        grad = r.ga[own(group), quad_lanes(quad)]
        delta = head_sums(grad.astype(F32) * r.ol[own(group), quad_lanes(quad)].astype(F32))
        prob_grad = dot_nt(split_quad(grad), r.qkv[window(group), quad_lanes(quad, 2 * D)])
        score_grad = r.prob_q[quad * 2 + group] * (prob_grad - delta).astype(BF16)
        query_grad = merge_quad(dot(score_grad, r.qkv[window(group), quad_lanes(quad, D)])) * 0.125
        r.dqkv[half(group), quad_lanes(quad)] = query_grad.astype(BF16)


def key_side(r, group):
    for quad in range(QUADS):
        value = split_quad(r.qkv[own(group), quad_lanes(quad, 2 * D)])
        prob_grad = dot_nt(value, r.ga[window(group), quad_lanes(quad)])
        prob = r.prob_k[quad * 2 + group]
        score_grad = prob * (prob_grad - quad_rows(r.rows, quad, group)).astype(BF16)
        key_grad = merge_quad(dot(score_grad, r.qkv[window(group), quad_lanes(quad)])) * 0.125
        value_grad = merge_quad(dot(prob, r.ga[window(group), quad_lanes(quad)]))
        r.dqkv[half(group), quad_lanes(quad, D)] = key_grad.astype(BF16)
        r.dqkv[half(group), quad_lanes(quad, 2 * D)] = value_grad.astype(BF16)


def attn_grads(r, regions):
    rows = [span(region * GROUP, GROUP, 16) for region in regions]
    grads = jnp.concatenate([r.gs[at, :] for at in rows], axis=0)
    grads = dot(grads, r.out_t[...]).astype(BF16)
    attn = jnp.concatenate([r.ol[at, 0:D] for at in rows], axis=0)
    wide = lax.broadcasted_iota(jnp.int32, (16, D), 1)
    head_wide = lax.broadcasted_iota(jnp.int32, (16, D), 0)
    deltas = dot_nt(onehot(wide // 64 == head_wide), grads * attn)
    for index, region in enumerate(regions):
        part = slice(index * GROUP, (index + 1) * GROUP)
        r.ga[rows[index], :] = grads[part]
        r.deltas[region, :, 0:GROUP] = deltas[:, part]


def join_deltas(r):
    r.rows[...] = jnp.concatenate([r.deltas[region, :, 0:GROUP] for region in range(4)], axis=1)


def finish(r, group):
    rows = half(group)
    token = r.token[rows, :] + dot(r.dqkv[rows, D:WIDE], r.qkv_t[D:WIDE, :])
    scaled = token * r.gain[...]
    part = r.normal[rows, :]
    first_mean = jnp.mean(scaled, axis=-1, keepdims=True)
    second_mean = jnp.mean(scaled * part, axis=-1, keepdims=True)
    branch = r.inverse[rows, 0:1] * (scaled - first_mean - part * second_mean)
    r.outb[rows, :] = (r.gs[own(group), :].astype(F32) + branch).astype(BF16)


def onehot(mask):
    return mask.astype(F32).astype(BF16)


def pack_shard(r, rows):
    at_row = lax.broadcasted_iota(jnp.int32, (16, 12), 0)
    at_col = lax.broadcasted_iota(jnp.int32, (16, 12), 1)
    whole = dot(onehot(at_row == at_col), r.qkv_in[...])
    for part in range(3):
        pick = onehot((at_row == 12 + at_col // 3) & (at_col % 3 == part))
        lanes = slice(part * D, (part + 1) * D)
        r.shards[rows, lanes] = (whole[:, lanes] + dot(pick, r.out_in[...])).astype(BF16)


def unpack_group(r, group, zs):
    rows = lax.broadcasted_iota(jnp.int32, (192, 256), 0)
    cols = lax.broadcasted_iota(jnp.int32, (192, 256), 1)
    shard = ((rows % 96) // 24) * 4 + ((rows % 24) // 12) * 2 + rows // 96
    feature = rows % 12
    source = pl.ds(pl.multiple_of(group * 256, 256), 256)
    low = pl.ds(pl.multiple_of(group * 96, 16), 96)
    high = pl.ds(pl.multiple_of(24 * zs + group * 96, 16), 96)
    block = dot(onehot(cols == shard * 16 + feature), r.shards[source, :]).astype(BF16)
    r.qkv_w[low, :] = block[:96]
    r.qkv_w[high, :] = block[96:]
    total = jnp.zeros((192, D), F32)
    for part in range(3):
        pick = onehot((cols == shard * 16 + 12 + feature // 3) & (feature % 3 == part))
        total = total + dot(pick, r.shards[source, part * D : (part + 1) * D])
    block = total.astype(BF16)
    r.out_w[low, :] = block[:96]
    r.out_w[high, :] = block[96:]


def half_order(rows, cols):
    return onehot(cols == (rows % 8) * TW + (rows // 64) * 8 + (rows % 64) // 8)


def fill_bias(r):
    span = 2 * RAD + 1
    table = r.table[...]
    high = table.astype(BF16)
    rest = table - high.astype(F32)
    middle = rest.astype(BF16)
    low = (rest - middle.astype(F32)).astype(BF16)
    index = lax.broadcasted_iota(jnp.int32, (span * span, WIN), 0)
    slot = lax.broadcasted_iota(jnp.int32, (1, WIN), 1)
    across = (slot % GROUP) // 8
    for row in range(8):
        up = 8 * (slot // GROUP - 1) + slot % 8 - row + RAD
        valid = (up >= 0) & (up < span) & (across < span) & (slot < 3 * GROUP)
        want = up * span + across
        for side in (0, 1):
            pick = onehot(index == (want if side == 0 else span * span - 1 - want))
            value = dot(high, pick) + dot(middle, pick) + dot(low, pick)
            value = jnp.where(valid, value, NEG_FILL)
            for head in range(HEADS):
                r.base[side, head, row : row + 1, :] = value[head : head + 1]


def fill_edge(r, place):
    slot = lax.broadcasted_iota(jnp.int32, (8, SLOTS), 1)
    group = slot // GROUP
    col = (slot % GROUP) // 8 - RAD
    first = jnp.where(place.z == 0, 0, -SLOTS)
    last = jnp.where(place.z == place.zs - 1, 7, SLOTS)
    top = jnp.where(place.has_up, 0, 1)
    bottom = jnp.where(place.has_down, 3, 2)
    outside = (col < first) | (col > last) | (group < top) | (group > bottom)
    r.edge[...] = jnp.where(outside, NEG_FILL, 0.0)


class Ring:
    def __init__(self, place, buf, send, recv, mate_send, mate_recv):
        self.place, self.buf = place, buf
        self.send, self.recv, self.mate_send, self.mate_recv = send, recv, mate_send, mate_recv
        self.half = place.zs // 2

    def rows(self, offset, core, which):
        z = (self.place.z + offset + self.place.zs) % self.place.zs
        yh = self.place.yh if which < 2 else 1 - self.place.yh
        return pl.ds(pl.multiple_of(((z * 2 + core) * 2 + yh) * 16, 16), 16)

    def copy(self, way, step, which, offset):
        lanes = slice(which % 2 * (WIDE // 2), (which % 2 + 1) * (WIDE // 2))
        part = self.buf.at[self.rows(offset, self.place.core, which), lanes]
        device = self.place.right if way == 0 else self.place.left
        return remote(
            part, part, self.send.at[way, which, step], self.recv.at[way, which, step], (self.place.seg, device)
        )

    def has(self, way, step, which):
        return step < self.half - 1 or (step == self.half - 1 and which // 2 == way)

    def leave(self, way, step, which):
        return self.copy(way, step, which, -step if way == 0 else step)

    def arrive(self, way, step, which):
        return self.copy(way, step, which, -step - 1 if way == 0 else step + 1)

    def share(self, offset, shard, core=None):
        core = self.place.core if core is None else core
        part = self.buf.at[self.rows(offset, core, 2 * shard)]
        index = (offset + self.place.zs) % self.place.zs
        return remote(
            part, part, self.mate_send.at[shard, index], self.mate_recv.at[shard, index],
            (self.place.seg, self.place.mate),
        )

    def begin(self, shard):
        for which in (2 * shard, 2 * shard + 1):
            self.leave(0, 0, which).start()
            self.leave(1, 0, which).start()
        self.share(0, shard).start()

    def turn(self, step, shard):
        for which in (2 * shard, 2 * shard + 1):
            for way in (0, 1):
                if self.has(way, step, which):
                    self.arrive(way, step, which).wait_recv()
                    if self.has(way, step + 1, which):
                        self.leave(way, step + 1, which).start()
                    if which % 2 == 1:
                        self.share(-step - 1 if way == 0 else step + 1, which // 2).start()

    def wait_shared(self, group):
        for member in range(4):
            offset = (group * 4 + member - self.place.z + self.place.zs) % self.place.zs
            for shard in (0, 1):
                self.share(offset, shard, 1 - self.place.core).wait_recv()

    def wait_send(self):
        for which in range(4):
            for way in (0, 1):
                for step in range(self.half):
                    if self.has(way, step, which):
                        self.leave(way, step, which).wait_send()
        for shard in (0, 1):
            for offset in range(self.place.zs):
                self.share(offset, shard).wait_send()


class Halo:
    def __init__(self, place, buf, send, recv, at, group, relay=False, more=0):
        base = pl.multiple_of(T0 + group * GROUP, 16)
        over = pl.multiple_of(3 * GROUP * (1 - group), 16)
        self.has = jnp.where(group == 0, one(place.has_up), one(place.has_down)) > 0
        self.gets = jnp.where(group == 0, one(place.has_down), one(place.has_up)) > 0

        def pick(up, down):
            return (place.seg, jnp.where(group == 0, up, down))

        def copy(role, src, rows, dst, device):
            index = at + 5 * group + role
            return remote(
                buf.at[pl.ds(src, rows)], buf.at[pl.ds(dst, rows)], send.at[index], recv.at[index], device
            )

        self.vertical = [copy(0, base + 48, 64, over + 48, pick(place.up, place.down))]
        self.corners = [
            copy(1, base + 48, 48, over + 112, pick(place.up_left, place.down_left)),
            copy(2, base + 64, 48, over, pick(place.up_right, place.down_right)),
        ]
        self.beyond = self.has & ((group == place.core) if relay else True)
        self.expects = self.gets & ((group != place.core) if relay else True)
        left, right = (place.seg, place.left), (place.seg, place.right)
        self.rest = []
        if more:
            self.sides = [copy(3, base + 48, 32, base + 112, left), copy(4, base + 64, 16, base, right)]
            self.rest = [
                remote(buf.at[pl.ds(base + src, rows)], buf.at[pl.ds(base + dst, rows)], send.at[index], recv.at[index], device)
                for src, rows, dst, index, device in ((80, 16, 144, more, left), (80, 32, 16, more + 1, right))
            ]
        else:
            self.sides = [copy(3, base + 48, 48, base + 112, left), copy(4, base + 64, 48, base, right)]

    def start_sides(self):
        for copy in self.sides:
            copy.start()

    def start_vertical(self):
        @pl.when(self.has)
        def _():
            for copy in self.vertical:
                copy.start()

        @pl.when(self.beyond)
        def _():
            for copy in self.corners:
                copy.start()

    def start(self, sides=True):
        if not self.rest:
            self.start_vertical()
        for copy in (self.sides if sides else []) + self.rest:
            copy.start()
        if self.rest:
            self.start_vertical()

    def wait_sides(self):
        for copy in self.sides + self.rest:
            copy.wait_recv()

    def wait_vertical(self):
        @pl.when(self.gets)
        def _():
            for copy in self.vertical:
                copy.wait_recv()

        @pl.when(self.expects)
        def _():
            for copy in self.corners:
                copy.wait_recv()

    def wait_send(self):
        @pl.when(self.has)
        def _():
            for copy in self.vertical:
                copy.wait_send()

        @pl.when(self.beyond)
        def _():
            for copy in self.corners:
                copy.wait_send()

        for copy in self.sides + self.rest:
            copy.wait_send()


def greet(place, barrier):
    seg = place.seg
    signal(barrier, (seg, place.left))
    signal(barrier, (seg, place.right))

    @pl.when(place.has_up)
    def _():
        for device in (place.up, place.up_left, place.up_right):
            signal(barrier, (seg, device))

    @pl.when(place.has_down)
    def _():
        for device in (place.down, place.down_left, place.down_right):
            signal(barrier, (seg, device))

    return 2 + 3 * one(place.has_up) + 3 * one(place.has_down)


def own_layer_norm(r):
    own_x = own_rows(r.slots, slice(0, D)).astype(F32)
    deviation = own_x - jnp.mean(own_x, axis=-1, keepdims=True)
    variance = jnp.mean(deviation * deviation, axis=-1, keepdims=True)
    own_inverse = lax.rsqrt(variance + EPSILON)
    r.normal[...] = deviation * own_inverse
    r.inverse[...] = jnp.broadcast_to(own_inverse, (128, 128))


def window_layer_norm(r):
    @pl.loop(0, 5)
    def _(chunk):
        rows = pl.ds(pl.multiple_of(chunk * 128, 128), 128)
        values = r.slots[rows, :].astype(F32)
        deviation = values - jnp.mean(values, axis=-1, keepdims=True)
        variance = jnp.mean(deviation * deviation, axis=-1, keepdims=True)
        part = deviation * lax.rsqrt(variance + EPSILON)
        r.normed[rows, :] = (part * r.gain[...]).astype(BF16)


REFS = [
    "x", "g", "gain", "table", "qkv_in", "out_in", "out",
    "shards", "xs", "slots", "top", "qkv_w", "out_w", "qkv_t", "out_t", "normed", "qkv", "prob_q", "prob_k", "ol",
    "gs", "ga", "dqkv", "outb", "got", "lent", "normal", "inverse", "token", "rows", "deltas", "base", "edge",
]


def main_kernel(tile_count, *refs):
    r = types.SimpleNamespace(**dict(zip(REFS, refs)))
    send, recv, local, ring_send, ring_recv, mate_send, mate_recv = refs[len(REFS) :]
    place = Place(tile_count)
    seg, zs = place.seg, place.zs
    last_seg = lax.axis_size("segment") - 1
    tiles = [place.tile_t, place.tile_b]
    blocks = [place.block_of(0), place.block_of(1)]
    barrier = pltpu.get_barrier_semaphore()
    helper = last_seg - 4
    count = greet(place, barrier) + 2 + one(seg > 0) + 3 * one(seg == helper) + 3 * one(seg == last_seg)
    signal(barrier, (seg, place.mate))
    signal(barrier, (seg, place.cross))

    @pl.when(seg < last_seg)
    def _():
        signal(barrier, (seg + 1, place.tile))

    @pl.when(seg == last_seg)
    def _():
        for device in tiles:
            signal(barrier, (helper, device))

        signal(barrier, (helper, place.tile))

    @pl.when(seg == helper)
    def _():
        signal(barrier, (last_seg, place.tile))
        for device in blocks:
            signal(barrier, (last_seg, device))

    @pl.when(seg == 4)
    def _():
        signal(barrier, (0, place.tile))

    @pl.when((seg == 0) & (place.row % 2 == (place.row // 2) % 2))
    def _():
        for device in blocks:
            signal(barrier, (4, device))

    count = count + one(seg == 0) + one(seg == 4)
    for device in tiles + blocks:

        @pl.when(device != place.tile)
        def _():
            signal(barrier, (seg, device))

        count = count + one(device != place.tile)

    ring = Ring(place, r.shards, ring_send, ring_recv, mate_send, mate_recv)
    pack_shard(r, ring.rows(0, place.core, 0))
    new_row = lax.broadcasted_iota(jnp.int32, (128, 128), 0)
    new_col = lax.broadcasted_iota(jnp.int32, (128, 128), 1)
    to_halves = half_order(new_row, new_col)
    r.xs[0:128, :] = dot(to_halves, r.x[...]).astype(BF16)
    for buf in (r.slots, r.ol, r.gs):
        clear_outside(place, buf)
    r.ga[...] = jnp.zeros_like(r.ga)
    r.deltas[...] = jnp.zeros_like(r.deltas)
    pl.semaphore_wait(barrier, count)

    mine = r.shards.at[ring.rows(0, place.core, 0)]
    theirs = r.shards.at[ring.rows(0, place.core, 2)]
    tile_group = place.row % 2
    x_at = OWN_T + tile_group * GROUP
    g_at = tile_group * 64

    def lend(part):
        rows = pl.ds(part * 128, 128)
        return remote(r.xs.at[rows], r.lent.at[rows], send.at[45 + part], recv.at[45 + part], (helper, place.tile))

    def forward(part, side_half):
        dst, at = ((r.slots, x_at), (r.top, g_at))[part]
        index = 2 * part + side_half
        return remote(
            r.lent.at[pl.ds(index * 64, 64)], dst.at[pl.ds(pl.multiple_of(at, 16), 64)],
            send.at[47 + index], recv.at[2 * part + tile_group], (last_seg, blocks[side_half]),
        )

    @pl.when(seg == helper)
    def _():
        for part in (0, 1):
            lend(part).wait_recv()
            for side_half in (0, 1):
                forward(part, side_half).start()
        for part in (0, 1):
            for side_half in (0, 1):
                forward(part, side_half).wait_send()

    cross_send = remote(mine, mine, send.at[44], recv.at[44], (seg, place.cross))
    cross_send.start()
    ring.begin(0)

    def move(side_half):
        return remote(
            r.xs.at[pl.ds(side_half * 64, 64)], r.slots.at[pl.ds(pl.multiple_of(x_at, 16), 64)],
            send.at[side_half], recv.at[tile_group], (seg, blocks[side_half]),
        )

    def move_local(side_half):
        return pltpu.make_async_copy(
            r.xs.at[pl.ds(side_half * 64, 64)], r.slots.at[pl.ds(pl.multiple_of(x_at, 16), 64)], local.at[side_half]
        )

    for side_half in (0, 1):

        @pl.when((seg < last_seg) & (blocks[side_half] != place.tile))
        def _():
            move(side_half).start()

        @pl.when((seg < last_seg) & (blocks[side_half] == place.tile))
        def _():
            move_local(side_half).start()
            move_local(side_half).wait()

    def moves_wait_recv(part, dst, rows):
        for group in (0, 1):

            @pl.when((seg == last_seg) | (tiles[group] != place.tile))
            def _():
                index = 2 * part + group
                remote(
                    r.xs.at[0:64], dst.at[rows[group]], send.at[index], recv.at[index], (seg, place.left)
                ).wait_recv()

    ring.turn(0, 0)
    fill_edge(r, place)
    fill_bias(r)
    remote(mine, theirs, send.at[44], recv.at[44], (seg, place.cross)).wait_recv()
    ring.begin(1)

    @pl.when(seg == last_seg)
    def _():
        lend(0).start()
        r.xs[128:256, :] = dot(to_halves, r.g[...]).astype(BF16)

    x_halos = [Halo(place, r.slots, send, recv, 4, group) for group in (0, 1)]
    near = jnp.where(place.z % 4 < 2, -1, 1)
    home = place.z // 4
    groups = zs // 4
    for step in range(ring.half):
        ring.turn(step, 1)
        if step + 1 < ring.half:
            ring.turn(step + 1, 0)
        if step == 2:

            @pl.when(seg == last_seg)
            def _():
                lend(1).start()

        if step == ring.half - 4:
            moves_wait_recv(0, r.slots, [own(0), own(1)])
            for halo in x_halos:
                halo.start()
            own_layer_norm(r)
            ring.wait_shared(home)
            unpack_group(r, home, zs)
        if step == ring.half - 3:
            ring.wait_shared((home + near + groups) % groups)
            unpack_group(r, (home + near + groups) % groups, zs)
        if step == ring.half - 2:
            for halo in x_halos:
                halo.wait_sides()
                halo.wait_vertical()
            window_layer_norm(r)
            ring.wait_shared((home - near + groups) % groups)
            unpack_group(r, (home - near + groups) % groups, zs)

    ring.wait_shared((home + 2) % groups)
    unpack_group(r, (home + 2) % groups, zs)
    r.qkv[...] = dot(r.normed[...], r.qkv_w[...]).astype(BF16)
    ol_halos = [Halo(place, r.ol, send, recv, 14, group) for group in (0, 1)]
    for group in (0, 1):
        query_probs(r, group)
        ol_halos[group].start()
    r.qkv_t[...] = r.qkv_w[...].T
    r.out_t[...] = r.out_w[...].T

    first, second = place.core, 1 - place.core

    def passing(group, skip, size, index):
        row = pl.multiple_of(group * 64 + skip, 16)
        slot = pl.multiple_of(OWN_T + group * GROUP + skip, 16)
        return remote(
            r.outb.at[pl.ds(row, size)], r.gs.at[pl.ds(slot, size)], send.at[index], recv.at[index],
            (jnp.maximum(seg - 1, 0), place.tile),
        )

    passes = [passing(first, 0, 64, 34), passing(second, 0, 32, 35), passing(second, 32, 32, 55)]
    gs_halos = [
        Halo(place, r.gs, send, recv, 24, first, True),
        Halo(place, r.gs, send, recv, 24, second, True, 56),
    ]

    relay_group = 1 - place.core
    side_at = pl.multiple_of(T0 + GROUP * relay_group, 16)
    over = pl.multiple_of(3 * GROUP * place.core, 16)
    corners = [
        remote(
            r.gs.at[pl.ds(side_at + skip, 48)], r.gs.at[pl.ds(over + skip, 48)],
            send.at[at], recv.at[at], (seg, place.mate),
        )
        for skip, at in ((0, 38), (112, 39))
    ]
    over_here = pl.multiple_of(3 * GROUP * (1 - place.core), 16)
    corner_arrivals = [
        remote(
            r.gs.at[pl.ds(side_at + skip, 48)], r.gs.at[pl.ds(over_here + skip, 48)],
            send.at[at], recv.at[at], (seg, place.mate),
        )
        for skip, at in ((0, 38), (112, 39))
    ]

    def as_queries(group):
        r.ga[own(group), :] = dot(r.gs[own(group), :], r.out_t[...]).astype(BF16)
        query_side(r, group)

    def query_tokens():
        r.token[...] = dot(r.dqkv[:, 0:D], r.qkv_t[0:D, :])

    @pl.when(seg == last_seg)
    def _():
        moves_wait_recv(1, r.top, [slice(0, 64), slice(64, 128)])
        put_own(r.gs, slice(0, D), r.top[...])
        for halo in gs_halos:
            halo.start()
        for group in (0, 1):
            as_queries(group)
        query_tokens()

    for halo in ol_halos:
        halo.wait_sides()
        halo.wait_vertical()
    thirds = lax.broadcasted_iota(jnp.int32, (16, 128), 1)
    head_row = lax.broadcasted_iota(jnp.int32, (16, 128), 0)
    r.rows[...] = dot_nt(onehot((thirds < 48) & (thirds % 16 == head_row)), r.ol[:, D:OLW])
    key_probs(r)

    @pl.when(seg < last_seg)
    def _():
        passes[0].wait_recv()
        gs_halos[0].start()
        as_queries(first)
        passes[1].wait_recv()
        gs_halos[1].start_sides()
        passes[2].wait_recv()
        gs_halos[1].start(sides=False)
        as_queries(second)
        query_tokens()

    row_at = pl.multiple_of(place.half * 64, 16)

    def back(group):
        return remote(
            r.outb.at[pl.ds(group * 64, 64)], r.got.at[pl.ds(row_at, 64)],
            send.at[36 + group], recv.at[36 + place.half], (seg, tiles[group]),
        )

    def back_local(group):
        return pltpu.make_async_copy(r.outb.at[pl.ds(group * 64, 64)], r.got.at[pl.ds(row_at, 64)], local.at[4 + group])

    porter = 4

    def hand(chunk):
        return remote(
            r.outb.at[pl.ds(pl.multiple_of(first * 64 + chunk * 32, 16), 32)], r.lent.at[pl.ds(chunk * 32, 32)],
            send.at[51 + chunk], recv.at[51 + chunk], (porter, place.tile),
        )

    def carry(chunk):
        row = pl.multiple_of(row_at + chunk * 32, 16)
        return remote(
            r.lent.at[pl.ds(chunk * 32, 32)], r.got.at[pl.ds(row, 32)],
            send.at[53 + chunk], recv.at[40 + 2 * place.half + chunk], (0, jnp.where(first == 0, tiles[0], tiles[1])),
        )

    def straight(group):
        return (seg > 0) | (second == group)

    def go_back(group, when):
        @pl.when((tiles[group] != place.tile) & when)
        def _():
            back(group).start()

        @pl.when((tiles[group] == place.tile) & when)
        def _():
            back_local(group).start()
            back_local(group).wait()

    def hand_over():
        @pl.when(seg == 0)
        def _():
            hand(0).start()
            hand(1).start()

    def send_on(copies):
        @pl.when(seg > 0)
        def _():
            for copy in copies:
                copy.start()

    gs_halos[0].wait_sides()
    gs_halos[1].wait_vertical()
    attn_grads(r, [1 + first, 3 * first])
    gs_halos[1].wait_sides()
    for copy in corners:
        copy.start()
    attn_grads(r, [1 + second])
    join_deltas(r)
    key_side(r, first)
    finish(r, first)
    send_on(passes[:1])
    hand_over()

    gs_halos[0].wait_vertical()
    for copy in corner_arrivals:
        copy.wait_recv()
    attn_grads(r, [3 * second])
    join_deltas(r)
    key_side(r, second)
    finish(r, second)
    send_on(passes[1:])
    for group in (0, 1):
        go_back(group, (seg == 0) & (second == group))

    @pl.when(seg > 0)
    def _():
        for one_pass in passes:
            one_pass.wait_send()

    for group in (0, 1):
        go_back(group, seg > 0)

    ring.wait_send()
    cross_send.wait_send()

    @pl.when(seg == last_seg)
    def _():
        lend(0).wait_send()
        lend(1).wait_send()

    for side_half in (0, 1):

        @pl.when((seg < last_seg) & (blocks[side_half] != place.tile))
        def _():
            move(side_half).wait_send()

    for halo in x_halos + ol_halos + gs_halos:
        halo.wait_send()
    for copy in corners:
        copy.wait_send()

    @pl.when(seg == porter)
    def _():
        for chunk in (0, 1):
            hand(chunk).wait_recv()
            carry(chunk).start()

    carried = (seg == 0) & (tile_group == (place.row // 2) % 2)
    for side_half in (0, 1):

        @pl.when((blocks[side_half] != place.tile) & jnp.logical_not(carried))
        def _():
            remote(
                r.outb.at[0:64], r.got.at[pl.ds(side_half * 64, 64)], send.at[36 + side_half], recv.at[36 + side_half],
                (seg, place.left),
            ).wait_recv()

        @pl.when(carried)
        def _():
            for chunk in (0, 1):
                index = 40 + 2 * side_half + chunk
                remote(
                    r.outb.at[0:32], r.got.at[pl.ds(side_half * 64 + chunk * 32, 32)], send.at[index], recv.at[index],
                    (seg, place.left),
                ).wait_recv()

    r.out[...] = dot(half_order(new_col, new_row), r.got[...]).astype(BF16)

    for group in (0, 1):

        @pl.when((tiles[group] != place.tile) & straight(group))
        def _():
            back(group).wait_send()

    @pl.when(seg == 0)
    def _():
        hand(0).wait_send()
        hand(1).wait_send()

    @pl.when(seg == porter)
    def _():
        carry(0).wait_send()
        carry(1).wait_send()


def main(x, g, gain, table, qkv_in, out_in, tile_count):
    zs = tile_count // 4
    vmem = pl.BlockSpec(memory_space=pltpu.VMEM)
    bf16 = [
        (zs * 64, WIDE), (256, D), (SLOTS, D), (128, D), (D, WIDE), (D, D), (WIDE, D), (D, D), (SLOTS, D), (SLOTS, WIDE),
        (6, 256, WIN), (6, 256, WIN), (SLOTS, OLW), (SLOTS, D), (SLOTS, D), (128, WIDE), (128, D), (128, D),
        (256, D),
    ]
    f32 = [(128, D), (128, 128), (128, D), (16, SLOTS), (4, 16, 256), (2, HEADS, 8, WIN), (8, SLOTS)]
    return pl.pallas_call(
        functools.partial(main_kernel, tile_count),
        out_shape=jax.ShapeDtypeStruct((128, D), BF16),
        in_specs=[vmem] * 6,
        out_specs=vmem,
        scratch_shapes=[pltpu.VMEM(shape, BF16) for shape in bf16]
        + [pltpu.VMEM(shape, F32) for shape in f32]
        + [
            pltpu.SemaphoreType.DMA((58,)),
            pltpu.SemaphoreType.DMA((58,)),
            pltpu.SemaphoreType.DMA((6,)),
            pltpu.SemaphoreType.DMA((2, 4, zs // 2)),
            pltpu.SemaphoreType.DMA((2, 4, zs // 2)),
            pltpu.SemaphoreType.DMA((2, zs)),
            pltpu.SemaphoreType.DMA((2, zs)),
        ],
        compiler_params=pltpu.CompilerParams(
            collective_id=0, has_side_effects=True, vmem_limit_bytes=58 * 2**20
        ),
    )(x, g, gain, table, qkv_in, out_in)


def body(stored_inputs, output_grads, norm_gain, position_bias, qkv_weight, out_weight):
    tokens = TH * TW
    out = main(
        stored_inputs.reshape(tokens, D), output_grads.reshape(tokens, D), norm_gain,
        position_bias.reshape(HEADS, -1), qkv_weight[0], out_weight[0], lax.axis_size("tile"),
    )
    return out.reshape(1, 1, 1, TH, TW, D)


def solution(mesh):
    return jax.shard_map(
        body,
        mesh=mesh,
        in_specs=(
            P("segment", None, "tile", None, None, None),
            P(None, "tile", None, None, None),
            P("segment", None),
            P("segment", None, None, None),
            P("segment", "tile", None),
            P("segment", "tile", None),
        ),
        out_specs=P("segment", None, "tile", None, None, None),
        check_vma=False,
    )
```
